128 devices in a mesh: lat: 8 (over y, z_lo), lon: 16 (over x, z_hi, core).
Axes of the slice: x: 4, y: 4, z: 4 (z_hi: 2, z_lo: 2; z = z_hi * 2 + z_lo), core: 2. Of those that a mesh axis runs over, the one named last changes fastest.
Arguments:
- atmos_features: bfloat16 [256, 512, 768], P('lat', 'lon'), may hold values from -6 to 6
- ocean_features: bfloat16 [512, 1024, 192], P('lat', 'lon'), may hold values from -6 to 6
- wet_cell_mask: int32 [512, 1024], P('lat', 'lon'), may hold values from 0 to 1, as said below
- overlay_cell_index: int32 [4, 512, 1024], P(None, 'lat', 'lon'), may hold values from 0 to 16383, as said below
- remap_weight: float32 [4, 512, 1024], P(None, 'lat', 'lon'), may hold values from 0.1 to 1
- query_key_value_weight: bfloat16 [768, 2304], replicated, may hold values from -5 to 5
- attention_out_weight: bfloat16 [768, 768], replicated, may hold values from -0.21875 to 0.21875
- feedforward_up_weight: bfloat16 [768, 3072], replicated, may hold values from -0.21875 to 0.21875
- feedforward_down_weight: bfloat16 [3072, 768], replicated, may hold values from -0.109375 to 0.109375
- attention_gain: float32 [768], replicated, may hold values from 0.25 to 1.75
- feedforward_gain: float32 [768], replicated, may hold values from 0.25 to 1.75
- flux_head_weight: bfloat16 [768, 8], replicated, may hold values from -0.21875 to 0.21875
- surface_temp_embedding: float32 [768], replicated, may hold values from -5 to 5
- forcing_lift_weight: float32 [8, 192], replicated, may hold values from -2 to 2
- depthwise_kernels: float32 [2, 49, 192], replicated, may hold values from -0.875 to 0.875
- ocean_norm_gains: float32 [2, 192], replicated, may hold values from 0.25 to 1.75
- ocean_up_weights: bfloat16 [2, 192, 768], replicated, may hold values from -0.4375 to 0.4375
- ocean_down_weights: bfloat16 [2, 768, 192], replicated, may hold values from -0.21875 to 0.21875
- surface_temp_head: float32 [192], replicated, may hold values from -0.4375 to 0.4375
Outputs:
- atmos_updated: bfloat16 [256, 512, 768], P('lat', 'lon')
- ocean_out: bfloat16 [512, 1024, 192], P('lat', 'lon')
The draws below stay inside these ranges and needn't reach their ends.
Inputs may be any that keep to these rules, and one draw needn't show every extreme that they name: `wet_cell_mask`: the ocean tile of rows [i * 64, i * 64 + 64) and columns [j * 64, j * 64 + 64) and the tile 512 / 2 rows north or south of it in the same columns together hold at most 4096 wet cells; some pair holds exactly that many. `overlay_cell_index`: each entry names an atmosphere cell of the latitude band of the ocean row: ocean row r belongs to the band of atmosphere rows [(r // 64) * 32, (r // 64) * 32 + 32), and the entry is (row within the band) * 512 + column.
All inputs are finite; a program needn't handle non-finite values.
Results may differ from the reference program's by a relative error of at most 0.013.
Values may be sent and summed in bfloat16 or wider, within the bound.
A program may use at most 128 MiB of HBM per device.

```python
import math
import jax
import jax.numpy as jnp
from jax import lax

MODEL_WIDTH = 768
HEADS = 12
HD = 64
FFN = 3072
NF = 8
OCEAN_CHANNELS = 192
OFF = 768
NOV = 4
WR = 8
WC = 16
BLOCKS = 2
AR = 32
OR = 64
OCOL = 64
ATMOS_ROWS = 256
ATMOS_COLUMNS = 512
OLAT = 512
OLON = 1024


def draw_query_key_value_weight(key, part):
    base = jnp.clip(jax.random.normal(key, (MODEL_WIDTH, 3 * MODEL_WIDTH), jnp.float32), -5.5, 5.5) * MODEL_WIDTH ** (-0.5)
    return jnp.clip(base, -5.0, 5.0).astype(jnp.bfloat16)


def draw_wet_cell_mask(key, part):
    tiles_lat = OLAT // OR
    tiles_lon = OLON // OCOL
    half_lat = tiles_lat // 2
    cells = OR * OCOL
    key_low, key_slack, key_flip, key_rank = jax.random.split(key, 4)
    lower = jax.random.randint(key_low, (half_lat, tiles_lon), cells // 8, cells - cells // 8 + 1)
    slack = jax.random.randint(key_slack, (half_lat, tiles_lon), 0, cells // 8 + 1)
    first_tile = (jnp.arange(half_lat)[:, None] == 0) & (jnp.arange(tiles_lon)[None, :] == 0)
    slack = jnp.where(first_tile, 0, slack)
    upper = cells - lower - slack
    flipped = jax.random.randint(key_flip, (half_lat, tiles_lon), 0, 2)
    southern = jnp.where(flipped == 1, lower, upper)
    northern = jnp.where(flipped == 1, upper, lower)
    counts = jnp.concatenate([southern, northern], axis=0).reshape(-1, 1)
    tile_keys = jax.random.split(key_rank, tiles_lat * tiles_lon)
    ranks = jax.vmap(lambda single: jax.random.permutation(single, cells))(tile_keys)
    wet = (ranks < counts).astype(jnp.int32)
    wet = wet.reshape(tiles_lat, tiles_lon, OR, OCOL).transpose(0, 2, 1, 3)
    return wet.reshape(OLAT, OLON)


def draw_overlay_cell_index(key, part):
    atm_cols = OLON // 2
    keys_all = jax.random.split(key, 5)
    shape = (NOV, OLAT, OLON)
    row_shift = jax.random.randint(keys_all[0], shape, -1, 2)
    col_shift = jax.random.randint(keys_all[1], shape, -1, 2)
    ocean_rows = jnp.arange(OLAT, dtype=jnp.int32)[None, :, None]
    ocean_cols = jnp.arange(OLON, dtype=jnp.int32)[None, None, :]
    near_row = jnp.clip(ocean_rows % OR // 2 + row_shift, 0, AR - 1)
    near_col = (ocean_cols // 2 + col_shift) % atm_cols
    distant = jax.random.randint(keys_all[2], shape, 0, 8) == 0
    far_row = jax.random.randint(keys_all[3], shape, 0, AR)
    far_col = jax.random.randint(keys_all[4], shape, 0, atm_cols)
    row_pick = jnp.where(distant, far_row, near_row)
    col_pick = jnp.where(distant, far_col, near_col)
    return (row_pick * atm_cols + col_pick).astype(jnp.int32)


def shard_levels(stream_key, shape, shards, low, top_value):
    level = 1.0
    for position, shards_of in shards:
        draws = jax.random.uniform(jax.random.fold_in(jax.random.fold_in(stream_key, 6), position), (shards_of,), jnp.float32, low / len(shards), top_value / len(shards))
        level = level * jnp.repeat(jnp.exp(draws), shape[position] // shards_of).reshape((-1,) + (1,) * (len(shape) - 1 - position))
    return level


def centred(stream_key, shape, scale, bound, shards=(), held_as=jnp.bfloat16):
    loudness = shard_levels(stream_key, shape, shards, -0.22, 0.18) if shards else 1.0
    values = jax.random.normal(stream_key, shape, jnp.float32) * scale * loudness
    return jnp.minimum(jnp.maximum(values, -bound), bound).astype(held_as)


def setup_inputs(seed: int = 0) -> dict:
    key_list = jax.random.split(jax.random.key(seed), 20)
    return {
        "atmos_features": centred(key_list[0], (ATMOS_ROWS, ATMOS_COLUMNS, MODEL_WIDTH), 1.0, 6.0, ((0, 8), (1, 16))),
        "ocean_features": centred(key_list[1], (OLAT, OLON, OCEAN_CHANNELS), 1.0, 6.0, ((0, 8), (1, 16))),
        "wet_cell_mask": draw_wet_cell_mask(jax.random.fold_in(key_list[19], 71), 0),
        "overlay_cell_index": draw_overlay_cell_index(jax.random.fold_in(key_list[19], 71), 0),
        "remap_weight": jnp.clip(jnp.exp(math.log(1.0) - 2.3025851 * jax.random.uniform(key_list[4], (NOV, OLAT, OLON), jnp.float32) ** shard_levels(key_list[4], (NOV, OLAT, OLON), ((1, 8), (2, 16)), -0.2, 0.2)), 0.1, 1.0),
        "query_key_value_weight": draw_query_key_value_weight(jax.random.fold_in(key_list[19], 71), 0),
        "attention_out_weight": centred(key_list[6], (MODEL_WIDTH, MODEL_WIDTH), MODEL_WIDTH ** -0.5, 0.21875),
        "feedforward_up_weight": centred(key_list[7], (MODEL_WIDTH, FFN), MODEL_WIDTH ** -0.5, 0.21875),
        "feedforward_down_weight": centred(key_list[8], (FFN, MODEL_WIDTH), FFN ** -0.5, 0.109375),
        "attention_gain": jnp.clip(1.0 + 0.15 * jax.random.normal(key_list[9], (MODEL_WIDTH,), jnp.float32), 0.25, 1.75),
        "feedforward_gain": jnp.clip(1.0 + 0.15 * jax.random.normal(key_list[10], (MODEL_WIDTH,), jnp.float32), 0.25, 1.75),
        "flux_head_weight": centred(key_list[11], (MODEL_WIDTH, NF), MODEL_WIDTH ** -0.5, 0.21875),
        "surface_temp_embedding": centred(key_list[12], (MODEL_WIDTH,), 1.0, 5.0, (), jnp.float32),
        "forcing_lift_weight": centred(key_list[13], (NF, OCEAN_CHANNELS), NF ** -0.5, 2.0, (), jnp.float32),
        "depthwise_kernels": centred(key_list[14], (BLOCKS, 49, OCEAN_CHANNELS), 49 ** -0.5, 0.875, (), jnp.float32),
        "ocean_norm_gains": jnp.clip(1.0 + 0.15 * jax.random.normal(key_list[15], (BLOCKS, OCEAN_CHANNELS), jnp.float32), 0.25, 1.75),
        "ocean_up_weights": centred(key_list[16], (BLOCKS, OCEAN_CHANNELS, OFF), OCEAN_CHANNELS ** -0.5, 0.4375),
        "ocean_down_weights": centred(key_list[17], (BLOCKS, OFF, OCEAN_CHANNELS), OFF ** -0.5, 0.21875),
        "surface_temp_head": centred(key_list[18], (OCEAN_CHANNELS,), OCEAN_CHANNELS ** -0.5, 0.4375, (), jnp.float32),
    }


EPS = 1e-06

def rms_scale(values, gain):
    return values * lax.rsqrt(lax.optimization_barrier(jnp.mean(values * values, axis=-1, keepdims=True)) + EPS) * gain

def layer_scale(values, gain):
    center = values - lax.optimization_barrier(jnp.mean(values, axis=-1, keepdims=True))
    return center * lax.rsqrt(lax.optimization_barrier(jnp.mean(center * center, axis=-1, keepdims=True)) + EPS) * gain

def to_windows(tensor):
    row_total, column_total = (tensor.shape[0], tensor.shape[1])
    shaped = tensor.reshape(row_total // WR, WR, column_total // WC, WC, HEADS, HD)
    return shaped.transpose(0, 2, 4, 1, 3, 5).reshape(-1, HEADS, WR * WC, HD)

def from_windows(tensor, row_total, column_total):
    shaped = tensor.reshape(row_total // WR, column_total // WC, HEADS, WR, WC, HD)
    return shaped.transpose(0, 3, 1, 4, 2, 5).reshape(row_total, column_total, HEADS * HD)

def depthwise(padded, taps, row_total, column_total):
    total = jnp.zeros((row_total, column_total, padded.shape[2]), jnp.float32)
    for north in range(7):
        for east in range(7):
            window = padded[north:north + row_total, east:east + column_total].astype(jnp.float32)
            total = total + window * taps[north * 7 + east]
    return total

def atm_band(band, query_key_value_weight, attention_out_weight, feedforward_up_weight, feedforward_down_weight, attention_gain, feedforward_gain, flux_head_weight):
    model_state = band.astype(jnp.float32)
    normed = rms_scale(model_state, attention_gain).astype(jnp.bfloat16)
    projected = jnp.dot(normed, query_key_value_weight, preferred_element_type=jnp.float32).astype(jnp.bfloat16)
    rolled = jnp.roll(projected, WC // 2, axis=1)
    query = to_windows(rolled[..., :MODEL_WIDTH]).astype(jnp.float32)
    keys_win = to_windows(rolled[..., MODEL_WIDTH:2 * MODEL_WIDTH]).astype(jnp.float32)
    value_win = to_windows(rolled[..., 2 * MODEL_WIDTH:]).astype(jnp.float32)
    scores = jnp.einsum('whqd,whkd->whqk', query, keys_win) * HD ** (-0.5)
    probs = jax.nn.softmax(scores, axis=-1).astype(jnp.bfloat16)
    mixed = jnp.einsum('whqk,whkd->whqd', probs.astype(jnp.float32), value_win).astype(jnp.bfloat16)
    attended = jnp.roll(from_windows(mixed, WR, ATMOS_COLUMNS), -(WC // 2), axis=1)
    first = model_state + jnp.dot(attended, attention_out_weight, preferred_element_type=jnp.float32)
    normed_mlp = rms_scale(first, feedforward_gain).astype(jnp.bfloat16)
    active = jax.nn.gelu(jnp.dot(normed_mlp, feedforward_up_weight, preferred_element_type=jnp.float32)).astype(jnp.bfloat16)
    second_half = first + jnp.dot(active, feedforward_down_weight, preferred_element_type=jnp.float32)
    fluxes = jnp.dot(second_half.astype(jnp.bfloat16), flux_head_weight, preferred_element_type=jnp.float32).astype(jnp.bfloat16)
    return (second_half, fluxes)

def reference(atmos_features, ocean_features, wet_cell_mask, overlay_cell_index, remap_weight, query_key_value_weight, attention_out_weight, feedforward_up_weight, feedforward_down_weight, attention_gain, feedforward_gain, flux_head_weight, surface_temp_embedding, forcing_lift_weight, depthwise_kernels, ocean_norm_gains, ocean_up_weights, ocean_down_weights, surface_temp_head):
    bands = atmos_features.reshape(ATMOS_ROWS // WR, WR, ATMOS_COLUMNS, MODEL_WIDTH)
    second_half, fluxes = lax.map(lambda band: atm_band(band, query_key_value_weight, attention_out_weight, feedforward_up_weight, feedforward_down_weight, attention_gain, feedforward_gain, flux_head_weight), bands)
    second_half = second_half.reshape(ATMOS_ROWS, ATMOS_COLUMNS, MODEL_WIDTH)
    flux_flat = fluxes.reshape(ATMOS_ROWS * ATMOS_COLUMNS, NF)
    band_start = jnp.arange(OLAT, dtype=jnp.int32) // OR * (AR * ATMOS_COLUMNS)
    global_index = overlay_cell_index + band_start[None, :, None]
    picked = flux_flat[global_index].astype(jnp.float32)
    forcing = lax.optimization_barrier(jnp.sum(remap_weight[..., None] * picked, axis=0))
    wet = wet_cell_mask.astype(jnp.float32)[..., None]
    lifted = jnp.dot(forcing, forcing_lift_weight, precision=lax.Precision.HIGHEST, preferred_element_type=jnp.float32)
    model_state = wet * (ocean_features.astype(jnp.float32) + lifted)
    for block_id in range(BLOCKS):
        rounded = model_state.astype(jnp.bfloat16)
        wrapped = jnp.concatenate([rounded[:, -3:], rounded, rounded[:, :3]], axis=1)
        north_rows = wrapped[OLAT - 3:][::-1, ::-1]
        south_rows = jnp.zeros((3, OLON + 6, OCEAN_CHANNELS), jnp.bfloat16)
        padded = jnp.concatenate([south_rows, wrapped, north_rows], axis=0)
        taps = depthwise_kernels[block_id]
        gain = ocean_norm_gains[block_id]
        up_weight = ocean_up_weights[block_id]
        down_weight = ocean_down_weights[block_id]

        def band_step(band_id):
            rows_here = lax.dynamic_slice_in_dim(padded, band_id * OR, OR + 6, 0)
            convolved = depthwise(rows_here, taps, OR, OLON)
            normed = layer_scale(convolved, gain).astype(jnp.bfloat16)
            active = jax.nn.gelu(jnp.dot(normed, up_weight, preferred_element_type=jnp.float32)).astype(jnp.bfloat16)
            return jnp.dot(active, down_weight, preferred_element_type=jnp.float32)
        increment = lax.map(band_step, jnp.arange(OLAT // OR, dtype=jnp.int32)).reshape(OLAT, OLON, OCEAN_CHANNELS)
        model_state = model_state + wet * increment
    ocean_out = model_state.astype(jnp.bfloat16)
    sea_surface_temp = jnp.dot(model_state, surface_temp_head, precision=lax.Precision.HIGHEST, preferred_element_type=jnp.float32)
    numerator = sea_surface_temp.reshape(ATMOS_ROWS, 2, ATMOS_COLUMNS, 2).sum(axis=(1, 3))
    wet_cell_count = wet_cell_mask.reshape(ATMOS_ROWS, 2, ATMOS_COLUMNS, 2).sum(axis=(1, 3)).astype(jnp.float32)
    surface_temp_atmos = numerator / jnp.maximum(wet_cell_count, 1.0)
    atmos_updated = (second_half + surface_temp_atmos[..., None] * surface_temp_embedding).astype(jnp.bfloat16)
    return (atmos_updated, ocean_out)
```

```python
import functools

import jax
import jax.numpy as jnp
import numpy as np
from jax import lax
from jax.experimental import pallas as pl
from jax.experimental.pallas import tpu as pltpu
from jax.sharding import PartitionSpec as P

BF = jnp.bfloat16
F32 = jnp.float32
EPS = 1e-6
MESH = pl.DeviceIdType.MESH
CH = 8
CELLS = 512

def attend_kernel(q_ref, own_ref, halo_ref, out_ref):
    lane=lax.broadcasted_iota(jnp.int32,(128,128),1)
    even=lane<64
    zero=jnp.zeros((128,128),BF)
    def paired(block):
        return jnp.concatenate([jnp.where(even,block,zero),jnp.where(even,zero,block)],axis=0)
    for pair in range(6):
        lanes=slice(128*pair,128*pair+128)
        vl=slice(768+128*pair,768+128*pair+128)
        def window(first,second,query):
            keys=paired(jnp.concatenate([first(lanes),second(lanes)],axis=0))
            vals=paired(jnp.concatenate([first(vl),second(vl)],axis=0))
            s=lax.dot_general(query*BF(0.125),keys,(((1,),(1,)),((),())),preferred_element_type=F32)
            sa=s[:,:128]; sb=s[:,128:]
            ea=jnp.exp(sa-jnp.max(sa,axis=1,keepdims=True)); eb=jnp.exp(sb-jnp.max(sb,axis=1,keepdims=True))
            ra=1.0/jnp.sum(ea,axis=1,keepdims=True); rb=1.0/jnp.sum(eb,axis=1,keepdims=True)
            probs=jnp.concatenate([(ea*ra).astype(BF),(eb*rb).astype(BF)],axis=1)
            return jnp.dot(probs,vals,preferred_element_type=F32).astype(BF)
        own=lambda j: (lambda l: own_ref[0,j,:,l])
        halo=lambda j: (lambda l: halo_ref[j,0,:,l])
        out_ref[0,0,:,lanes]=window(halo(0),own(0),q_ref[0,0,:,lanes])
        mid=window(own(1),own(2),jnp.concatenate([q_ref[0,1,:,lanes],q_ref[0,2,:,lanes]],axis=0))
        out_ref[0,1,:,lanes]=mid[:64]
        out_ref[0,2,:,lanes]=mid[64:]
        out_ref[0,3,:,lanes]=window(own(3),halo(1),q_ref[0,3,:,lanes])

def attend(q,own,halo):
    return pl.pallas_call(attend_kernel,grid=(4,),
        out_shape=jax.ShapeDtypeStruct((4,4,64,768),BF),
        in_specs=[pl.BlockSpec((1,4,64,768),lambda i:(i,0,0,0)),pl.BlockSpec((1,4,64,1536),lambda i:(i,0,0,0)),pl.BlockSpec((2,1,64,1536),lambda i:(0,i,0,0))],
        out_specs=pl.BlockSpec((1,4,64,768),lambda i:(i,0,0,0)),
        compiler_params=pltpu.CompilerParams(vmem_limit_bytes=48*2**20),
        name="attend",
        cost_estimate=pl.CostEstimate(flops=10**10,bytes_accessed=8*2**20,transcendentals=2*10**6),
    )(q,own,halo)

def pick_kernel(table_ref, lo_ref, hi_ref, w_ref, out_ref, t_ref):
    for h in range(4):
        t_ref[128*h:128*h+128,:]=table_ref[:,256*h:256*h+256]
    ids=lax.broadcasted_iota(jnp.int32,(256,CELLS),0)
    def chunk(i,_):
        total=jnp.zeros((8,CELLS),F32)
        for e in range(4):
            lo=lo_ref[e,pl.ds(i,1),:]
            hit=jnp.where(ids==lo,1.0,0.0).astype(BF)
            res=jnp.dot(t_ref[...],hit,preferred_element_type=F32)
            hi=jnp.broadcast_to(hi_ref[e,pl.ds(i,1),:],(8,CELLS))
            got=res[0:8]
            for k in range(1,64):
                got=jnp.where(hi==k,res[8*k:8*k+8],got)
            total=total+got*w_ref[e,pl.ds(i,1),:]
        out_ref[i]=total
        return 0
    lax.fori_loop(0,4096//CELLS,chunk,0)

def picked_forcing(table,idx,w):
    lo=((idx>>3)&3)<<6|((idx>>9)&7)<<3|(idx&7)
    hi=((idx>>12)&3)<<4|((idx>>5)&15)
    n=4096//CELLS
    lo=lo.reshape(4,n,CELLS); hi=hi.reshape(4,n,CELLS); w=w.reshape(4,n,CELLS)
    vm=pl.BlockSpec(memory_space=pltpu.VMEM)
    return pl.pallas_call(pick_kernel,out_shape=jax.ShapeDtypeStruct((n,8,CELLS),F32),
        in_specs=[vm]*4,out_specs=vm,scratch_shapes=[pltpu.VMEM((512,256),BF)],
        compiler_params=pltpu.CompilerParams(vmem_limit_bytes=48*2**20),name="pick",
        cost_estimate=pl.CostEstimate(flops=10**10,bytes_accessed=2**20,transcendentals=0))(table,lo,hi,w)


def tap_rows(depthwise_kernels):
    nb=depthwise_kernels.shape[0]
    pick=np.zeros((3,4,4,7),np.float32)
    for d in range(3):
        for q in range(4):
            for p in range(4):
                a=4*(d-1)+q-p+3
                if 0<=a<7: pick[d,q,p,a]=1
    k=depthwise_kernels.reshape(nb,7,7,3,64)
    v=jnp.einsum("dqpa,nabgc->ngdbqpc",jnp.asarray(pick),k, precision=lax.Precision.HIGHEST)
    return v.reshape(nb,3,84,256)

def split_dot(x, ones):
    hi=x.astype(BF); lo=(x-hi.astype(F32)).astype(BF)
    return jnp.dot(hi,ones,preferred_element_type=F32)+jnp.dot(lo,ones,preferred_element_type=F32)

def gelu(x):
    inner=x*(0.7978845608028654+0.035677408136300125*(x*x))
    h=0.5*x
    return h+h*jnp.tanh(inner)

def ocean_kernel(last, pad_ref, v_ref, gain_ref, up_ref, down_ref, ocean_ref, wet_ref, head_ref, *rest):
    if last:
        out_ref, sst_ref, w_ref, x4_ref, a_ref, y_ref = rest
    else:
        out_ref, w_ref, x4_ref, a_ref, y_ref = rest
    sub=lax.broadcasted_iota(jnp.int32,(64,256),0)
    lane=lax.broadcasted_iota(jnp.int32,(64,256),1)
    diag=(lane%64)==sub
    for g in range(3):
        def build(t, _):
            for q in range(4):
                row=v_ref[g, pl.ds(t*4+q,1), :]
                w_ref[g, pl.ds(pl.multiple_of(t*256+q*64,64),64), :]=jnp.where(diag,row,0.0).astype(BF)
            return 0
        lax.fori_loop(0,21,build,0)
    def group(i,_):
        rows=[pad_ref[4*i+p].astype(F32) for p in range(4)]
        for g in range(3):
            x4_ref[g]=jnp.concatenate([r[:,64*g:64*g+64] for r in rows],axis=1)
            for b in range(7):
                a_ref[g,i,:,256*b:256*b+256]=x4_ref[g,pl.ds(b,64),:].astype(BF)
        return 0
    lax.fori_loop(0,18,group,0)
    s2=lax.broadcasted_iota(jnp.int32,(256,256),0)//64
    l2=lax.broadcasted_iota(jnp.int32,(256,256),1)//64
    ones=jnp.where(s2==l2,1.0,0.0).astype(BF)
    def chunk(ci,_):
        base=ci*CH
        M=CH*64
        for g in range(3):
            acc=None
            for d in range(3):
                lhs=a_ref[g,pl.ds(base+d,CH)].reshape(M,1792)
                part=jnp.dot(lhs,w_ref[g,d*1792:(d+1)*1792,:],preferred_element_type=F32)
                acc=part if acc is None else acc+part
            y_ref[g]=acc
        tot=y_ref[0]+y_ref[1]+y_ref[2]
        mean=split_dot(tot,ones)*(1/192)
        cs=[y_ref[g]-mean for g in range(3)]
        var=split_dot(cs[0]*cs[0]+cs[1]*cs[1]+cs[2]*cs[2],ones)*(1/192)
        inv=lax.rsqrt(var+EPS)
        ns=[(cs[g]*inv*gain_ref[g]).astype(BF) for g in range(3)]
        for p in range(4):
            n=jnp.concatenate([ns[g][:,64*p:64*p+64] for g in range(3)],axis=1)
            act=gelu(jnp.dot(n,up_ref[...],preferred_element_type=F32)).astype(BF)
            inc=jnp.dot(act,down_ref[...],preferred_element_type=F32)
            wet=wet_ref[ci,p]
            for j in range(CH):
                r=4*(base+j)+p
                new=ocean_ref[r]+wet[:,j:j+1]*inc[64*j:64*j+64]
                if last:
                    out_ref[r]=new.astype(BF)
                    sst_ref[r]=jnp.sum(new*head_ref[...],axis=1,keepdims=True)
                else:
                    out_ref[r]=new
        return 0
    lax.fori_loop(0,16//CH,chunk,0)

def ocean_block(last,padded,v,gain,up,down,ocean,wet,head):
    gain_t=jnp.tile(gain.reshape(3,1,1,64),(1,1,4,1)).reshape(3,1,256)
    wt=wet.reshape(16//CH,CH,4,64).transpose(0,2,3,1)
    vm=pl.BlockSpec(memory_space=pltpu.VMEM)
    outs=[jax.ShapeDtypeStruct((64,64,192),BF if last else F32)]
    if last: outs.append(jax.ShapeDtypeStruct((64,64,1),F32))
    return pl.pallas_call(functools.partial(ocean_kernel,last),
        out_shape=outs, in_specs=[vm]*8, out_specs=[vm]*len(outs),
        scratch_shapes=[pltpu.VMEM((3,21*256,256),BF),pltpu.VMEM((3,80,256),F32),pltpu.VMEM((3,18,64,1792),BF),pltpu.VMEM((3,CH*64,256),F32)],
        compiler_params=pltpu.CompilerParams(vmem_limit_bytes=60*2**20),
        name="ocean_last" if last else "ocean_first",
        cost_estimate=pl.CostEstimate(flops=40*10**9,bytes_accessed=8*2**20,transcendentals=3*10**6),
    )(padded,v,gain_t,up,down,ocean,wt,head.reshape(1,192))


def ring(axis):
    count = lax.axis_size(axis)
    forward = [(i, (i + 1) % count) for i in range(count)]
    return forward, [(target, source) for source, target in forward]


def ocean_halo(rounded):
    rows, cols, channels = rounded.shape
    forward, backward = ring("lat")
    lon_count = lax.axis_size("lon")
    lat_index = lax.axis_index("lat")
    south = lax.ppermute(rounded[-3:], "lat", forward)
    north = lax.ppermute(rounded[:3], "lat", backward)
    fold = lax.ppermute(rounded[-3:][::-1, ::-1], "lon", [(i, lon_count - 1 - i) for i in range(lon_count)])
    north = jnp.where(lat_index == lax.axis_size("lat") - 1, fold, north)
    south = jnp.where(lat_index == 0, jnp.zeros_like(south), south)
    tall = jnp.concatenate([south, rounded, north], axis=0)
    forward, backward = ring("lon")
    west = lax.ppermute(tall[:, -3:], "lon", forward)
    east = lax.ppermute(tall[:, :3], "lon", backward)
    wide = jnp.concatenate([west, tall, east], axis=1)
    return jnp.pad(wide, ((1, 1), (0, 10), (0, 0)))


def rms_scale(values, gain):
    return values * lax.rsqrt(jnp.mean(values * values, axis=-1, keepdims=True) + EPS) * gain


def body(
    atmos_features,
    ocean_features,
    wet_cell_mask,
    overlay_cell_index,
    remap_weight,
    query_key_value_weight,
    attention_out_weight,
    feedforward_up_weight,
    feedforward_down_weight,
    attention_gain,
    feedforward_gain,
    flux_head_weight,
    surface_temp_embedding,
    forcing_lift_weight,
    depthwise_kernels,
    ocean_norm_gains,
    ocean_up_weights,
    ocean_down_weights,
    surface_temp_head,
):
    width = atmos_features.shape[2]
    blocks = atmos_features.reshape(4, 8, 4, 8, width).transpose(0, 2, 1, 3, 4).reshape(4, 4, 64, width)
    forward, backward = ring("lon")
    west = lax.ppermute(blocks[:, 3], "lon", forward)
    east = lax.ppermute(blocks[:, 0], "lon", backward)
    model_state = blocks.reshape(1024, width).astype(F32)
    normed = rms_scale(model_state, attention_gain).astype(BF)
    query = jnp.dot(normed, query_key_value_weight[:, :width], preferred_element_type=F32).astype(BF)
    own = jnp.dot(normed, query_key_value_weight[:, width:], preferred_element_type=F32).astype(BF)
    beside = jnp.stack([west, east]).reshape(512, width).astype(F32)
    normed_beside = rms_scale(beside, attention_gain).astype(BF)
    halo = jnp.dot(normed_beside, query_key_value_weight[:, width:], preferred_element_type=F32).astype(BF)
    attended = attend(query.reshape(4, 4, 64, width), own.reshape(4, 4, 64, 2 * width), halo.reshape(2, 4, 64, 2 * width))
    first = model_state + jnp.dot(attended.reshape(1024, width), attention_out_weight, preferred_element_type=F32)
    normed_mlp = rms_scale(first, feedforward_gain).astype(BF)
    active = jax.nn.gelu(jnp.dot(normed_mlp, feedforward_up_weight, preferred_element_type=F32)).astype(BF)
    second = first + jnp.dot(active, feedforward_down_weight, preferred_element_type=F32)
    fluxes = lax.dot_general(
        flux_head_weight, second.astype(BF), (((0,), (1,)), ((), ())), preferred_element_type=F32
    ).astype(BF)
    table = lax.all_gather(fluxes, "lon", axis=0, tiled=True)
    forcing = picked_forcing(table, overlay_cell_index, remap_weight)
    lifted = jnp.einsum("nfc,fk->nck", forcing, forcing_lift_weight, preferred_element_type=F32).reshape(64, 64, 192)
    wet = wet_cell_mask.astype(F32)
    field = wet[..., None] * (ocean_features.astype(F32) + lifted)
    taps = tap_rows(depthwise_kernels)
    downs = ocean_down_weights
    (field,) = ocean_block(
        False, ocean_halo(field.astype(BF)), taps[0], ocean_norm_gains[0], ocean_up_weights[0], downs[0], field, wet, surface_temp_head
    )
    ocean_out, temps = ocean_block(
        True, ocean_halo(field.astype(BF)), taps[1], ocean_norm_gains[1], ocean_up_weights[1], downs[1], field, wet, surface_temp_head
    )
    numerator = temps.reshape(32, 2, 32, 2).sum(axis=(1, 3))
    count = wet.reshape(32, 2, 32, 2).sum(axis=(1, 3))
    warmth = numerator / jnp.maximum(count, 1.0)
    warmth = warmth.reshape(4, 8, 4, 8).transpose(0, 2, 1, 3).reshape(1024, 1)
    updated = (second + warmth * surface_temp_embedding).astype(BF)
    updated = updated.reshape(4, 4, 8, 8, width).transpose(0, 2, 1, 3, 4).reshape(32, 32, width)
    return (updated, ocean_out)


def solution(mesh):
    cells = P("lat", "lon", None)
    in_specs = (cells, cells, P("lat", "lon"), P(None, "lat", "lon"), P(None, "lat", "lon")) + (P(),) * 14
    return jax.shard_map(body, mesh=mesh, in_specs=in_specs, out_specs=(cells, cells), check_vma=False)
```

```python
import functools

import jax
import jax.numpy as jnp
import numpy as np
from jax import lax
from jax.experimental import pallas as pl
from jax.experimental.pallas import tpu as pltpu
from jax.sharding import PartitionSpec as P

BF = jnp.bfloat16
F32 = jnp.float32
EPS = 1e-6
MESH = pl.DeviceIdType.MESH
CH = 4
CELLS = 512

def attend_kernel(q_ref, own_ref, halo_ref, out_ref):
    lane=lax.broadcasted_iota(jnp.int32,(128,128),1)
    even=lane<64
    zero=jnp.zeros((128,128),BF)
    def paired(block):
        return jnp.concatenate([jnp.where(even,block,zero),jnp.where(even,zero,block)],axis=0)
    for pair in range(6):
        lanes=slice(128*pair,128*pair+128)
        vl=slice(768+128*pair,768+128*pair+128)
        def window(first,second,query):
            keys=paired(jnp.concatenate([first(lanes),second(lanes)],axis=0))
            vals=paired(jnp.concatenate([first(vl),second(vl)],axis=0))
            s=lax.dot_general(query*BF(0.125),keys,(((1,),(1,)),((),())),preferred_element_type=F32)
            sa=s[:,:128]; sb=s[:,128:]
            ea=jnp.exp(sa-jnp.max(sa,axis=1,keepdims=True)); eb=jnp.exp(sb-jnp.max(sb,axis=1,keepdims=True))
            ra=1.0/jnp.sum(ea,axis=1,keepdims=True); rb=1.0/jnp.sum(eb,axis=1,keepdims=True)
            probs=jnp.concatenate([(ea*ra).astype(BF),(eb*rb).astype(BF)],axis=1)
            return jnp.dot(probs,vals,preferred_element_type=F32).astype(BF)
        own=lambda j: (lambda l: own_ref[0,j,:,l])
        halo=lambda j: (lambda l: halo_ref[j,0,:,l])
        out_ref[0,0,:,lanes]=window(halo(0),own(0),q_ref[0,0,:,lanes])
        mid=window(own(1),own(2),jnp.concatenate([q_ref[0,1,:,lanes],q_ref[0,2,:,lanes]],axis=0))
        out_ref[0,1,:,lanes]=mid[:64]
        out_ref[0,2,:,lanes]=mid[64:]
        out_ref[0,3,:,lanes]=window(own(3),halo(1),q_ref[0,3,:,lanes])

def attend(q,own,halo):
    return pl.pallas_call(attend_kernel,grid=(4,),
        out_shape=jax.ShapeDtypeStruct((4,4,64,768),BF),
        in_specs=[pl.BlockSpec((1,4,64,768),lambda i:(i,0,0,0)),pl.BlockSpec((1,4,64,1536),lambda i:(i,0,0,0)),pl.BlockSpec((2,1,64,1536),lambda i:(0,i,0,0))],
        out_specs=pl.BlockSpec((1,4,64,768),lambda i:(i,0,0,0)),
        compiler_params=pltpu.CompilerParams(vmem_limit_bytes=48*2**20),
        name="attend",
        cost_estimate=pl.CostEstimate(flops=10**10,bytes_accessed=8*2**20,transcendentals=2*10**6),
    )(q,own,halo)


def tap_rows(depthwise_kernels):
    nb=depthwise_kernels.shape[0]
    pick=np.zeros((3,4,4,7),np.float32)
    for d in range(3):
        for q in range(4):
            for p in range(4):
                a=4*(d-1)+q-p+3
                if 0<=a<7: pick[d,q,p,a]=1
    k=depthwise_kernels.reshape(nb,7,7,3,64)
    v=jnp.einsum("dqpa,nabgc->ngdbqpc",jnp.asarray(pick),k, precision=lax.Precision.HIGHEST)
    return v.reshape(nb,3,84,256)

def split(x):
    hi=x.astype(BF)
    return hi,(x-hi.astype(F32)).astype(BF)

def split_dot(x, ones):
    hi,lo=split(x)
    return jnp.dot(hi,ones,preferred_element_type=F32)+jnp.dot(lo,ones,preferred_element_type=F32)

def gelu(x):
    inner=x*(0.7978845608028654+0.035677408136300125*(x*x))
    h=0.5*x
    return h+h*jnp.tanh(inner)

NT=(((1,),(1,)),((),()))

def ocean_kernel(comm, field_ref, v_ref, gain_ref, up_ref, down_ref, wet_ref, head_ref, out_ref, sst_ref,
                 next_ref, w_ref, x4_ref, a_ref, y_ref, n_ref, rows_send, rows_recv, side_send, side_recv, corner_send, corner_recv, send_sem, recv_sem):
    if comm:
        lat=lax.axis_index("lat"); lon=lax.axis_index("lon")
        lats=lax.axis_size("lat"); lons=lax.axis_size("lon")
        top=lat==lats-1; bottom=lat==0
        mirror=lons-1-lon
        up_id=(jnp.where(top,lat,lat+1),jnp.where(top,mirror,lon))
        down_id=(jnp.where(bottom,lat,lat-1),jnp.where(bottom,mirror,lon))
        west_id=(lat,lax.rem(lon+lons-1,lons)); east_id=(lat,lax.rem(lon+1,lons))
        barrier=pltpu.get_barrier_semaphore()
        for other in (up_id,down_id,west_id,east_id):
            pl.semaphore_signal(barrier,inc=1,device_id=other,device_id_type=MESH)
        up_slot=jnp.where(top,0,1)
        down_slot=jnp.where(bottom,1,0)
    sub=lax.broadcasted_iota(jnp.int32,(64,256),0)
    lane=lax.broadcasted_iota(jnp.int32,(64,256),1)
    diag=(lane%64)==sub
    s2=lax.broadcasted_iota(jnp.int32,(256,256),0)//64
    l2=lax.broadcasted_iota(jnp.int32,(256,256),1)//64
    ones=jnp.where(s2==l2,1.0,0.0).astype(BF)
    flip=jnp.where(lax.broadcasted_iota(jnp.int32,(64,64),0)+lax.broadcasted_iota(jnp.int32,(64,64),1)==63,1.0,0.0).astype(BF)

    for blk in range(2):
        src=field_ref if blk==0 else next_ref
        def remote(source,target,index,slot,device):
            return pltpu.make_async_remote_copy(src_ref=source,dst_ref=target,send_sem=send_sem.at[blk,index],recv_sem=recv_sem.at[blk,slot],device_id=device,device_id_type=MESH)
        if comm:
            for k in range(3):
                turned=jnp.dot(flip,src[63-k].astype(BF),preferred_element_type=F32)
                rows_send[blk,0,k]=jnp.where(top,turned,src[61+k]).astype(BF)
                rows_send[blk,1,k]=src[k].astype(BF)
            side_send[blk,0]=src[:,0:8,:].astype(BF)
            side_send[blk,1]=src[:,56:64,:].astype(BF)
            if blk==0:
                pl.semaphore_wait(barrier,4)
            copies=[remote(rows_send.at[blk,0],rows_recv.at[blk,up_slot],0,up_slot,up_id),
                    remote(rows_send.at[blk,1],rows_recv.at[blk,down_slot],1,down_slot,down_id),
                    remote(side_send.at[blk,0],side_recv.at[blk,1],2,3,west_id),
                    remote(side_send.at[blk,1],side_recv.at[blk,0],3,2,east_id)]
            for c in copies: c.start()
        for g in range(3):
            def build(t, _):
                for q in range(4):
                    row=v_ref[blk,g, pl.ds(t*4+q,1), :]
                    w_ref[g, pl.ds(pl.multiple_of(t*256+q*64,64),64), :]=jnp.where(diag,row,0.0).astype(BF)
                return 0
            lax.fori_loop(0,21,build,0)
        if comm:
            remote(rows_send.at[blk,0],rows_recv.at[blk,0],0,0,up_id).wait_recv()
            remote(rows_send.at[blk,0],rows_recv.at[blk,1],0,1,up_id).wait_recv()
            for s in range(2):
                corner_send[blk,0,s]=rows_recv[blk,s,:,0:8,:]
                corner_send[blk,1,s]=rows_recv[blk,s,:,56:64,:]
            more=[remote(corner_send.at[blk,0],corner_recv.at[blk,1],4,5,west_id),
                  remote(corner_send.at[blk,1],corner_recv.at[blk,0],5,4,east_id)]
            for c in more: c.start()
            remote(side_send.at[blk,0],side_recv.at[blk,0],2,2,west_id).wait_recv()
            remote(side_send.at[blk,0],side_recv.at[blk,1],2,3,west_id).wait_recv()
        def place(i,rows):
            for g in range(3):
                x4_ref[g]=jnp.concatenate([r[:,64*g:64*g+64] for r in rows],axis=1)
                for b in range(7):
                    a_ref[g,i,:,256*b:256*b+256]=x4_ref[g,pl.ds(5+b,64),:].astype(BF)
        def group(i,_):
            rows=[]
            for p in range(4):
                r=4*(i-1)+p
                rows.append(jnp.concatenate([side_recv[blk,0,r].astype(F32),src[r],side_recv[blk,1,r].astype(F32)],axis=0))
            place(i,rows)
            return 0
        lax.fori_loop(1,17,group,0)
        if comm:
            remote(corner_send.at[blk,0],corner_recv.at[blk,0],4,4,west_id).wait_recv()
            remote(corner_send.at[blk,0],corner_recv.at[blk,1],4,5,west_id).wait_recv()
        empty=jnp.zeros((80,192),F32)
        def outer(s,k):
            return jnp.concatenate([corner_recv[blk,0,s,k].astype(F32),rows_recv[blk,s,k].astype(F32),corner_recv[blk,1,s,k].astype(F32)],axis=0)
        place(17,[outer(0,k) for k in range(3)]+[empty])
        souths=[outer(1,k) for k in range(3)]
        if comm:
            souths=[jnp.where(bottom,0.0,s) for s in souths]
        place(0,[empty]+souths)
        def conv(ci):
            base=ci*CH
            for g in range(3):
                acc=None
                for d in range(3):
                    lhs=a_ref[g,pl.ds(base+d,CH)].reshape(CH*64,1792)
                    part=jnp.dot(lhs,w_ref[g,d*1792:(d+1)*1792,:],preferred_element_type=F32)
                    acc=part if acc is None else acc+part
                y_ref[g]=acc
        def norm():
            tot=y_ref[0]+y_ref[1]+y_ref[2]
            mean=split_dot(tot,ones)*(1/192)
            cs=[y_ref[g]-mean for g in range(3)]
            var=split_dot(cs[0]*cs[0]+cs[1]*cs[1]+cs[2]*cs[2],ones)*(1/192)
            inv=lax.rsqrt(var+EPS)
            ns=[(cs[g]*inv*gain_ref[blk,g]).astype(BF) for g in range(3)]
            for p in range(4):
                n_ref[p]=jnp.concatenate([ns[g][:,64*p:64*p+64] for g in range(3)],axis=1)
        def mlp(ci):
            base=ci*CH
            temps=[]
            for p in range(4):
                act=gelu(jnp.dot(n_ref[p],up_ref[blk],preferred_element_type=F32)).astype(BF)
                inc=lax.dot_general(act,down_ref[blk],NT,preferred_element_type=F32)
                wet=wet_ref[ci,p]
                news=[]
                for j in range(CH):
                    r=4*(base+j)+p
                    new=src[r]+wet[:,j:j+1]*inc[64*j:64*j+64]
                    if blk==1:
                        out_ref[r]=new.astype(BF)
                        news.append(new)
                    else:
                        next_ref[r]=new
                if blk==1:
                    hi,lo=split(jnp.concatenate(news,axis=0))
                    hh,hl=split(head_ref[...])
                    dot=lambda a,b: lax.dot_general(a,b,NT,preferred_element_type=F32)
                    temps.append(dot(hh,hi)+dot(hh,lo)+dot(hl,hi))
            if blk==1:
                sst_ref[ci,0]=temps[0]+temps[1]
                sst_ref[ci,1]=temps[2]+temps[3]
        conv(0)
        def step(ci,_):
            norm()
            conv(ci)
            mlp(ci-1)
            return 0
        lax.fori_loop(1,16//CH,step,0)
        norm()
        mlp(16//CH-1)
        if comm:
            for c in copies+more: c.wait_send()

def ocean_blocks(comm,field,v,gains,up,down,wet,head):
    gain_t=jnp.tile(gains.reshape(2,3,1,64),(1,1,4,1)).reshape(2,3,1,256)
    wt=wet.reshape(16//CH,CH,4,64).transpose(0,2,3,1)
    vm=pl.BlockSpec(memory_space=pltpu.VMEM)
    outs=[jax.ShapeDtypeStruct((64,64,192),BF),jax.ShapeDtypeStruct((16//CH,2,8,CH*64),F32)]
    out,sst=pl.pallas_call(functools.partial(ocean_kernel,comm),
        out_shape=outs, in_specs=[vm]*7, out_specs=[vm]*2,
        scratch_shapes=[pltpu.VMEM((64,64,192),F32),pltpu.VMEM((3,21*256,256),BF),pltpu.VMEM((3,80,256),F32),pltpu.VMEM((3,18,64,1792),BF),pltpu.VMEM((3,CH*64,256),F32),pltpu.VMEM((4,CH*64,192),BF),
            pltpu.VMEM((2,2,3,64,192),BF),pltpu.VMEM((2,2,3,64,192),BF),pltpu.VMEM((2,2,64,8,192),BF),pltpu.VMEM((2,2,64,8,192),BF),pltpu.VMEM((2,2,2,3,8,192),BF),pltpu.VMEM((2,2,2,3,8,192),BF),
            pltpu.SemaphoreType.DMA((2,6)),pltpu.SemaphoreType.DMA((2,6))],
        compiler_params=pltpu.CompilerParams(vmem_limit_bytes=60*2**20,**(dict(collective_id=1,has_side_effects=True) if comm else {})),
        name="ocean",
        cost_estimate=pl.CostEstimate(flops=40*10**9,bytes_accessed=8*2**20,transcendentals=3*10**6),
    )(field,v,gain_t,up,down,wt,jnp.broadcast_to(head.reshape(1,192),(8,192)))
    rows=sst[:,:,0].reshape(16//CH,2,CH,64).transpose(0,2,1,3).reshape(32,64)
    return out,rows


def pick_kernel(flux_ref, lo_ref, hi_ref, w_ref, lift_ref, ocean_ref, wet_ref, out_ref, table_ref, t_ref, send_sem, recv_sem):
    lat = lax.axis_index("lat")
    lon = lax.axis_index("lon")
    count = lax.axis_size("lon")
    barrier = pltpu.get_barrier_semaphore()

    def greet(k, _):
        pl.semaphore_signal(barrier, inc=1, device_id=(lat, lax.rem(lon + k, count)), device_id_type=MESH)
        return 0

    lax.fori_loop(1, count, greet, 0)
    pl.semaphore_wait(barrier, count - 1)

    def to_peer(k):
        return pltpu.make_async_remote_copy(
            src_ref=flux_ref, dst_ref=table_ref.at[lon], send_sem=send_sem.at[k], recv_sem=recv_sem.at[lon],
            device_id=(lat, lax.rem(lon + k, count)), device_id_type=MESH,
        )

    def send(k, _):
        to_peer(k).start()
        return 0

    lax.fori_loop(1, count, send, 0)
    table_ref[lon] = flux_ref[...]

    def receive(k, _):
        peer = lax.rem(lon + k, count)
        pltpu.make_async_remote_copy(
            src_ref=flux_ref, dst_ref=table_ref.at[peer], send_sem=send_sem.at[k], recv_sem=recv_sem.at[peer],
            device_id=(lat, peer), device_id_type=MESH,
        ).wait_recv()
        return 0

    lax.fori_loop(1, count, receive, 0)
    whole = table_ref[...].astype(F32).reshape(128, 1024).astype(BF)
    for h in range(4):
        t_ref[128 * h : 128 * h + 128, :] = whole[:, 256 * h : 256 * h + 256]
    ids = lax.broadcasted_iota(jnp.int32, (256, CELLS), 0)
    lift_hi, lift_lo = split(lift_ref[...])
    lift = jnp.concatenate([lift_hi, lift_hi, lift_lo], axis=0)

    def chunk(i, _):
        total = jnp.zeros((8, CELLS), F32)
        for e in range(4):
            lo = lo_ref[e, pl.ds(i, 1), :]
            hit = jnp.where(ids == lo, 1.0, 0.0).astype(BF)
            res = jnp.dot(t_ref[...], hit, preferred_element_type=F32)
            hi = jnp.broadcast_to(hi_ref[e, pl.ds(i, 1), :], (8, CELLS))
            got = res[0:8]
            for k in range(1, 64):
                got = jnp.where(hi == k, res[8 * k : 8 * k + 8], got)
            total = total + got * w_ref[e, pl.ds(i, 1), :]
        high = total.astype(BF).astype(F32)
        low = total - high
        spread = jnp.concatenate([high, low, high], axis=0).astype(BF)
        lifted = lax.dot_general(spread, lift, (((0,), (0,)), ((), ())), preferred_element_type=F32)
        wet = wet_ref[i]
        for j in range(8):
            row = ocean_ref[8 * i + j].astype(F32) + lifted[64 * j : 64 * j + 64]
            out_ref[8 * i + j] = wet[:, j : j + 1] * row
        return 0

    lax.fori_loop(0, 4096 // CELLS, chunk, 0)

    def sent(k, _):
        to_peer(k).wait_send()
        return 0

    lax.fori_loop(1, count, sent, 0)


def forced_ocean(fluxes, idx, w, lift, ocean, wet):
    lo = ((idx >> 3) & 3) << 6 | ((idx >> 9) & 7) << 3 | (idx & 7)
    hi = ((idx >> 12) & 3) << 4 | ((idx >> 5) & 15)
    n = 4096 // CELLS
    lo = lo.reshape(4, n, CELLS)
    hi = hi.reshape(4, n, CELLS)
    w = w.reshape(4, n, CELLS)
    wt = wet.reshape(8, 8, 64).transpose(0, 2, 1)
    vm = pl.BlockSpec(memory_space=pltpu.VMEM)
    return pl.pallas_call(
        pick_kernel,
        out_shape=jax.ShapeDtypeStruct((64, 64, 192), F32),
        in_specs=[vm] * 7,
        out_specs=vm,
        scratch_shapes=[
            pltpu.VMEM((16, 8, 1024), BF),
            pltpu.VMEM((512, 256), BF),
            pltpu.SemaphoreType.DMA((16,)),
            pltpu.SemaphoreType.DMA((16,)),
        ],
        compiler_params=pltpu.CompilerParams(vmem_limit_bytes=48 * 2**20, collective_id=0, has_side_effects=True),
        name="pick",
        cost_estimate=pl.CostEstimate(flops=10**10, bytes_accessed=2**20, transcendentals=0),
    )(fluxes, lo, hi, w, lift, ocean, wt)


def ring(axis):
    count = lax.axis_size(axis)
    forward = [(i, (i + 1) % count) for i in range(count)]
    return forward, [(target, source) for source, target in forward]


def rms_scale(values, gain):
    return values * lax.rsqrt(jnp.mean(values * values, axis=-1, keepdims=True) + EPS) * gain


def body(
    atmos_features,
    ocean_features,
    wet_cell_mask,
    overlay_cell_index,
    remap_weight,
    query_key_value_weight,
    attention_out_weight,
    feedforward_up_weight,
    feedforward_down_weight,
    attention_gain,
    feedforward_gain,
    flux_head_weight,
    surface_temp_embedding,
    forcing_lift_weight,
    depthwise_kernels,
    ocean_norm_gains,
    ocean_up_weights,
    ocean_down_weights,
    surface_temp_head,
):
    width = atmos_features.shape[2]
    blocks = atmos_features.reshape(4, 8, 4, 8, width).transpose(0, 2, 1, 3, 4).reshape(4, 4, 64, width)
    forward, backward = ring("lon")
    west = lax.ppermute(blocks[:, 3], "lon", forward)
    east = lax.ppermute(blocks[:, 0], "lon", backward)
    model_state = blocks.reshape(1024, width).astype(F32)
    normed = rms_scale(model_state, attention_gain).astype(BF)
    query = jnp.dot(normed, query_key_value_weight[:, :width], preferred_element_type=F32).astype(BF)
    own = jnp.dot(normed, query_key_value_weight[:, width:], preferred_element_type=F32).astype(BF)
    beside = jnp.stack([west, east]).reshape(512, width).astype(F32)
    normed_beside = rms_scale(beside, attention_gain).astype(BF)
    halo = jnp.dot(normed_beside, query_key_value_weight[:, width:], preferred_element_type=F32).astype(BF)
    attended = attend(query.reshape(4, 4, 64, width), own.reshape(4, 4, 64, 2 * width), halo.reshape(2, 4, 64, 2 * width))
    first = model_state + jnp.dot(attended.reshape(1024, width), attention_out_weight, preferred_element_type=F32)
    normed_mlp = rms_scale(first, feedforward_gain).astype(BF)
    active = jax.nn.gelu(jnp.dot(normed_mlp, feedforward_up_weight, preferred_element_type=F32)).astype(BF)
    second = first + jnp.dot(active, feedforward_down_weight, preferred_element_type=F32)
    fluxes = lax.dot_general(
        flux_head_weight, second.astype(BF), (((0,), (1,)), ((), ())), preferred_element_type=F32
    ).astype(BF)
    wet = wet_cell_mask.astype(F32)
    field = forced_ocean(fluxes, overlay_cell_index, remap_weight, forcing_lift_weight, ocean_features, wet)
    ocean_out, temps = ocean_blocks(
        True, field, tap_rows(depthwise_kernels), ocean_norm_gains, ocean_up_weights,
        jnp.swapaxes(ocean_down_weights, 1, 2), wet, surface_temp_head,
    )
    numerator = temps.reshape(32, 32, 2).sum(axis=2)
    count = wet.reshape(32, 2, 32, 2).sum(axis=(1, 3))
    warmth = numerator / jnp.maximum(count, 1.0)
    warmth = warmth.reshape(4, 8, 4, 8).transpose(0, 2, 1, 3).reshape(1024, 1)
    updated = (second + warmth * surface_temp_embedding).astype(BF)
    updated = updated.reshape(4, 4, 8, 8, width).transpose(0, 2, 1, 3, 4).reshape(32, 32, width)
    return (updated, ocean_out)


def solution(mesh):
    cells = P("lat", "lon", None)
    in_specs = (cells, cells, P("lat", "lon"), P(None, "lat", "lon"), P(None, "lat", "lon")) + (P(),) * 14
    return jax.shard_map(body, mesh=mesh, in_specs=in_specs, out_specs=(cells, cells), check_vma=False)
```

```python
import functools

import jax
import jax.numpy as jnp
from jax import lax
from jax.experimental import pallas as pl
from jax.experimental.pallas import tpu as pltpu
from jax.sharding import PartitionSpec as P

BF = jnp.bfloat16
F32 = jnp.float32
EPS = 1e-6
MESH = pl.DeviceIdType.MESH
CH = 4

CELLS = 512
def split(x):
    hi=x.astype(BF)
    return hi,(x-hi.astype(F32)).astype(BF)

def split_dot(x, ones):
    hi,lo=split(x)
    return jnp.dot(hi,ones,preferred_element_type=F32)+jnp.dot(lo,ones,preferred_element_type=F32)

def gelu(x):
    inner=x*(0.7978845608028654+0.035677408136300125*(x*x))
    h=0.5*x
    return h+h*jnp.tanh(inner)

NT = (((1,),(1,)),((),()))


def ocean_kernel(comm, flux_ref, index_ref, remap_ref, lift_ref, ocean_ref, wet_ref, taps_ref, gains_ref, up_ref, down_ref, head_ref, second_hbm, embed_ref,
                 updated_ref, out_ref, field_ref, next_ref, second_ref, table_ref, t_ref, wet_t, taps_pair, w_ref, x4_ref, a_ref, y_ref, n_ref, warm_ref,
                 rows_send, rows_recv, side_send, side_recv, corner_send, corner_recv, load_sem, flux_send, flux_recv, send_sem, recv_sem):
    load = pltpu.make_async_copy(second_hbm, second_ref, load_sem)
    load.start()
    if comm:
        lat = lax.axis_index("lat")
        lon = lax.axis_index("lon")
        lats = lax.axis_size("lat")
        lons = lax.axis_size("lon")
        top = lat == lats - 1
        bottom = lat == 0
        mirror = lons - 1 - lon
        up_id = (jnp.where(top, lat, lat + 1), jnp.where(top, mirror, lon))
        down_id = (jnp.where(bottom, lat, lat - 1), jnp.where(bottom, mirror, lon))
        west_id = (lat, lax.rem(lon + lons - 1, lons))
        east_id = (lat, lax.rem(lon + 1, lons))
        barrier = pltpu.get_barrier_semaphore()

        def greet(k, _):
            pl.semaphore_signal(barrier, inc=1, device_id=(lat, lax.rem(lon + k, lons)), device_id_type=MESH)
            return 0

        lax.fori_loop(1, lons, greet, 0)
        for other in (up_id, down_id):
            pl.semaphore_signal(barrier, inc=1, device_id=other, device_id_type=MESH)
        pl.semaphore_wait(barrier, lons + 1)
        up_slot = jnp.where(top, 0, 1)
        down_slot = jnp.where(bottom, 1, 0)

        def to_peer(k):
            return pltpu.make_async_remote_copy(
                src_ref=flux_ref, dst_ref=table_ref.at[lon], send_sem=flux_send.at[k], recv_sem=flux_recv.at[lon],
                device_id=(lat, lax.rem(lon + k, lons)), device_id_type=MESH,
            )

        def send(k, _):
            to_peer(k).start()
            return 0

        lax.fori_loop(1, lons, send, 0)
        table_ref[lon] = flux_ref[...]
    else:
        for d in range(16):
            table_ref[d] = flux_ref[...]

    wet = wet_ref[...].astype(F32)
    wet_t[...] = jnp.concatenate([wet, wet], axis=0).T

    def wet_from(row):
        return pltpu.roll(wet_t[...], 128 - row, axis=1)

    for blk in range(2):
        for g in range(3):
            piece = taps_ref[blk][:, 64 * g : 64 * g + 64]
            taps_pair[blk, g, 0:49] = jnp.concatenate([piece, piece], axis=1)
    sub = lax.broadcasted_iota(jnp.int32, (64, 128), 0)
    lane = lax.broadcasted_iota(jnp.int32, (64, 128), 1)
    low_diag = lane == sub
    high_diag = lane == sub + 64
    s2 = lax.broadcasted_iota(jnp.int32, (256, 256), 0) // 64
    l2 = lax.broadcasted_iota(jnp.int32, (256, 256), 1) // 64
    ones = jnp.where(s2 == l2, 1.0, 0.0).astype(BF)
    flip = lax.broadcasted_iota(jnp.int32, (64, 64), 0) + lax.broadcasted_iota(jnp.int32, (64, 64), 1)
    flip = jnp.where(flip == 63, 1.0, 0.0).astype(BF)

    def build_weights(blk):
        def build(b, _):
            for g in range(3):
                for d in range(3):
                    for q in range(4):
                        halves = []
                        for half in range(2):
                            a = 4 * (d - 1) + q - 2 * half + 3
                            value = jnp.zeros((64, 128), F32)
                            if 0 <= a - 1 < 7:
                                value = jnp.where(high_diag, taps_pair[blk, g, pl.ds(7 * (a - 1) + b, 1), :], value)
                            if 0 <= a < 7:
                                value = jnp.where(low_diag, taps_pair[blk, g, pl.ds(7 * a + b, 1), :], value)
                            halves.append(value.astype(BF))
                        row = pl.multiple_of(b * 256, 256) + (1792 * d + 64 * q)
                        w_ref[g, pl.ds(pl.multiple_of(row, 64), 64), :] = jnp.concatenate(halves, axis=1)
            return 0

        lax.fori_loop(0, 7, build, 0)

    build_weights(0)

    if comm:

        def receive(k, _):
            peer = lax.rem(lon + k, lons)
            pltpu.make_async_remote_copy(
                src_ref=flux_ref, dst_ref=table_ref.at[peer], send_sem=flux_send.at[k], recv_sem=flux_recv.at[peer],
                device_id=(lat, peer), device_id_type=MESH,
            ).wait_recv()
            return 0

        lax.fori_loop(1, lons, receive, 0)
    for h in range(4):
        t_ref[128 * h : 128 * h + 128, :] = table_ref[:, h].astype(F32).reshape(128, 256).astype(BF)
    ids = lax.broadcasted_iota(jnp.int32, (256, CELLS), 0)
    lift_hi, lift_lo = split(lift_ref[...])
    lift = jnp.concatenate([lift_hi, lift_hi, lift_lo], axis=0)

    def line(rows):
        return jnp.concatenate([rows[j : j + 1] for j in range(8)], axis=1)

    def force(i, _):
        total = jnp.zeros((8, CELLS), F32)
        for e in range(4):
            index = line(index_ref[e, pl.ds(pl.multiple_of(8 * i, 8), 8), :])
            lo = (index & 24) << 3 | ((index >> 9) & 7) << 3 | (index & 7)
            hi = jnp.broadcast_to((index >> 12) << 4 | ((index >> 5) & 15), (8, CELLS))
            hit = jnp.where(ids == lo, 1.0, 0.0).astype(BF)
            res = jnp.dot(t_ref[...], hit, preferred_element_type=F32)
            got = res[0:8]
            for k in range(1, 64):
                got = jnp.where(hi == k, res[8 * k : 8 * k + 8], got)
            total = total + got * line(remap_ref[e, pl.ds(pl.multiple_of(8 * i, 8), 8), :])
        high = total.astype(BF).astype(F32)
        spread = jnp.concatenate([high, total - high, high], axis=0).astype(BF)
        lifted = lax.dot_general(spread, lift, (((0,), (0,)), ((), ())), preferred_element_type=F32)
        here = wet_from(8 * i)
        for j in range(8):
            row = ocean_ref[8 * i + j].astype(F32) + lifted[64 * j : 64 * j + 64]
            field_ref[8 * i + j] = here[:, j : j + 1] * row
        return 0

    lax.fori_loop(0, 4096 // CELLS, force, 0)

    for blk in range(2):
        src = field_ref if blk == 0 else next_ref

        def remote(source, target, index, slot, device):
            return pltpu.make_async_remote_copy(
                src_ref=source, dst_ref=target, send_sem=send_sem.at[blk, index], recv_sem=recv_sem.at[blk, slot],
                device_id=device, device_id_type=MESH,
            )

        if comm:
            for k in range(3):
                turned = jnp.dot(flip, src[63 - k].astype(BF), preferred_element_type=F32)
                rows_send[blk, 0, k] = jnp.where(top, turned, src[61 + k]).astype(BF)
                rows_send[blk, 1, k] = src[k].astype(BF)
            early = lax.broadcasted_iota(jnp.int32, (32, 8, 192), 1) < 4
            west = src[:, 0:8, :].reshape(32, 2, 8, 192)
            east = src[:, 56:64, :].reshape(32, 2, 8, 192)
            side_send[blk, 0] = jnp.where(early, west[:, 0], pltpu.roll(west[:, 1], 4, axis=1)).astype(BF)
            side_send[blk, 1] = jnp.where(early, pltpu.roll(east[:, 0], 4, axis=1), east[:, 1]).astype(BF)
            copies = [
                remote(rows_send.at[blk, 0], rows_recv.at[blk, up_slot], 0, up_slot, up_id),
                remote(rows_send.at[blk, 1], rows_recv.at[blk, down_slot], 1, down_slot, down_id),
                remote(side_send.at[blk, 0], side_recv.at[blk, 1], 2, 3, west_id),
                remote(side_send.at[blk, 1], side_recv.at[blk, 0], 3, 2, east_id),
            ]
            for c in copies:
                c.start()
        if blk == 1:
            build_weights(1)
        if comm:
            remote(rows_send.at[blk, 0], rows_recv.at[blk, 0], 0, 0, up_id).wait_recv()
            remote(rows_send.at[blk, 0], rows_recv.at[blk, 1], 0, 1, up_id).wait_recv()
            for s in range(2):
                corner_send[blk, 0, s] = rows_recv[blk, s, :, 0:8, :]
                corner_send[blk, 1, s] = rows_recv[blk, s, :, 56:64, :]
            more = [
                remote(corner_send.at[blk, 0], corner_recv.at[blk, 1], 4, 5, west_id),
                remote(corner_send.at[blk, 1], corner_recv.at[blk, 0], 5, 4, east_id),
            ]
            for c in more:
                c.start()
            remote(side_send.at[blk, 0], side_recv.at[blk, 0], 2, 2, west_id).wait_recv()
            remote(side_send.at[blk, 0], side_recv.at[blk, 1], 2, 3, west_id).wait_recv()

        def place(i, rows):
            for g in range(3):
                x4_ref[g] = jnp.concatenate([r[:, 64 * g : 64 * g + 64] for r in rows], axis=1)
                for b in range(7):
                    a_ref[g, i, :, 256 * b : 256 * b + 256] = x4_ref[g, pl.ds(5 + b, 64), :].astype(BF)

        def group(i, _):
            rows = []
            for p in range(4):
                r = 4 * (i - 1) + p
                west = side_recv[blk, 0, 2 * (i - 1) + p // 2].astype(F32)
                east = side_recv[blk, 1, 2 * (i - 1) + p // 2].astype(F32)
                if p % 2 == 0:
                    west = pltpu.roll(west, 4, axis=0)
                else:
                    east = pltpu.roll(east, 4, axis=0)
                rows.append(jnp.concatenate([west, src[r], east], axis=0))
            place(i, rows)
            return 0

        lax.fori_loop(1, 17, group, 0)
        if comm:
            remote(corner_send.at[blk, 0], corner_recv.at[blk, 0], 4, 4, west_id).wait_recv()
            remote(corner_send.at[blk, 0], corner_recv.at[blk, 1], 4, 5, west_id).wait_recv()
        empty = jnp.zeros((80, 192), F32)

        def outer(s, k):
            pieces = [corner_recv[blk, 0, s, k], rows_recv[blk, s, k], corner_recv[blk, 1, s, k]]
            return jnp.concatenate([piece.astype(F32) for piece in pieces], axis=0)

        place(17, [outer(0, k) for k in range(3)] + [empty])
        souths = [outer(1, k) for k in range(3)]
        if comm:
            souths = [jnp.where(bottom, 0.0, s) for s in souths]
        place(0, [empty] + souths)

        def conv(ci):
            base = ci * CH
            for g in range(3):
                acc = None
                for d in range(3):
                    lhs = a_ref[g, pl.ds(base + d, CH)].reshape(CH * 64, 1792)
                    part = jnp.dot(lhs, w_ref[g, d * 1792 : (d + 1) * 1792, :], preferred_element_type=F32)
                    acc = part if acc is None else acc + part
                y_ref[g] = acc

        gains = [jnp.concatenate([gains_ref[blk : blk + 1, 64 * g : 64 * g + 64]] * 4, axis=1) for g in range(3)]

        def norm():
            mean = split_dot(y_ref[0] + y_ref[1] + y_ref[2], ones) * (1 / 192)
            cs = [y_ref[g] - mean for g in range(3)]
            var = split_dot(cs[0] * cs[0] + cs[1] * cs[1] + cs[2] * cs[2], ones) * (1 / 192)
            inv = lax.rsqrt(var + EPS)
            ns = [(cs[g] * inv * gains[g]).astype(BF) for g in range(3)]
            for p in range(4):
                n_ref[p] = jnp.concatenate([ns[g][:, 64 * p : 64 * p + 64] for g in range(3)], axis=1)

        def mlp(ci):
            base = ci * CH
            here = wet_from(16 * ci)
            temps = []
            for p in range(4):
                act = gelu(jnp.dot(n_ref[p], up_ref[blk], preferred_element_type=F32)).astype(BF)
                inc = lax.dot_general(act, down_ref[blk], NT, preferred_element_type=F32)
                news = []
                for j in range(CH):
                    r = 4 * (base + j) + p
                    new = src[r] + here[:, 4 * j + p : 4 * j + p + 1] * inc[64 * j : 64 * j + 64]
                    if blk == 1:
                        out_ref[r] = new.astype(BF)
                        news.append(new)
                    else:
                        next_ref[r] = new
                if blk == 1:
                    hi, lo = split(jnp.concatenate(news, axis=0))
                    head_hi, head_lo = split(jnp.broadcast_to(head_ref[...].reshape(1, 192), (128, 192)))
                    temps.append(
                        lax.dot_general(hi, head_hi, NT, preferred_element_type=F32)
                        + lax.dot_general(lo, head_hi, NT, preferred_element_type=F32)
                        + lax.dot_general(hi, head_lo, NT, preferred_element_type=F32)
                    )
            if blk == 1:
                for s in range(2):
                    warm_ref[0] = temps[2 * s] + temps[2 * s + 1]
                    for j in range(CH):
                        both = here[:, 4 * j + 2 * s : 4 * j + 2 * s + 1] + here[:, 4 * j + 2 * s + 1 : 4 * j + 2 * s + 2]
                        warm_ref[1, 64 * j : 64 * j + 64] = jnp.broadcast_to(both, (64, 128))
                    pair = lambda k: warm_ref[k, pl.ds(0, 128, stride=2), :] + warm_ref[k, pl.ds(1, 128, stride=2), :]
                    warmth = pair(0) / jnp.maximum(pair(1), 1.0)
                    for j in range(CH):
                        r = 2 * j + s
                        old = jnp.concatenate([second_ref[ci, 64 * c + 8 * r : 64 * c + 8 * r + 8, :] for c in range(4)], axis=0)
                        row = jnp.concatenate([warmth[32 * j : 32 * j + 32]] * 6, axis=1)
                        updated_ref[8 * ci + r] = (old + row * embed_ref[...].reshape(1, 768)).astype(BF)

        conv(0)
        if blk == 1:
            load.wait()

        def step(ci, _):
            norm()
            conv(ci)
            mlp(ci - 1)
            return 0

        lax.fori_loop(1, 16 // CH, step, 0)
        norm()
        mlp(16 // CH - 1)
        if comm:
            for c in copies + more:
                c.wait_send()
    if comm:

        def sent(k, _):
            to_peer(k).wait_send()
            return 0

        lax.fori_loop(1, lons, sent, 0)


def ocean_step(comm, fluxes, idx, remap, lift, ocean, wet, taps, gains, up, down, head, second, embed):
    vm = pl.BlockSpec(memory_space=pltpu.VMEM)
    far = pl.BlockSpec(memory_space=pl.ANY)
    width = second.shape[-1]
    dma = pltpu.SemaphoreType.DMA
    params = dict(collective_id=1, has_side_effects=True) if comm else {}
    return pl.pallas_call(
        functools.partial(ocean_kernel, comm),
        out_shape=[jax.ShapeDtypeStruct((32, 32, width), BF), jax.ShapeDtypeStruct((64, 64, 192), BF)],
        in_specs=[vm] * 11 + [far, vm],
        out_specs=[vm] * 2,
        scratch_shapes=[
            pltpu.VMEM((64, 64, 192), F32), pltpu.VMEM((64, 64, 192), F32), pltpu.VMEM((4, 256, width), F32),
            pltpu.VMEM((16, 4, 8, 256), BF), pltpu.VMEM((512, 256), BF), pltpu.VMEM((64, 128), F32), pltpu.VMEM((2, 3, 56, 128), F32),
            pltpu.VMEM((3, 21 * 256, 256), BF), pltpu.VMEM((3, 80, 256), F32), pltpu.VMEM((3, 18, 64, 1792), BF),
            pltpu.VMEM((3, CH * 64, 256), F32), pltpu.VMEM((4, CH * 64, 192), BF), pltpu.VMEM((2, CH * 64, 128), F32),
            pltpu.VMEM((2, 2, 3, 64, 192), BF), pltpu.VMEM((2, 2, 3, 64, 192), BF),
            pltpu.VMEM((2, 2, 32, 8, 192), BF), pltpu.VMEM((2, 2, 32, 8, 192), BF),
            pltpu.VMEM((2, 2, 2, 3, 8, 192), BF), pltpu.VMEM((2, 2, 2, 3, 8, 192), BF),
            dma, dma((16,)), dma((16,)), dma((2, 6)), dma((2, 6)),
        ],
        compiler_params=pltpu.CompilerParams(vmem_limit_bytes=60 * 2**20, **params),
        name="ocean",
        cost_estimate=pl.CostEstimate(flops=50 * 10**9, bytes_accessed=16 * 2**20, transcendentals=6 * 10**6),
    )(fluxes, idx, remap, lift, ocean, wet, taps, gains, up, down, head, second, embed)


def air_kernel(comm, x_ref, gain_attn_ref, gain_mlp_ref, qkv_hbm, out_hbm, up_hbm, down_hbm, head_ref, second_ref, flux_ref,
               qkv_w, out_w, up_w, down_w, normed, edge_send, edge_recv, qkv, beside, mixed, load_sem, send_sem, recv_sem):
    width = x_ref.shape[-1]
    loads = [
        pltpu.make_async_copy(source, target, load_sem.at[i])
        for i, (source, target) in enumerate(((qkv_hbm, qkv_w), (out_hbm, out_w), (up_hbm, up_w), (down_hbm, down_w)))
    ]
    for load in loads:
        load.start()
    if comm:
        lat = lax.axis_index("lat")
        lon = lax.axis_index("lon")
        count = lax.axis_size("lon")
        west_id = (lat, lax.rem(lon + count - 1, count))
        east_id = (lat, lax.rem(lon + 1, count))
        barrier = pltpu.get_barrier_semaphore()
        for other in (west_id, east_id):
            pl.semaphore_signal(barrier, inc=1, device_id=other, device_id_type=MESH)

    def cells(band, j):
        return x_ref[band, :, 8 * j : 8 * j + 8, :].astype(F32).reshape(64, width)

    def rms(values, gain):
        return (values * lax.rsqrt(jnp.mean(values * values, axis=1, keepdims=True) + EPS) * gain).astype(BF)

    for band in range(4):
        for side, j in ((0, 0), (1, 3)):
            block = rms(cells(band, j), gain_attn_ref[...].reshape(1, width))
            normed[band, j] = block
            edge_send[side, band] = block
    if comm:
        pl.semaphore_wait(barrier, 2)
        copies = [
            pltpu.make_async_remote_copy(
                src_ref=edge_send.at[side], dst_ref=edge_recv.at[1 - side], send_sem=send_sem.at[side],
                recv_sem=recv_sem.at[1 - side], device_id=device, device_id_type=MESH,
            )
            for side, device in ((0, west_id), (1, east_id))
        ]
        for copy in copies:
            copy.start()
    for band in range(4):
        for j in (1, 2):
            normed[band, j] = rms(cells(band, j), gain_attn_ref[...].reshape(1, width))
    loads[0].wait()

    def project(band, _):
        rows = normed[band].reshape(256, width)
        for part in range(3):
            lanes = slice(width * part, width * part + width)
            result = jnp.dot(rows, qkv_w[:, lanes], preferred_element_type=F32)
            if part == 0:
                result = result.astype(BF) * BF(0.125)
            qkv[band, :, :, lanes] = result.astype(BF).reshape(4, 64, width)
        return 0

    lax.fori_loop(0, 4, project, 0)
    if comm:
        for copy in copies:
            copy.wait_recv()

    def project_beside(side, _):
        rows = edge_recv[side].reshape(256, width)
        for part in range(2):
            lanes = slice(width * part, width * part + width)
            result = jnp.dot(rows, qkv_w[:, width * (part + 1) : width * (part + 2)], preferred_element_type=F32)
            beside[side, :, :, lanes] = result.astype(BF).reshape(4, 64, width)
        return 0

    lax.fori_loop(0, 2, project_beside, 0)
    even = lax.broadcasted_iota(jnp.int32, (128, 128), 1) < 64
    zero = jnp.zeros((128, 128), BF)
    tally = jnp.concatenate([jnp.where(even, 1.0, 0.0), jnp.where(even, 0.0, 1.0)], axis=0).astype(BF)

    def paired(block):
        return jnp.concatenate([jnp.where(even, block, zero), jnp.where(even, zero, block)], axis=0)

    def attention(band):
        for pair in range(6):
            q_lanes = slice(128 * pair, 128 * pair + 128)
            k_lanes = slice(width + 128 * pair, width + 128 * pair + 128)
            v_lanes = slice(2 * width + 128 * pair, 2 * width + 128 * pair + 128)
            hk_lanes, hv_lanes = q_lanes, k_lanes

            def window(keys, vals, query):
                keys = paired(keys)
                vals = jnp.concatenate([paired(vals), tally], axis=1)
                scores = lax.dot_general(query, keys, NT, preferred_element_type=F32)
                parts = [scores[:, :128], scores[:, 128:]]
                parts = [jnp.exp(s - jnp.max(s, axis=1, keepdims=True)).astype(BF) for s in parts]
                result = jnp.dot(jnp.concatenate(parts, axis=1), vals, preferred_element_type=F32)
                return (result[:, :128] / result[:, 128:]).astype(BF)

            def stack(*blocks):
                return jnp.concatenate(blocks, axis=0)

            mixed[0:64, q_lanes] = window(
                stack(beside[0, band, :, hk_lanes], qkv[band, 0, :, k_lanes]),
                stack(beside[0, band, :, hv_lanes], qkv[band, 0, :, v_lanes]),
                qkv[band, 0, :, q_lanes],
            )
            mixed[64:192, q_lanes] = window(
                stack(qkv[band, 1, :, k_lanes], qkv[band, 2, :, k_lanes]),
                stack(qkv[band, 1, :, v_lanes], qkv[band, 2, :, v_lanes]),
                stack(qkv[band, 1, :, q_lanes], qkv[band, 2, :, q_lanes]),
            )
            mixed[192:256, q_lanes] = window(
                stack(qkv[band, 3, :, k_lanes], beside[1, band, :, hk_lanes]),
                stack(qkv[band, 3, :, v_lanes], beside[1, band, :, hv_lanes]),
                qkv[band, 3, :, q_lanes],
            )

    def feed_forward(band):
        first = jnp.concatenate([cells(band, j) for j in range(4)], axis=0)
        first = first + jnp.dot(mixed[...], out_w[...], preferred_element_type=F32)
        rows = rms(first, gain_mlp_ref[...].reshape(1, width))
        total = first
        for part in range(4):
            lanes = slice(width * part, width * part + width)
            hidden = gelu(jnp.dot(rows, up_w[:, lanes], preferred_element_type=F32)).astype(BF)
            total = total + jnp.dot(hidden, down_w[lanes, :], preferred_element_type=F32)
        second_ref[band] = total
        flux_ref[band] = lax.dot_general(head_ref[...], total.astype(BF), NT, preferred_element_type=F32).astype(BF)

    attention(0)
    for load in loads[1:]:
        load.wait()

    def step(band, _):
        feed_forward(band - 1)
        attention(band)
        return 0

    lax.fori_loop(1, 4, step, 0)
    feed_forward(3)
    if comm:
        for copy in copies:
            copy.wait_send()


def atmosphere(comm, x, gain_attn, gain_mlp, qkv_w, out_w, up_w, down_w, flux_head):
    width = x.shape[-1]
    vm = pl.BlockSpec(memory_space=pltpu.VMEM)
    far = pl.BlockSpec(memory_space=pl.ANY)
    params = dict(collective_id=2, has_side_effects=True) if comm else {}
    return pl.pallas_call(
        functools.partial(air_kernel, comm),
        out_shape=[jax.ShapeDtypeStruct((4, 256, width), F32), jax.ShapeDtypeStruct((4, 8, 256), BF)],
        in_specs=[vm, vm, vm, far, far, far, far, vm],
        out_specs=[vm, vm],
        scratch_shapes=[
            pltpu.VMEM(qkv_w.shape, BF), pltpu.VMEM(out_w.shape, BF), pltpu.VMEM(up_w.shape, BF), pltpu.VMEM(down_w.shape, BF),
            pltpu.VMEM((4, 4, 64, width), BF),
            pltpu.VMEM((2, 4, 64, width), BF), pltpu.VMEM((2, 4, 64, width), BF),
            pltpu.VMEM((4, 4, 64, 3 * width), BF),
            pltpu.VMEM((2, 4, 64, 2 * width), BF),
            pltpu.VMEM((256, width), BF),
            pltpu.SemaphoreType.DMA((4,)), pltpu.SemaphoreType.DMA((2,)), pltpu.SemaphoreType.DMA((2,)),
        ],
        compiler_params=pltpu.CompilerParams(vmem_limit_bytes=56 * 2**20, **params),
        name="air",
        cost_estimate=pl.CostEstimate(flops=16 * 10**9, bytes_accessed=20 * 2**20, transcendentals=5 * 10**6),
    )(x.reshape(4, 8, 32, width), gain_attn, gain_mlp, qkv_w, out_w, up_w, down_w, jnp.swapaxes(flux_head, 0, 1))


def body(
    atmos_features,
    ocean_features,
    wet_cell_mask,
    overlay_cell_index,
    remap_weight,
    query_key_value_weight,
    attention_out_weight,
    feedforward_up_weight,
    feedforward_down_weight,
    attention_gain,
    feedforward_gain,
    flux_head_weight,
    surface_temp_embedding,
    forcing_lift_weight,
    depthwise_kernels,
    ocean_norm_gains,
    ocean_up_weights,
    ocean_down_weights,
    surface_temp_head,
):
    second, fluxes = atmosphere(
        True, atmos_features, attention_gain, feedforward_gain, query_key_value_weight, attention_out_weight,
        feedforward_up_weight, feedforward_down_weight, flux_head_weight,
    )
    updated, ocean_out = ocean_step(
        True, fluxes, overlay_cell_index, remap_weight, forcing_lift_weight, ocean_features, wet_cell_mask, depthwise_kernels,
        ocean_norm_gains, ocean_up_weights, jnp.swapaxes(ocean_down_weights, 1, 2), surface_temp_head, second,
        surface_temp_embedding,
    )
    return (updated, ocean_out)


def solution(mesh):
    cells = P("lat", "lon", None)
    in_specs = (cells, cells, P("lat", "lon"), P(None, "lat", "lon"), P(None, "lat", "lon")) + (P(),) * 14
    return jax.shard_map(body, mesh=mesh, in_specs=in_specs, out_specs=(cells, cells), check_vma=False)
```

```python
import functools

import jax
import jax.numpy as jnp
from jax import lax
from jax.experimental import pallas as pl
from jax.experimental.pallas import tpu as pltpu
from jax.sharding import PartitionSpec as P

BF = jnp.bfloat16
F32 = jnp.float32
EPS = 1e-6
MESH = pl.DeviceIdType.MESH
CH = 4

CELLS = 512
def split(x):
    hi=x.astype(BF)
    return hi,(x-hi.astype(F32)).astype(BF)

def split_dot(x, ones):
    hi,lo=split(x)
    return jnp.dot(hi,ones,preferred_element_type=F32)+jnp.dot(lo,ones,preferred_element_type=F32)

def gelu(x):
    inner=x*(0.7978845608028654+0.035677408136300125*(x*x))
    h=0.5*x
    return h+h*jnp.tanh(inner)

NT = (((1,),(1,)),((),()))


def ocean_kernel(comm, table_ref, index_ref, remap_ref, lift_ref, ocean_ref, wet_ref, taps_ref, gains_ref, up_ref, down_ref, head_ref, second_hbm, embed_ref,
                 updated_ref, out_ref, field_ref, next_ref, second_ref, t_ref, wet_t, taps_pair, w_ref, x4_ref, a_ref, y_ref, n_ref, warm_ref,
                 rows_send, rows_recv, side_send, side_recv, corner_send, corner_recv, load_sem, send_sem, recv_sem):
    load = pltpu.make_async_copy(second_hbm, second_ref, load_sem)
    load.start()
    if comm:
        lat = lax.axis_index("lat")
        lon = lax.axis_index("lon")
        lats = lax.axis_size("lat")
        lons = lax.axis_size("lon")
        top = lat == lats - 1
        bottom = lat == 0
        mirror = lons - 1 - lon
        up_id = (jnp.where(top, lat, lat + 1), jnp.where(top, mirror, lon))
        down_id = (jnp.where(bottom, lat, lat - 1), jnp.where(bottom, mirror, lon))
        west_id = (lat, lax.rem(lon + lons - 1, lons))
        east_id = (lat, lax.rem(lon + 1, lons))
        barrier = pltpu.get_barrier_semaphore()

        for other in (up_id, down_id, west_id, east_id):
            pl.semaphore_signal(barrier, inc=1, device_id=other, device_id_type=MESH)
        up_slot = jnp.where(top, 0, 1)
        down_slot = jnp.where(bottom, 1, 0)

    wet = wet_ref[...].astype(F32)
    wet_t[...] = jnp.concatenate([wet, wet], axis=0).T

    def wet_from(row):
        return pltpu.roll(wet_t[...], 128 - row, axis=1)

    for blk in range(2):
        for g in range(3):
            piece = taps_ref[blk][:, 64 * g : 64 * g + 64]
            taps_pair[blk, g, 0:49] = jnp.concatenate([piece, piece], axis=1)
    sub = lax.broadcasted_iota(jnp.int32, (64, 128), 0)
    lane = lax.broadcasted_iota(jnp.int32, (64, 128), 1)
    low_diag = lane == sub
    high_diag = lane == sub + 64
    s2 = lax.broadcasted_iota(jnp.int32, (256, 256), 0) // 64
    l2 = lax.broadcasted_iota(jnp.int32, (256, 256), 1) // 64
    ones = jnp.where(s2 == l2, 1.0, 0.0).astype(BF)
    flip = lax.broadcasted_iota(jnp.int32, (64, 64), 0) + lax.broadcasted_iota(jnp.int32, (64, 64), 1)
    flip = jnp.where(flip == 63, 1.0, 0.0).astype(BF)

    def build_weights(blk):
        def build(b, _):
            for g in range(3):
                for d in range(3):
                    for q in range(4):
                        halves = []
                        for half in range(2):
                            a = 4 * (d - 1) + q - 2 * half + 3
                            value = jnp.zeros((64, 128), F32)
                            if 0 <= a - 1 < 7:
                                value = jnp.where(high_diag, taps_pair[blk, g, pl.ds(7 * (a - 1) + b, 1), :], value)
                            if 0 <= a < 7:
                                value = jnp.where(low_diag, taps_pair[blk, g, pl.ds(7 * a + b, 1), :], value)
                            halves.append(value.astype(BF))
                        row = pl.multiple_of(b * 256, 256) + (1792 * d + 64 * q)
                        w_ref[g, pl.ds(pl.multiple_of(row, 64), 64), :] = jnp.concatenate(halves, axis=1)
            return 0

        lax.fori_loop(0, 7, build, 0)

    for h in range(4):
        t_ref[128 * h : 128 * h + 128, :] = table_ref[:, h].astype(F32).reshape(128, 256).astype(BF)
    ids = lax.broadcasted_iota(jnp.int32, (256, CELLS), 0)
    lift_hi, lift_lo = split(lift_ref[...])
    lift = jnp.concatenate([lift_hi, lift_hi, lift_lo], axis=0)

    def line(rows):
        return jnp.concatenate([rows[j : j + 1] for j in range(8)], axis=1)

    def force(i, _):
        total = jnp.zeros((8, CELLS), F32)
        for e in range(4):
            index = line(index_ref[e, pl.ds(pl.multiple_of(8 * i, 8), 8), :])
            lo = (index & 24) << 3 | ((index >> 9) & 7) << 3 | (index & 7)
            hi = jnp.broadcast_to((index >> 12) << 4 | ((index >> 5) & 15), (8, CELLS))
            hit = jnp.where(ids == lo, 1.0, 0.0).astype(BF)
            res = jnp.dot(t_ref[...], hit, preferred_element_type=F32)
            got = res[0:8]
            for k in range(1, 64):
                got = jnp.where(hi == k, res[8 * k : 8 * k + 8], got)
            total = total + got * line(remap_ref[e, pl.ds(pl.multiple_of(8 * i, 8), 8), :])
        high = total.astype(BF).astype(F32)
        spread = jnp.concatenate([high, total - high, high], axis=0).astype(BF)
        lifted = lax.dot_general(spread, lift, (((0,), (0,)), ((), ())), preferred_element_type=F32)
        here = wet_from(8 * i)
        for j in range(8):
            row = ocean_ref[8 * i + j].astype(F32) + lifted[64 * j : 64 * j + 64]
            field_ref[8 * i + j] = here[:, j : j + 1] * row
        return 0

    def remote(blk, source, target, index, slot, device):
        return pltpu.make_async_remote_copy(
            src_ref=source, dst_ref=target, send_sem=send_sem.at[blk, index], recv_sem=recv_sem.at[blk, slot],
            device_id=device, device_id_type=MESH,
        )

    def down_copy(blk):
        return remote(blk, rows_send.at[blk, 1], rows_recv.at[blk, down_slot], 1, down_slot, down_id)

    def up_copy(blk):
        return remote(blk, rows_send.at[blk, 0], rows_recv.at[blk, up_slot], 0, up_slot, up_id)

    def corner_copies(blk):
        return [
            remote(blk, corner_send.at[blk, 0], corner_recv.at[blk, 1], 2, 3, west_id),
            remote(blk, corner_send.at[blk, 1], corner_recv.at[blk, 0], 3, 2, east_id),
        ]

    def side_copies(blk, ci):
        part = pl.ds(8 * ci, 8)
        return [
            remote(blk, side_send.at[blk, 0, part], side_recv.at[blk, 1, part], 4 + ci, 8 + ci, west_id),
            remote(blk, side_send.at[blk, 1, part], side_recv.at[blk, 0, part], 8 + ci, 4 + ci, east_id),
        ]

    def ship(blk, src, ci):
        early = lax.broadcasted_iota(jnp.int32, (8, 8, 192), 1) < 4
        west = src[pl.ds(16 * ci, 16), 0:8, :].reshape(8, 2, 8, 192)
        east = src[pl.ds(16 * ci, 16), 56:64, :].reshape(8, 2, 8, 192)
        part = pl.ds(8 * ci, 8)
        side_send[blk, 0, part] = jnp.where(early, west[:, 0], pltpu.roll(west[:, 1], 4, axis=1)).astype(BF)
        side_send[blk, 1, part] = jnp.where(early, pltpu.roll(east[:, 0], 4, axis=1), east[:, 1]).astype(BF)
        for c in side_copies(blk, ci):
            c.start()

    def ship_down(blk, src):
        for k in range(3):
            rows_send[blk, 1, k] = src[k].astype(BF)
        down_copy(blk).start()

    def ship_up(blk, src):
        for k in range(3):
            turned = jnp.dot(flip, src[63 - k].astype(BF), preferred_element_type=F32)
            rows_send[blk, 0, k] = jnp.where(top, turned, src[61 + k]).astype(BF)
        up_copy(blk).start()

    if comm:
        pl.semaphore_wait(barrier, 4)

    def force_part(ci, _):
        force(2 * ci, 0)
        force(2 * ci + 1, 0)
        if comm:
            ship(0, field_ref, ci)

            @pl.when(ci == 0)
            def _():
                ship_down(0, field_ref)

        return 0

    lax.fori_loop(0, 4, force_part, 0)
    if comm:
        ship_up(0, field_ref)

    for blk in range(2):
        src = field_ref if blk == 0 else next_ref

        build_weights(blk)
        if comm:
            remote(blk, rows_send.at[blk, 0], rows_recv.at[blk, 0], 0, 0, up_id).wait_recv()
            remote(blk, rows_send.at[blk, 0], rows_recv.at[blk, 1], 0, 1, up_id).wait_recv()
            for s in range(2):
                corner_send[blk, 0, s] = rows_recv[blk, s, :, 0:8, :]
                corner_send[blk, 1, s] = rows_recv[blk, s, :, 56:64, :]
            for c in corner_copies(blk):
                c.start()
            for ci in range(4):
                for c in side_copies(blk, ci):
                    c.wait_recv()

        def place(i, rows):
            for g in range(3):
                x4_ref[g] = jnp.concatenate([r[:, 64 * g : 64 * g + 64] for r in rows], axis=1)
                for b in range(7):
                    a_ref[g, i, :, 256 * b : 256 * b + 256] = x4_ref[g, pl.ds(5 + b, 64), :].astype(BF)

        def group(i, _):
            rows = []
            for p in range(4):
                r = 4 * (i - 1) + p
                west = side_recv[blk, 0, 2 * (i - 1) + p // 2].astype(F32)
                east = side_recv[blk, 1, 2 * (i - 1) + p // 2].astype(F32)
                if p % 2 == 0:
                    west = pltpu.roll(west, 4, axis=0)
                else:
                    east = pltpu.roll(east, 4, axis=0)
                rows.append(jnp.concatenate([west, src[r], east], axis=0))
            place(i, rows)
            return 0

        lax.fori_loop(1, 17, group, 0)
        if comm:
            for c in corner_copies(blk):
                c.wait_recv()
        empty = jnp.zeros((80, 192), F32)

        def outer(s, k):
            pieces = [corner_recv[blk, 0, s, k], rows_recv[blk, s, k], corner_recv[blk, 1, s, k]]
            return jnp.concatenate([piece.astype(F32) for piece in pieces], axis=0)

        place(17, [outer(0, k) for k in range(3)] + [empty])
        souths = [outer(1, k) for k in range(3)]
        if comm:
            souths = [jnp.where(bottom, 0.0, s) for s in souths]
        place(0, [empty] + souths)

        def conv(ci):
            base = ci * CH
            for g in range(3):
                acc = None
                for d in range(3):
                    lhs = a_ref[g, pl.ds(base + d, CH)].reshape(CH * 64, 1792)
                    part = jnp.dot(lhs, w_ref[g, d * 1792 : (d + 1) * 1792, :], preferred_element_type=F32)
                    acc = part if acc is None else acc + part
                y_ref[g] = acc

        gains = [jnp.concatenate([gains_ref[blk : blk + 1, 64 * g : 64 * g + 64]] * 4, axis=1) for g in range(3)]

        def norm():
            mean = split_dot(y_ref[0] + y_ref[1] + y_ref[2], ones) * (1 / 192)
            cs = [y_ref[g] - mean for g in range(3)]
            var = split_dot(cs[0] * cs[0] + cs[1] * cs[1] + cs[2] * cs[2], ones) * (1 / 192)
            inv = lax.rsqrt(var + EPS)
            ns = [(cs[g] * inv * gains[g]).astype(BF) for g in range(3)]
            for p in range(4):
                n_ref[p] = jnp.concatenate([ns[g][:, 64 * p : 64 * p + 64] for g in range(3)], axis=1)

        def mlp(ci):
            base = ci * CH
            here = wet_from(16 * ci)
            temps = []
            for p in range(4):
                act = gelu(jnp.dot(n_ref[p], up_ref[blk], preferred_element_type=F32)).astype(BF)
                inc = lax.dot_general(act, down_ref[blk], NT, preferred_element_type=F32)
                news = []
                for j in range(CH):
                    r = 4 * (base + j) + p
                    new = src[r] + here[:, 4 * j + p : 4 * j + p + 1] * inc[64 * j : 64 * j + 64]
                    if blk == 1:
                        out_ref[r] = new.astype(BF)
                        news.append(new)
                    else:
                        next_ref[r] = new
                if blk == 1:
                    hi, lo = split(jnp.concatenate(news, axis=0))
                    head_hi, head_lo = split(jnp.broadcast_to(head_ref[...].reshape(1, 192), (128, 192)))
                    temps.append(
                        lax.dot_general(hi, head_hi, NT, preferred_element_type=F32)
                        + lax.dot_general(lo, head_hi, NT, preferred_element_type=F32)
                        + lax.dot_general(hi, head_lo, NT, preferred_element_type=F32)
                    )
            if blk == 1:
                for s in range(2):
                    warm_ref[0] = temps[2 * s] + temps[2 * s + 1]
                    for j in range(CH):
                        both = here[:, 4 * j + 2 * s : 4 * j + 2 * s + 1] + here[:, 4 * j + 2 * s + 1 : 4 * j + 2 * s + 2]
                        warm_ref[1, 64 * j : 64 * j + 64] = jnp.broadcast_to(both, (64, 128))
                    pair = lambda k: warm_ref[k, pl.ds(0, 128, stride=2), :] + warm_ref[k, pl.ds(1, 128, stride=2), :]
                    warmth = pair(0) / jnp.maximum(pair(1), 1.0)
                    for j in range(CH):
                        r = 2 * j + s
                        old = jnp.concatenate([second_ref[ci, 64 * c + 8 * r : 64 * c + 8 * r + 8, :] for c in range(4)], axis=0)
                        row = jnp.concatenate([warmth[32 * j : 32 * j + 32]] * 6, axis=1)
                        updated_ref[8 * ci + r] = (old + row * embed_ref[...].reshape(1, 768)).astype(BF)

        conv(0)
        if blk == 1:
            load.wait()

        def step(ci, _):
            norm()
            conv(ci)
            mlp(ci - 1)
            if comm and blk == 0:
                ship(1, next_ref, ci - 1)

                @pl.when(ci == 1)
                def _():
                    ship_down(1, next_ref)

            return 0

        lax.fori_loop(1, 16 // CH, step, 0)
        norm()
        mlp(16 // CH - 1)
        if comm and blk == 0:
            ship(1, next_ref, 16 // CH - 1)
            ship_up(1, next_ref)
    if comm:
        for blk in range(2):
            for c in [up_copy(blk), down_copy(blk), *corner_copies(blk)]:
                c.wait_send()
            for ci in range(4):
                for c in side_copies(blk, ci):
                    c.wait_send()


def ocean_step(comm, table, idx, remap, lift, ocean, wet, taps, gains, up, down, head, second, embed):
    vm = pl.BlockSpec(memory_space=pltpu.VMEM)
    far = pl.BlockSpec(memory_space=pl.ANY)
    width = second.shape[-1]
    dma = pltpu.SemaphoreType.DMA
    params = dict(collective_id=1, has_side_effects=True) if comm else {}
    return pl.pallas_call(
        functools.partial(ocean_kernel, comm),
        out_shape=[jax.ShapeDtypeStruct((32, 32, width), BF), jax.ShapeDtypeStruct((64, 64, 192), BF)],
        in_specs=[vm] * 11 + [far, vm],
        out_specs=[vm] * 2,
        scratch_shapes=[
            pltpu.VMEM((64, 64, 192), F32), pltpu.VMEM((64, 64, 192), F32), pltpu.VMEM((4, 256, width), F32),
            pltpu.VMEM((512, 256), BF), pltpu.VMEM((64, 128), F32), pltpu.VMEM((2, 3, 56, 128), F32),
            pltpu.VMEM((3, 21 * 256, 256), BF), pltpu.VMEM((3, 80, 256), F32), pltpu.VMEM((3, 18, 64, 1792), BF),
            pltpu.VMEM((3, CH * 64, 256), F32), pltpu.VMEM((4, CH * 64, 192), BF), pltpu.VMEM((2, CH * 64, 128), F32),
            pltpu.VMEM((2, 2, 3, 64, 192), BF), pltpu.VMEM((2, 2, 3, 64, 192), BF),
            pltpu.VMEM((2, 2, 32, 8, 192), BF), pltpu.VMEM((2, 2, 32, 8, 192), BF),
            pltpu.VMEM((2, 2, 2, 3, 8, 192), BF), pltpu.VMEM((2, 2, 2, 3, 8, 192), BF),
            dma, dma((2, 12)), dma((2, 12)),
        ],
        compiler_params=pltpu.CompilerParams(vmem_limit_bytes=60 * 2**20, **params),
        name="ocean",
        cost_estimate=pl.CostEstimate(flops=50 * 10**9, bytes_accessed=16 * 2**20, transcendentals=6 * 10**6),
    )(table, idx, remap, lift, ocean, wet, taps, gains, up, down, head, second, embed)


def air_kernel(comm, x_ref, gain_attn_ref, gain_mlp_ref, qkv_hbm, out_hbm, up_hbm, down_hbm, head_ref, second_ref, table_ref,
               qkv_w, out_w, up_w, down_w, normed, edge_send, edge_recv, qkv, beside, mixed, flux_ref, load_sem, send_sem, recv_sem, flux_send, flux_recv):
    width = x_ref.shape[-1]
    loads = [
        pltpu.make_async_copy(source, target, load_sem.at[i])
        for i, (source, target) in enumerate(((qkv_hbm, qkv_w), (out_hbm, out_w), (up_hbm, up_w), (down_hbm, down_w)))
    ]
    for load in loads:
        load.start()
    if comm:
        lat = lax.axis_index("lat")
        lon = lax.axis_index("lon")
        count = lax.axis_size("lon")
        west_id = (lat, lax.rem(lon + count - 1, count))
        east_id = (lat, lax.rem(lon + 1, count))
        barrier = pltpu.get_barrier_semaphore()

        def greet(k, _):
            pl.semaphore_signal(barrier, inc=1, device_id=(lat, lax.rem(lon + k, count)), device_id_type=MESH)
            return 0

        lax.fori_loop(1, count, greet, 0)

        def flux_copy(part, k):
            bands = (slice(0, 3), slice(3, 4))[part]
            return pltpu.make_async_remote_copy(
                src_ref=flux_ref.at[bands], dst_ref=table_ref.at[lon, bands], send_sem=flux_send.at[part, k],
                recv_sem=flux_recv.at[part, lon], device_id=(lat, lax.rem(lon + k, count)), device_id_type=MESH,
            )

        def flux_arrival(part, k):
            bands = (slice(0, 3), slice(3, 4))[part]
            peer = lax.rem(lon + k, count)
            return pltpu.make_async_remote_copy(
                src_ref=flux_ref.at[bands], dst_ref=table_ref.at[peer, bands], send_sem=flux_send.at[part, k],
                recv_sem=flux_recv.at[part, peer], device_id=(lat, peer), device_id_type=MESH,
            )

        def over_peers(part, act):
            def one(k, _):
                act(part, k)
                return 0

            lax.fori_loop(1, count, one, 0)

    def cells(band, j):
        return x_ref[band, :, 8 * j : 8 * j + 8, :].astype(F32).reshape(64, width)

    def rms(values, gain):
        return (values * lax.rsqrt(jnp.mean(values * values, axis=1, keepdims=True) + EPS) * gain).astype(BF)

    for band in range(4):
        for side, j in ((0, 0), (1, 3)):
            block = rms(cells(band, j), gain_attn_ref[...].reshape(1, width))
            normed[band, j] = block
            edge_send[side, band] = block
    if comm:
        pl.semaphore_wait(barrier, count - 1)
        copies = [
            pltpu.make_async_remote_copy(
                src_ref=edge_send.at[side], dst_ref=edge_recv.at[1 - side], send_sem=send_sem.at[side],
                recv_sem=recv_sem.at[1 - side], device_id=device, device_id_type=MESH,
            )
            for side, device in ((0, west_id), (1, east_id))
        ]
        for copy in copies:
            copy.start()
    for band in range(4):
        for j in (1, 2):
            normed[band, j] = rms(cells(band, j), gain_attn_ref[...].reshape(1, width))
    loads[0].wait()

    def project(band, _):
        rows = normed[band].reshape(256, width)
        for part in range(3):
            lanes = slice(width * part, width * part + width)
            result = jnp.dot(rows, qkv_w[:, lanes], preferred_element_type=F32)
            if part == 0:
                result = result.astype(BF) * BF(0.125)
            qkv[band, :, :, lanes] = result.astype(BF).reshape(4, 64, width)
        return 0

    lax.fori_loop(0, 4, project, 0)
    if comm:
        for copy in copies:
            copy.wait_recv()

    def project_beside(side, _):
        rows = edge_recv[side].reshape(256, width)
        for part in range(2):
            lanes = slice(width * part, width * part + width)
            result = jnp.dot(rows, qkv_w[:, width * (part + 1) : width * (part + 2)], preferred_element_type=F32)
            beside[side, :, :, lanes] = result.astype(BF).reshape(4, 64, width)
        return 0

    lax.fori_loop(0, 2, project_beside, 0)
    even = lax.broadcasted_iota(jnp.int32, (128, 128), 1) < 64
    zero = jnp.zeros((128, 128), BF)
    tally = jnp.concatenate([jnp.where(even, 1.0, 0.0), jnp.where(even, 0.0, 1.0)], axis=0).astype(BF)

    def paired(block):
        return jnp.concatenate([jnp.where(even, block, zero), jnp.where(even, zero, block)], axis=0)

    def attention(band):
        for pair in range(6):
            q_lanes = slice(128 * pair, 128 * pair + 128)
            k_lanes = slice(width + 128 * pair, width + 128 * pair + 128)
            v_lanes = slice(2 * width + 128 * pair, 2 * width + 128 * pair + 128)
            hk_lanes, hv_lanes = q_lanes, k_lanes

            def window(keys, vals, query):
                keys = paired(keys)
                vals = jnp.concatenate([paired(vals), tally], axis=1)
                scores = lax.dot_general(query, keys, NT, preferred_element_type=F32)
                parts = [scores[:, :128], scores[:, 128:]]
                parts = [jnp.exp(s - jnp.max(s, axis=1, keepdims=True)).astype(BF) for s in parts]
                result = jnp.dot(jnp.concatenate(parts, axis=1), vals, preferred_element_type=F32)
                return (result[:, :128] / result[:, 128:]).astype(BF)

            def stack(*blocks):
                return jnp.concatenate(blocks, axis=0)

            mixed[0:64, q_lanes] = window(
                stack(beside[0, band, :, hk_lanes], qkv[band, 0, :, k_lanes]),
                stack(beside[0, band, :, hv_lanes], qkv[band, 0, :, v_lanes]),
                qkv[band, 0, :, q_lanes],
            )
            mixed[64:192, q_lanes] = window(
                stack(qkv[band, 1, :, k_lanes], qkv[band, 2, :, k_lanes]),
                stack(qkv[band, 1, :, v_lanes], qkv[band, 2, :, v_lanes]),
                stack(qkv[band, 1, :, q_lanes], qkv[band, 2, :, q_lanes]),
            )
            mixed[192:256, q_lanes] = window(
                stack(qkv[band, 3, :, k_lanes], beside[1, band, :, hk_lanes]),
                stack(qkv[band, 3, :, v_lanes], beside[1, band, :, hv_lanes]),
                qkv[band, 3, :, q_lanes],
            )

    def feed_forward(band):
        first = jnp.concatenate([cells(band, j) for j in range(4)], axis=0)
        first = first + jnp.dot(mixed[...], out_w[...], preferred_element_type=F32)
        rows = rms(first, gain_mlp_ref[...].reshape(1, width))
        total = first
        for part in range(4):
            lanes = slice(width * part, width * part + width)
            hidden = gelu(jnp.dot(rows, up_w[:, lanes], preferred_element_type=F32)).astype(BF)
            total = total + jnp.dot(hidden, down_w[lanes, :], preferred_element_type=F32)
        second_ref[band] = total
        flux_ref[band] = lax.dot_general(head_ref[...], total.astype(BF), NT, preferred_element_type=F32).astype(BF)

    attention(0)
    for load in loads[1:]:
        load.wait()

    def step(band, _):
        feed_forward(band - 1)
        attention(band)
        return 0

    lax.fori_loop(1, 4, step, 0)
    if comm:
        over_peers(0, lambda part, k: flux_copy(part, k).start())
    feed_forward(3)
    if comm:
        over_peers(1, lambda part, k: flux_copy(part, k).start())
        table_ref[lon] = flux_ref[...]
        for copy in copies:
            copy.wait_send()
        for part in range(2):
            over_peers(part, lambda part, k: flux_arrival(part, k).wait_recv())
            over_peers(part, lambda part, k: flux_copy(part, k).wait_send())
    else:
        table_ref[0] = flux_ref[...]


def atmosphere(comm, x, gain_attn, gain_mlp, qkv_w, out_w, up_w, down_w, flux_head):
    width = x.shape[-1]
    vm = pl.BlockSpec(memory_space=pltpu.VMEM)
    far = pl.BlockSpec(memory_space=pl.ANY)
    params = dict(collective_id=2, has_side_effects=True) if comm else {}
    return pl.pallas_call(
        functools.partial(air_kernel, comm),
        out_shape=[jax.ShapeDtypeStruct((4, 256, width), F32), jax.ShapeDtypeStruct((16, 4, 8, 256), BF)],
        in_specs=[vm, vm, vm, far, far, far, far, vm],
        out_specs=[vm, vm],
        scratch_shapes=[
            pltpu.VMEM(qkv_w.shape, BF), pltpu.VMEM(out_w.shape, BF), pltpu.VMEM(up_w.shape, BF), pltpu.VMEM(down_w.shape, BF),
            pltpu.VMEM((4, 4, 64, width), BF),
            pltpu.VMEM((2, 4, 64, width), BF), pltpu.VMEM((2, 4, 64, width), BF),
            pltpu.VMEM((4, 4, 64, 3 * width), BF),
            pltpu.VMEM((2, 4, 64, 2 * width), BF),
            pltpu.VMEM((256, width), BF), pltpu.VMEM((4, 8, 256), BF),
            pltpu.SemaphoreType.DMA((4,)), pltpu.SemaphoreType.DMA((2,)), pltpu.SemaphoreType.DMA((2,)),
            pltpu.SemaphoreType.DMA((2, 16)), pltpu.SemaphoreType.DMA((2, 16)),
        ],
        compiler_params=pltpu.CompilerParams(vmem_limit_bytes=56 * 2**20, **params),
        name="air",
        cost_estimate=pl.CostEstimate(flops=16 * 10**9, bytes_accessed=20 * 2**20, transcendentals=5 * 10**6),
    )(x.reshape(4, 8, 32, width), gain_attn, gain_mlp, qkv_w, out_w, up_w, down_w, jnp.swapaxes(flux_head, 0, 1))


def body(
    atmos_features,
    ocean_features,
    wet_cell_mask,
    overlay_cell_index,
    remap_weight,
    query_key_value_weight,
    attention_out_weight,
    feedforward_up_weight,
    feedforward_down_weight,
    attention_gain,
    feedforward_gain,
    flux_head_weight,
    surface_temp_embedding,
    forcing_lift_weight,
    depthwise_kernels,
    ocean_norm_gains,
    ocean_up_weights,
    ocean_down_weights,
    surface_temp_head,
):
    second, table = atmosphere(
        True, atmos_features, attention_gain, feedforward_gain, query_key_value_weight, attention_out_weight,
        feedforward_up_weight, feedforward_down_weight, flux_head_weight,
    )
    updated, ocean_out = ocean_step(
        True, table, overlay_cell_index, remap_weight, forcing_lift_weight, ocean_features, wet_cell_mask, depthwise_kernels,
        ocean_norm_gains, ocean_up_weights, jnp.swapaxes(ocean_down_weights, 1, 2), surface_temp_head, second,
        surface_temp_embedding,
    )
    return (updated, ocean_out)


def solution(mesh):
    cells = P("lat", "lon", None)
    in_specs = (cells, cells, P("lat", "lon"), P(None, "lat", "lon"), P(None, "lat", "lon")) + (P(),) * 14
    return jax.shard_map(body, mesh=mesh, in_specs=in_specs, out_specs=(cells, cells), check_vma=False)
```

```python
import functools

import jax
import jax.numpy as jnp
from jax import lax
from jax.experimental import pallas as pl
from jax.experimental.pallas import tpu as pltpu
from jax.sharding import PartitionSpec as P

BF = jnp.bfloat16
F32 = jnp.float32
EPS = 1e-6
MESH = pl.DeviceIdType.MESH
CH = 4

CELLS = 512
def split(x):
    hi=x.astype(BF)
    return hi,(x-hi.astype(F32)).astype(BF)

def split_dot(x, ones):
    hi,lo=split(x)
    return jnp.dot(hi,ones,preferred_element_type=F32)+jnp.dot(lo,ones,preferred_element_type=F32)

def gelu(x):
    inner=x*(0.7978845608028654+0.035677408136300125*(x*x))
    h=0.5*x
    return h+h*jnp.tanh(inner)

NT = (((1,),(1,)),((),()))


def ocean_kernel(comm, table_ref, index_ref, remap_ref, lift_ref, ocean_ref, wet_ref, taps_ref, gains_ref, up_ref, down_ref, head_ref, second_hbm, embed_ref,
                 updated_ref, out_ref, field_ref, next_ref, second_ref, t_ref, wet_t, taps_pair, w_ref, x4_ref, a_ref, y_ref, n_ref, warm_ref,
                 rows_send, rows_recv, side_send, side_recv, corner_send, corner_recv, load_sem, send_sem, recv_sem):
    load = pltpu.make_async_copy(second_hbm, second_ref, load_sem)
    load.start()
    if comm:
        lat = lax.axis_index("lat")
        lon = lax.axis_index("lon")
        lats = lax.axis_size("lat")
        lons = lax.axis_size("lon")
        top = lat == lats - 1
        bottom = lat == 0
        mirror = lons - 1 - lon
        up_id = (jnp.where(top, lat, lat + 1), jnp.where(top, mirror, lon))
        down_id = (jnp.where(bottom, lat, lat - 1), jnp.where(bottom, mirror, lon))
        west_id = (lat, lax.rem(lon + lons - 1, lons))
        east_id = (lat, lax.rem(lon + 1, lons))
        barrier = pltpu.get_barrier_semaphore()

        for other in (up_id, down_id, west_id, east_id):
            pl.semaphore_signal(barrier, inc=1, device_id=other, device_id_type=MESH)
        up_slot = jnp.where(top, 0, 1)
        down_slot = jnp.where(bottom, 1, 0)

    wet = wet_ref[...].astype(F32)
    wet_t[...] = jnp.concatenate([wet, wet], axis=0).T

    def wet_from(row):
        return pltpu.roll(wet_t[...], 128 - row, axis=1)

    for blk in range(2):
        for g in range(3):
            piece = taps_ref[:, blk, 64 * g : 64 * g + 64]
            taps_pair[blk, g, 0:49] = jnp.concatenate([piece, piece], axis=1)
    sub = lax.broadcasted_iota(jnp.int32, (64, 128), 0)
    lane = lax.broadcasted_iota(jnp.int32, (64, 128), 1)
    low_diag = lane == sub
    high_diag = lane == sub + 64
    s2 = lax.broadcasted_iota(jnp.int32, (256, 256), 0) // 64
    l2 = lax.broadcasted_iota(jnp.int32, (256, 256), 1) // 64
    ones = jnp.where(s2 == l2, 1.0, 0.0).astype(BF)
    flip = lax.broadcasted_iota(jnp.int32, (64, 64), 0) + lax.broadcasted_iota(jnp.int32, (64, 64), 1)
    flip = jnp.where(flip == 63, 1.0, 0.0).astype(BF)

    def build_weights(blk):
        def build(b, _):
            for g in range(3):
                for d in range(3):
                    for q in range(4):
                        halves = []
                        for half in range(2):
                            a = 4 * (d - 1) + q - 2 * half + 3
                            value = jnp.zeros((64, 128), F32)
                            if 0 <= a - 1 < 7:
                                value = jnp.where(high_diag, taps_pair[blk, g, pl.ds(7 * (a - 1) + b, 1), :], value)
                            if 0 <= a < 7:
                                value = jnp.where(low_diag, taps_pair[blk, g, pl.ds(7 * a + b, 1), :], value)
                            halves.append(value.astype(BF))
                        row = pl.multiple_of(b * 256, 256) + (1792 * d + 64 * q)
                        w_ref[g, pl.ds(pl.multiple_of(row, 64), 64), :] = jnp.concatenate(halves, axis=1)
            return 0

        lax.fori_loop(0, 7, build, 0)

    for h in range(4):
        t_ref[128 * h : 128 * h + 128, :] = table_ref[:, h].astype(F32).reshape(128, 256).astype(BF)
    ids = lax.broadcasted_iota(jnp.int32, (256, CELLS), 0)
    lift_hi, lift_lo = split(lift_ref[...])
    lift = jnp.concatenate([lift_hi, lift_hi, lift_lo], axis=0)

    def line(rows):
        return jnp.concatenate([rows[j : j + 1] for j in range(8)], axis=1)

    def force(i, _):
        total = jnp.zeros((8, CELLS), F32)
        for e in range(4):
            index = line(index_ref[e, pl.ds(pl.multiple_of(8 * i, 8), 8), :])
            lo = (index & 24) << 3 | ((index >> 9) & 7) << 3 | (index & 7)
            hi = jnp.broadcast_to((index >> 12) << 4 | ((index >> 5) & 15), (8, CELLS))
            hit = jnp.where(ids == lo, 1.0, 0.0).astype(BF)
            res = jnp.dot(t_ref[...], hit, preferred_element_type=F32)
            got = res[0:8]
            for k in range(1, 64):
                got = jnp.where(hi == k, res[8 * k : 8 * k + 8], got)
            total = total + got * line(remap_ref[e, pl.ds(pl.multiple_of(8 * i, 8), 8), :])
        high = total.astype(BF).astype(F32)
        spread = jnp.concatenate([high, total - high, high], axis=0).astype(BF)
        lifted = lax.dot_general(spread, lift, (((0,), (0,)), ((), ())), preferred_element_type=F32)
        here = wet_from(8 * i)
        for j in range(8):
            row = ocean_ref[8 * i + j].astype(F32) + lifted[64 * j : 64 * j + 64]
            field_ref[8 * i + j] = here[:, j : j + 1] * row
        return 0

    def remote(blk, source, target, index, slot, device):
        return pltpu.make_async_remote_copy(
            src_ref=source, dst_ref=target, send_sem=send_sem.at[blk, index], recv_sem=recv_sem.at[blk, slot],
            device_id=device, device_id_type=MESH,
        )

    def down_copy(blk):
        return remote(blk, rows_send.at[blk, 1], rows_recv.at[blk, down_slot], 1, down_slot, down_id)

    def up_copy(blk):
        return remote(blk, rows_send.at[blk, 0], rows_recv.at[blk, up_slot], 0, up_slot, up_id)

    def corner_copies(blk):
        return [
            remote(blk, corner_send.at[blk, 0], corner_recv.at[blk, 1], 2, 3, west_id),
            remote(blk, corner_send.at[blk, 1], corner_recv.at[blk, 0], 3, 2, east_id),
        ]

    def side_copies(blk, ci):
        part = pl.ds(8 * ci, 8)
        return [
            remote(blk, side_send.at[blk, 0, part], side_recv.at[blk, 1, part], 4 + ci, 8 + ci, west_id),
            remote(blk, side_send.at[blk, 1, part], side_recv.at[blk, 0, part], 8 + ci, 4 + ci, east_id),
        ]

    def ship(blk, src, ci):
        early = lax.broadcasted_iota(jnp.int32, (8, 8, 192), 1) < 4
        west = src[pl.ds(16 * ci, 16), 0:8, :].reshape(8, 2, 8, 192)
        east = src[pl.ds(16 * ci, 16), 56:64, :].reshape(8, 2, 8, 192)
        part = pl.ds(8 * ci, 8)
        side_send[blk, 0, part] = jnp.where(early, west[:, 0], pltpu.roll(west[:, 1], 4, axis=1)).astype(BF)
        side_send[blk, 1, part] = jnp.where(early, pltpu.roll(east[:, 0], 4, axis=1), east[:, 1]).astype(BF)
        for c in side_copies(blk, ci):
            c.start()

    def ship_down(blk, src):
        for k in range(3):
            rows_send[blk, 1, k] = src[k].astype(BF)
        down_copy(blk).start()

    def ship_up(blk, src):
        for k in range(3):
            turned = jnp.dot(flip, src[63 - k].astype(BF), preferred_element_type=F32)
            rows_send[blk, 0, k] = jnp.where(top, turned, src[61 + k]).astype(BF)
        up_copy(blk).start()

    if comm:
        pl.semaphore_wait(barrier, 4)

    def force_part(ci, _):
        force(2 * ci, 0)
        force(2 * ci + 1, 0)
        if comm:
            ship(0, field_ref, ci)

            @pl.when(ci == 0)
            def _():
                ship_down(0, field_ref)

        return 0

    lax.fori_loop(0, 4, force_part, 0)
    if comm:
        ship_up(0, field_ref)

    for blk in range(2):
        src = field_ref if blk == 0 else next_ref

        build_weights(blk)
        if comm:
            remote(blk, rows_send.at[blk, 0], rows_recv.at[blk, 0], 0, 0, up_id).wait_recv()
            remote(blk, rows_send.at[blk, 0], rows_recv.at[blk, 1], 0, 1, up_id).wait_recv()
            for s in range(2):
                corner_send[blk, 0, s] = rows_recv[blk, s, :, 0:8, :]
                corner_send[blk, 1, s] = rows_recv[blk, s, :, 56:64, :]
            for c in corner_copies(blk):
                c.start()
            for ci in range(4):
                for c in side_copies(blk, ci):
                    c.wait_recv()

        def place(i, rows):
            for g in range(3):
                x4_ref[g] = jnp.concatenate([r[:, 64 * g : 64 * g + 64] for r in rows], axis=1)
                for b in range(7):
                    a_ref[g, i, :, 256 * b : 256 * b + 256] = x4_ref[g, pl.ds(5 + b, 64), :].astype(BF)

        def group(i, _):
            rows = []
            for p in range(4):
                r = 4 * (i - 1) + p
                west = side_recv[blk, 0, 2 * (i - 1) + p // 2].astype(F32)
                east = side_recv[blk, 1, 2 * (i - 1) + p // 2].astype(F32)
                if p % 2 == 0:
                    west = pltpu.roll(west, 4, axis=0)
                else:
                    east = pltpu.roll(east, 4, axis=0)
                rows.append(jnp.concatenate([west, src[r], east], axis=0))
            place(i, rows)
            return 0

        lax.fori_loop(1, 17, group, 0)
        if comm:
            for c in corner_copies(blk):
                c.wait_recv()
        empty = jnp.zeros((80, 192), F32)

        def outer(s, k):
            pieces = [corner_recv[blk, 0, s, k], rows_recv[blk, s, k], corner_recv[blk, 1, s, k]]
            return jnp.concatenate([piece.astype(F32) for piece in pieces], axis=0)

        place(17, [outer(0, k) for k in range(3)] + [empty])
        souths = [outer(1, k) for k in range(3)]
        if comm:
            souths = [jnp.where(bottom, 0.0, s) for s in souths]
        place(0, [empty] + souths)

        def conv(ci):
            base = ci * CH
            for g in range(3):
                acc = None
                for d in range(3):
                    lhs = a_ref[g, pl.ds(base + d, CH)].reshape(CH * 64, 1792)
                    part = jnp.dot(lhs, w_ref[g, d * 1792 : (d + 1) * 1792, :], preferred_element_type=F32)
                    acc = part if acc is None else acc + part
                y_ref[g] = acc

        gains = [jnp.concatenate([gains_ref[blk : blk + 1, 64 * g : 64 * g + 64]] * 4, axis=1) for g in range(3)]

        def norm():
            mean = split_dot(y_ref[0] + y_ref[1] + y_ref[2], ones) * (1 / 192)
            cs = [y_ref[g] - mean for g in range(3)]
            var = split_dot(cs[0] * cs[0] + cs[1] * cs[1] + cs[2] * cs[2], ones) * (1 / 192)
            inv = lax.rsqrt(var + EPS)
            ns = [(cs[g] * inv * gains[g]).astype(BF) for g in range(3)]
            for p in range(4):
                n_ref[p] = jnp.concatenate([ns[g][:, 64 * p : 64 * p + 64] for g in range(3)], axis=1)

        def mlp(ci):
            base = ci * CH
            here = wet_from(16 * ci)
            temps = []
            for p in range(4):
                act = gelu(jnp.dot(n_ref[p], up_ref[blk], preferred_element_type=F32)).astype(BF)
                inc = lax.dot_general(act, down_ref[blk], NT, preferred_element_type=F32)
                news = []
                for j in range(CH):
                    r = 4 * (base + j) + p
                    new = src[r] + here[:, 4 * j + p : 4 * j + p + 1] * inc[64 * j : 64 * j + 64]
                    if blk == 1:
                        out_ref[r] = new.astype(BF)
                        news.append(new)
                    else:
                        next_ref[r] = new
                if blk == 1:
                    hi, lo = split(jnp.concatenate(news, axis=0))
                    head_hi, head_lo = split(jnp.broadcast_to(head_ref[...].reshape(1, 192), (128, 192)))
                    temps.append(
                        lax.dot_general(hi, head_hi, NT, preferred_element_type=F32)
                        + lax.dot_general(lo, head_hi, NT, preferred_element_type=F32)
                        + lax.dot_general(hi, head_lo, NT, preferred_element_type=F32)
                    )
            if blk == 1:
                for s in range(2):
                    warm_ref[0] = temps[2 * s] + temps[2 * s + 1]
                    for j in range(CH):
                        both = here[:, 4 * j + 2 * s : 4 * j + 2 * s + 1] + here[:, 4 * j + 2 * s + 1 : 4 * j + 2 * s + 2]
                        warm_ref[1, 64 * j : 64 * j + 64] = jnp.broadcast_to(both, (64, 128))
                    pair = lambda k: warm_ref[k, pl.ds(0, 128, stride=2), :] + warm_ref[k, pl.ds(1, 128, stride=2), :]
                    warmth = pair(0) / jnp.maximum(pair(1), 1.0)
                    for j in range(CH):
                        r = 2 * j + s
                        old = jnp.concatenate([second_ref[ci, 64 * c + 8 * r : 64 * c + 8 * r + 8, :] for c in range(4)], axis=0)
                        row = jnp.concatenate([warmth[32 * j : 32 * j + 32]] * 6, axis=1)
                        updated_ref[8 * ci + r] = (old + row * embed_ref[...].reshape(1, 768)).astype(BF)

        conv(0)
        if blk == 1:
            load.wait()

        def step(ci, _):
            norm()
            conv(ci)
            mlp(ci - 1)
            if comm and blk == 0:
                ship(1, next_ref, ci - 1)

                @pl.when(ci == 1)
                def _():
                    ship_down(1, next_ref)

            return 0

        lax.fori_loop(1, 16 // CH, step, 0)
        norm()
        mlp(16 // CH - 1)
        if comm and blk == 0:
            ship(1, next_ref, 16 // CH - 1)
            ship_up(1, next_ref)
    if comm:
        for blk in range(2):
            for c in [up_copy(blk), down_copy(blk), *corner_copies(blk)]:
                c.wait_send()
            for ci in range(4):
                for c in side_copies(blk, ci):
                    c.wait_send()


def ocean_step(comm, table, idx, remap, lift, ocean, wet, taps, gains, up, down, head, second, embed):
    vm = pl.BlockSpec(memory_space=pltpu.VMEM)
    far = pl.BlockSpec(memory_space=pl.ANY)
    width = second.shape[-1]
    dma = pltpu.SemaphoreType.DMA
    params = dict(collective_id=1, has_side_effects=True) if comm else {}
    return pl.pallas_call(
        functools.partial(ocean_kernel, comm),
        out_shape=[jax.ShapeDtypeStruct((32, 32, width), BF), jax.ShapeDtypeStruct((64, 64, 192), BF)],
        in_specs=[vm] * 11 + [far, vm],
        out_specs=[vm] * 2,
        scratch_shapes=[
            pltpu.VMEM((64, 64, 192), F32), pltpu.VMEM((64, 64, 192), F32), pltpu.VMEM((4, 256, width), F32),
            pltpu.VMEM((512, 256), BF), pltpu.VMEM((64, 128), F32), pltpu.VMEM((2, 3, 56, 128), F32),
            pltpu.VMEM((3, 21 * 256, 256), BF), pltpu.VMEM((3, 80, 256), F32), pltpu.VMEM((3, 18, 64, 1792), BF),
            pltpu.VMEM((3, CH * 64, 256), F32), pltpu.VMEM((4, CH * 64, 192), BF), pltpu.VMEM((2, CH * 64, 128), F32),
            pltpu.VMEM((2, 2, 3, 64, 192), BF), pltpu.VMEM((2, 2, 3, 64, 192), BF),
            pltpu.VMEM((2, 2, 32, 8, 192), BF), pltpu.VMEM((2, 2, 32, 8, 192), BF),
            pltpu.VMEM((2, 2, 2, 3, 8, 192), BF), pltpu.VMEM((2, 2, 2, 3, 8, 192), BF),
            dma, dma((2, 12)), dma((2, 12)),
        ],
        compiler_params=pltpu.CompilerParams(vmem_limit_bytes=60 * 2**20, **params),
        name="ocean",
        cost_estimate=pl.CostEstimate(flops=50 * 10**9, bytes_accessed=16 * 2**20, transcendentals=6 * 10**6),
    )(table, idx, remap, lift, ocean, wet, jnp.swapaxes(taps, 0, 1), gains, up, down, head, second, embed)


def air_kernel(comm, x_ref, gain_attn_ref, gain_mlp_ref, qkv_hbm, out_hbm, up_hbm, down_hbm, head_ref, second_ref, table_ref,
               qkv_w, out_w, up_w, down_w, normed, edge_send, edge_recv, qkv, beside, mixed, flux_ref, load_sem, send_sem, recv_sem, flux_send, flux_recv):
    width = x_ref.shape[-1]
    loads = [
        pltpu.make_async_copy(source, target, load_sem.at[i])
        for i, (source, target) in enumerate(((qkv_hbm, qkv_w), (out_hbm, out_w), (up_hbm, up_w), (down_hbm, down_w)))
    ]
    for load in loads:
        load.start()
    if comm:
        lat = lax.axis_index("lat")
        lon = lax.axis_index("lon")
        count = lax.axis_size("lon")
        west_id = (lat, lax.rem(lon + count - 1, count))
        east_id = (lat, lax.rem(lon + 1, count))
        barrier = pltpu.get_barrier_semaphore()

        def greet(k, _):
            pl.semaphore_signal(barrier, inc=1, device_id=(lat, lax.rem(lon + k, count)), device_id_type=MESH)
            return 0

        lax.fori_loop(1, count, greet, 0)

        def flux_copy(part, k):
            bands = (slice(0, 3), slice(3, 4))[part]
            return pltpu.make_async_remote_copy(
                src_ref=flux_ref.at[bands], dst_ref=table_ref.at[lon, bands], send_sem=flux_send.at[part, k],
                recv_sem=flux_recv.at[part, lon], device_id=(lat, lax.rem(lon + k, count)), device_id_type=MESH,
            )

        def flux_arrival(part, k):
            bands = (slice(0, 3), slice(3, 4))[part]
            peer = lax.rem(lon + k, count)
            return pltpu.make_async_remote_copy(
                src_ref=flux_ref.at[bands], dst_ref=table_ref.at[peer, bands], send_sem=flux_send.at[part, k],
                recv_sem=flux_recv.at[part, peer], device_id=(lat, peer), device_id_type=MESH,
            )

        def over_peers(part, act):
            def one(k, _):
                act(part, k)
                return 0

            lax.fori_loop(1, count, one, 0)

    def cells(band, j):
        return x_ref[band, :, 8 * j : 8 * j + 8, :].astype(F32).reshape(64, width)

    def rms(values, gain):
        return (values * lax.rsqrt(jnp.mean(values * values, axis=1, keepdims=True) + EPS) * gain).astype(BF)

    for band in range(4):
        for side, j in ((0, 0), (1, 3)):
            block = rms(cells(band, j), gain_attn_ref[...].reshape(1, width))
            normed[band, j] = block
            edge_send[side, band] = block
    if comm:
        pl.semaphore_wait(barrier, count - 1)
        copies = [
            pltpu.make_async_remote_copy(
                src_ref=edge_send.at[side], dst_ref=edge_recv.at[1 - side], send_sem=send_sem.at[side],
                recv_sem=recv_sem.at[1 - side], device_id=device, device_id_type=MESH,
            )
            for side, device in ((0, west_id), (1, east_id))
        ]
        for copy in copies:
            copy.start()
    for band in range(4):
        for j in (1, 2):
            normed[band, j] = rms(cells(band, j), gain_attn_ref[...].reshape(1, width))
    loads[0].wait()

    def project(band, _):
        rows = normed[band].reshape(256, width)
        for part in range(3):
            lanes = slice(width * part, width * part + width)
            result = jnp.dot(rows, qkv_w[:, lanes], preferred_element_type=F32)
            if part == 0:
                result = result.astype(BF) * BF(0.125)
            qkv[band, :, :, lanes] = result.astype(BF).reshape(4, 64, width)
        return 0

    lax.fori_loop(0, 4, project, 0)
    even = lax.broadcasted_iota(jnp.int32, (128, 128), 1) < 64
    zero = jnp.zeros((128, 128), BF)
    tally = jnp.concatenate([jnp.where(even, 1.0, 0.0), jnp.where(even, 0.0, 1.0)], axis=0).astype(BF)

    def paired(block):
        return jnp.concatenate([jnp.where(even, block, zero), jnp.where(even, zero, block)], axis=0)

    def window(keys, vals, query):
        keys = paired(stack(*keys))
        vals = jnp.concatenate([paired(stack(*vals)), tally], axis=1)
        scores = lax.dot_general(stack(*query), keys, NT, preferred_element_type=F32)
        parts = [scores[:, :128], scores[:, 128:]]
        parts = [jnp.exp(s - jnp.max(s, axis=1, keepdims=True)).astype(BF) for s in parts]
        result = jnp.dot(jnp.concatenate(parts, axis=1), vals, preferred_element_type=F32)
        return (result[:, :128] / result[:, 128:]).astype(BF)

    def stack(*blocks):
        return jnp.concatenate(blocks, axis=0)

    def pair_lanes(pair):
        return [slice(width * part + 128 * pair, width * part + 128 * pair + 128) for part in range(3)]

    def middle(band):
        for pair in range(6):
            q, k, v = pair_lanes(pair)
            mixed[band, 64:192, q] = window(
                [qkv[band, 1, :, k], qkv[band, 2, :, k]], [qkv[band, 1, :, v], qkv[band, 2, :, v]], [qkv[band, 1, :, q], qkv[band, 2, :, q]]
            )

    def edges(band):
        for pair in range(6):
            q, k, v = pair_lanes(pair)
            mixed[band, 0:64, q] = window(
                [beside[0, band, :, q], qkv[band, 0, :, k]], [beside[0, band, :, k], qkv[band, 0, :, v]], [qkv[band, 0, :, q]]
            )
            mixed[band, 192:256, q] = window(
                [qkv[band, 3, :, k], beside[1, band, :, q]], [qkv[band, 3, :, v], beside[1, band, :, k]], [qkv[band, 3, :, q]]
            )

    def feed_forward(band):
        first = jnp.concatenate([cells(band, j) for j in range(4)], axis=0)
        first = first + jnp.dot(mixed[band], out_w[...], preferred_element_type=F32)
        rows = rms(first, gain_mlp_ref[...].reshape(1, width))
        total = first
        for part in range(4):
            lanes = slice(width * part, width * part + width)
            hidden = gelu(jnp.dot(rows, up_w[:, lanes], preferred_element_type=F32)).astype(BF)
            total = total + jnp.dot(hidden, down_w[lanes, :], preferred_element_type=F32)
        second_ref[band] = total
        flux_ref[band] = lax.dot_general(head_ref[...], total.astype(BF), NT, preferred_element_type=F32).astype(BF)

    def middle_step(band, _):
        middle(band)
        return 0

    lax.fori_loop(0, 4, middle_step, 0)
    if comm:
        for copy in copies:
            copy.wait_recv()

    def project_beside(side, _):
        rows = edge_recv[side].reshape(256, width)
        for part in range(2):
            lanes = slice(width * part, width * part + width)
            result = jnp.dot(rows, qkv_w[:, width * (part + 1) : width * (part + 2)], preferred_element_type=F32)
            beside[side, :, :, lanes] = result.astype(BF).reshape(4, 64, width)
        return 0

    lax.fori_loop(0, 2, project_beside, 0)
    edges(0)
    for load in loads[1:]:
        load.wait()

    def step(band, _):
        feed_forward(band - 1)
        edges(band)
        return 0

    lax.fori_loop(1, 4, step, 0)
    if comm:
        over_peers(0, lambda part, k: flux_copy(part, k).start())
    feed_forward(3)
    if comm:
        over_peers(1, lambda part, k: flux_copy(part, k).start())
        table_ref[lon] = flux_ref[...]
        for copy in copies:
            copy.wait_send()
        for part in range(2):
            over_peers(part, lambda part, k: flux_arrival(part, k).wait_recv())
            over_peers(part, lambda part, k: flux_copy(part, k).wait_send())
    else:
        table_ref[0] = flux_ref[...]


def atmosphere(comm, x, gain_attn, gain_mlp, qkv_w, out_w, up_w, down_w, flux_head):
    width = x.shape[-1]
    vm = pl.BlockSpec(memory_space=pltpu.VMEM)
    far = pl.BlockSpec(memory_space=pl.ANY)
    params = dict(collective_id=2, has_side_effects=True) if comm else {}
    return pl.pallas_call(
        functools.partial(air_kernel, comm),
        out_shape=[jax.ShapeDtypeStruct((4, 256, width), F32), jax.ShapeDtypeStruct((16, 4, 8, 256), BF)],
        in_specs=[vm, vm, vm, far, far, far, far, vm],
        out_specs=[vm, vm],
        scratch_shapes=[
            pltpu.VMEM(qkv_w.shape, BF), pltpu.VMEM(out_w.shape, BF), pltpu.VMEM(up_w.shape, BF), pltpu.VMEM(down_w.shape, BF),
            pltpu.VMEM((4, 4, 64, width), BF),
            pltpu.VMEM((2, 4, 64, width), BF), pltpu.VMEM((2, 4, 64, width), BF),
            pltpu.VMEM((4, 4, 64, 3 * width), BF),
            pltpu.VMEM((2, 4, 64, 2 * width), BF),
            pltpu.VMEM((4, 256, width), BF), pltpu.VMEM((4, 8, 256), BF),
            pltpu.SemaphoreType.DMA((4,)), pltpu.SemaphoreType.DMA((2,)), pltpu.SemaphoreType.DMA((2,)),
            pltpu.SemaphoreType.DMA((2, 16)), pltpu.SemaphoreType.DMA((2, 16)),
        ],
        compiler_params=pltpu.CompilerParams(vmem_limit_bytes=56 * 2**20, **params),
        name="air",
        cost_estimate=pl.CostEstimate(flops=16 * 10**9, bytes_accessed=20 * 2**20, transcendentals=5 * 10**6),
    )(x.reshape(4, 8, 32, width), gain_attn, gain_mlp, qkv_w, out_w, up_w, down_w, jnp.swapaxes(flux_head, 0, 1))


def body(
    atmos_features,
    ocean_features,
    wet_cell_mask,
    overlay_cell_index,
    remap_weight,
    query_key_value_weight,
    attention_out_weight,
    feedforward_up_weight,
    feedforward_down_weight,
    attention_gain,
    feedforward_gain,
    flux_head_weight,
    surface_temp_embedding,
    forcing_lift_weight,
    depthwise_kernels,
    ocean_norm_gains,
    ocean_up_weights,
    ocean_down_weights,
    surface_temp_head,
):
    second, table = atmosphere(
        True, atmos_features, attention_gain, feedforward_gain, query_key_value_weight, attention_out_weight,
        feedforward_up_weight, feedforward_down_weight, flux_head_weight,
    )
    updated, ocean_out = ocean_step(
        True, table, overlay_cell_index, remap_weight, forcing_lift_weight, ocean_features, wet_cell_mask, depthwise_kernels,
        ocean_norm_gains, ocean_up_weights, jnp.swapaxes(ocean_down_weights, 1, 2), surface_temp_head, second,
        surface_temp_embedding,
    )
    return (updated, ocean_out)


def solution(mesh):
    cells = P("lat", "lon", None)
    in_specs = (cells, cells, P("lat", "lon"), P(None, "lat", "lon"), P(None, "lat", "lon")) + (P(),) * 14
    return jax.shard_map(body, mesh=mesh, in_specs=in_specs, out_specs=(cells, cells), check_vma=False)
```

```python
import functools

import jax
import jax.numpy as jnp
from jax import lax
from jax.experimental import pallas as pl
from jax.experimental.pallas import tpu as pltpu
from jax.sharding import PartitionSpec as P

BF = jnp.bfloat16
F32 = jnp.float32
EPS = 1e-6
MESH = pl.DeviceIdType.MESH
CH = 4

CELLS = 512
def split(x):
    hi=x.astype(BF)
    return hi,(x-hi.astype(F32)).astype(BF)

def split_dot(x, ones):
    hi,lo=split(x)
    return jnp.dot(hi,ones,preferred_element_type=F32)+jnp.dot(lo,ones,preferred_element_type=F32)

def gelu(x):
    inner=x*(0.7978845608028654+0.035677408136300125*(x*x))
    h=0.5*x
    return h+h*jnp.tanh(inner)

NT = (((1,),(1,)),((),()))


def ocean_kernel(comm, table_ref, index_ref, remap_ref, lift_ref, ocean_ref, wet_ref, taps_ref, gains_ref, up_ref, down_ref, head_ref, second_hbm, embed_ref,
                 updated_ref, out_ref, field_ref, next_ref, second_ref, t_ref, wet_t, taps_pair, w_ref, x4_ref, a_ref, y_ref, n_ref, warm_ref,
                 rows_send, rows_recv, side_send, side_recv, corner_send, corner_recv, load_sem, send_sem, recv_sem):
    load = pltpu.make_async_copy(second_hbm, second_ref, load_sem)
    load.start()
    if comm:
        lat = lax.axis_index("lat")
        lon = lax.axis_index("lon")
        lats = lax.axis_size("lat")
        lons = lax.axis_size("lon")
        top = lat == lats - 1
        bottom = lat == 0
        mirror = lons - 1 - lon
        up_id = (jnp.where(top, lat, lat + 1), jnp.where(top, mirror, lon))
        down_id = (jnp.where(bottom, lat, lat - 1), jnp.where(bottom, mirror, lon))
        west_id = (lat, lax.rem(lon + lons - 1, lons))
        east_id = (lat, lax.rem(lon + 1, lons))
        barrier = pltpu.get_barrier_semaphore()

        for other in (up_id, down_id, west_id, east_id):
            pl.semaphore_signal(barrier, inc=1, device_id=other, device_id_type=MESH)
        up_slot = jnp.where(top, 0, 1)
        down_slot = jnp.where(bottom, 1, 0)

    wet = wet_ref[...].astype(F32)
    wet_t[...] = jnp.concatenate([wet, wet], axis=0).T

    def wet_from(row):
        return pltpu.roll(wet_t[...], 128 - row, axis=1)

    for blk in range(2):
        for g in range(3):
            piece = taps_ref[:, blk, 64 * g : 64 * g + 64]
            taps_pair[blk, g, 0:49] = jnp.concatenate([piece, piece], axis=1)
    sub = lax.broadcasted_iota(jnp.int32, (64, 128), 0)
    lane = lax.broadcasted_iota(jnp.int32, (64, 128), 1)
    low_diag = lane == sub
    high_diag = lane == sub + 64
    s2 = lax.broadcasted_iota(jnp.int32, (256, 256), 0) // 64
    l2 = lax.broadcasted_iota(jnp.int32, (256, 256), 1) // 64
    ones = jnp.where(s2 == l2, 1.0, 0.0).astype(BF)
    flip = lax.broadcasted_iota(jnp.int32, (64, 64), 0) + lax.broadcasted_iota(jnp.int32, (64, 64), 1)
    flip = jnp.where(flip == 63, 1.0, 0.0).astype(BF)

    def build_weights(blk):
        def build(b, _):
            for g in range(3):
                for d in range(3):
                    for q in range(4):
                        halves = []
                        for half in range(2):
                            a = 4 * (d - 1) + q - 2 * half + 3
                            value = jnp.zeros((64, 128), F32)
                            if 0 <= a - 1 < 7:
                                value = jnp.where(high_diag, taps_pair[blk, g, pl.ds(7 * (a - 1) + b, 1), :], value)
                            if 0 <= a < 7:
                                value = jnp.where(low_diag, taps_pair[blk, g, pl.ds(7 * a + b, 1), :], value)
                            halves.append(value.astype(BF))
                        row = pl.multiple_of(b * 256, 256) + (1792 * d + 64 * q)
                        w_ref[g, pl.ds(pl.multiple_of(row, 64), 64), :] = jnp.concatenate(halves, axis=1)
            return 0

        lax.fori_loop(0, 7, build, 0)

    for h in range(4):
        t_ref[128 * h : 128 * h + 128, :] = table_ref[:, h].astype(F32).reshape(128, 256).astype(BF)
    ids = lax.broadcasted_iota(jnp.int32, (256, CELLS), 0)
    lift_hi, lift_lo = split(lift_ref[...])
    lift = jnp.concatenate([lift_hi, lift_hi, lift_lo], axis=0)

    def line(rows):
        return jnp.concatenate([rows[j : j + 1] for j in range(8)], axis=1)

    def force(i, _):
        total = jnp.zeros((8, CELLS), F32)
        for e in range(4):
            index = line(index_ref[e, pl.ds(pl.multiple_of(8 * i, 8), 8), :])
            lo = ((index >> 12) & 1) << 7 | ((index >> 4) & 1) << 6 | ((index >> 9) & 7) << 3 | (index & 7)
            edge = 1 - (((index >> 4) ^ (index >> 3)) & 1)
            hi = jnp.broadcast_to(edge << 5 | (index >> 13) << 4 | ((index >> 5) & 15), (8, CELLS))
            hit = jnp.where(ids == lo, 1.0, 0.0).astype(BF)
            res = jnp.dot(t_ref[...], hit, preferred_element_type=F32)
            got = res[0:8]
            for k in range(1, 64):
                got = jnp.where(hi == k, res[8 * k : 8 * k + 8], got)
            total = total + got * line(remap_ref[e, pl.ds(pl.multiple_of(8 * i, 8), 8), :])
        high = total.astype(BF).astype(F32)
        spread = jnp.concatenate([high, total - high, high], axis=0).astype(BF)
        lifted = lax.dot_general(spread, lift, (((0,), (0,)), ((), ())), preferred_element_type=F32)
        here = wet_from(8 * i)
        for j in range(8):
            row = ocean_ref[8 * i + j].astype(F32) + lifted[64 * j : 64 * j + 64]
            field_ref[8 * i + j] = here[:, j : j + 1] * row
        return 0

    def remote(blk, source, target, index, slot, device):
        return pltpu.make_async_remote_copy(
            src_ref=source, dst_ref=target, send_sem=send_sem.at[blk, index], recv_sem=recv_sem.at[blk, slot],
            device_id=device, device_id_type=MESH,
        )

    def down_copy(blk):
        return remote(blk, rows_send.at[blk, 1], rows_recv.at[blk, down_slot], 1, down_slot, down_id)

    def up_copy(blk):
        return remote(blk, rows_send.at[blk, 0], rows_recv.at[blk, up_slot], 0, up_slot, up_id)

    def corner_copies(blk):
        return [
            remote(blk, corner_send.at[blk, 0], corner_recv.at[blk, 1], 2, 3, west_id),
            remote(blk, corner_send.at[blk, 1], corner_recv.at[blk, 0], 3, 2, east_id),
        ]

    def side_copies(blk, ci):
        part = pl.ds(8 * ci, 8)
        return [
            remote(blk, side_send.at[blk, 0, part], side_recv.at[blk, 1, part], 4 + ci, 8 + ci, west_id),
            remote(blk, side_send.at[blk, 1, part], side_recv.at[blk, 0, part], 8 + ci, 4 + ci, east_id),
        ]

    def ship(blk, src, ci):
        early = lax.broadcasted_iota(jnp.int32, (8, 8, 192), 1) < 4
        west = src[pl.ds(16 * ci, 16), 0:8, :].reshape(8, 2, 8, 192)
        east = src[pl.ds(16 * ci, 16), 56:64, :].reshape(8, 2, 8, 192)
        part = pl.ds(8 * ci, 8)
        side_send[blk, 0, part] = jnp.where(early, west[:, 0], pltpu.roll(west[:, 1], 4, axis=1)).astype(BF)
        side_send[blk, 1, part] = jnp.where(early, pltpu.roll(east[:, 0], 4, axis=1), east[:, 1]).astype(BF)
        for c in side_copies(blk, ci):
            c.start()

    def ship_down(blk, src):
        for k in range(3):
            rows_send[blk, 1, k] = src[k].astype(BF)
        down_copy(blk).start()

    def ship_up(blk, src):
        for k in range(3):
            turned = jnp.dot(flip, src[63 - k].astype(BF), preferred_element_type=F32)
            rows_send[blk, 0, k] = jnp.where(top, turned, src[61 + k]).astype(BF)
        up_copy(blk).start()

    if comm:
        pl.semaphore_wait(barrier, 4)

    def force_part(ci, _):
        force(2 * ci, 0)
        force(2 * ci + 1, 0)
        if comm:
            ship(0, field_ref, ci)

            @pl.when(ci == 0)
            def _():
                ship_down(0, field_ref)

        return 0

    lax.fori_loop(0, 4, force_part, 0)
    if comm:
        ship_up(0, field_ref)

    for blk in range(2):
        src = field_ref if blk == 0 else next_ref

        build_weights(blk)
        if comm:
            remote(blk, rows_send.at[blk, 0], rows_recv.at[blk, 0], 0, 0, up_id).wait_recv()
            remote(blk, rows_send.at[blk, 0], rows_recv.at[blk, 1], 0, 1, up_id).wait_recv()
            for s in range(2):
                corner_send[blk, 0, s] = rows_recv[blk, s, :, 0:8, :]
                corner_send[blk, 1, s] = rows_recv[blk, s, :, 56:64, :]
            for c in corner_copies(blk):
                c.start()
            for ci in range(4):
                for c in side_copies(blk, ci):
                    c.wait_recv()

        def place(i, rows):
            for g in range(3):
                x4_ref[g] = jnp.concatenate([r[:, 64 * g : 64 * g + 64] for r in rows], axis=1)
                for b in range(7):
                    a_ref[g, i, :, 256 * b : 256 * b + 256] = x4_ref[g, pl.ds(5 + b, 64), :].astype(BF)

        def group(i, _):
            rows = []
            for p in range(4):
                r = 4 * (i - 1) + p
                west = side_recv[blk, 0, 2 * (i - 1) + p // 2].astype(F32)
                east = side_recv[blk, 1, 2 * (i - 1) + p // 2].astype(F32)
                if p % 2 == 0:
                    west = pltpu.roll(west, 4, axis=0)
                else:
                    east = pltpu.roll(east, 4, axis=0)
                rows.append(jnp.concatenate([west, src[r], east], axis=0))
            place(i, rows)
            return 0

        lax.fori_loop(1, 17, group, 0)
        if comm:
            for c in corner_copies(blk):
                c.wait_recv()
        empty = jnp.zeros((80, 192), F32)

        def outer(s, k):
            pieces = [corner_recv[blk, 0, s, k], rows_recv[blk, s, k], corner_recv[blk, 1, s, k]]
            return jnp.concatenate([piece.astype(F32) for piece in pieces], axis=0)

        place(17, [outer(0, k) for k in range(3)] + [empty])
        souths = [outer(1, k) for k in range(3)]
        if comm:
            souths = [jnp.where(bottom, 0.0, s) for s in souths]
        place(0, [empty] + souths)

        def conv(ci):
            base = ci * CH
            for g in range(3):
                acc = None
                for d in range(3):
                    lhs = a_ref[g, pl.ds(base + d, CH)].reshape(CH * 64, 1792)
                    part = jnp.dot(lhs, w_ref[g, d * 1792 : (d + 1) * 1792, :], preferred_element_type=F32)
                    acc = part if acc is None else acc + part
                y_ref[g] = acc

        gains = [jnp.concatenate([gains_ref[blk : blk + 1, 64 * g : 64 * g + 64]] * 4, axis=1) for g in range(3)]

        def norm():
            mean = split_dot(y_ref[0] + y_ref[1] + y_ref[2], ones) * (1 / 192)
            cs = [y_ref[g] - mean for g in range(3)]
            var = split_dot(cs[0] * cs[0] + cs[1] * cs[1] + cs[2] * cs[2], ones) * (1 / 192)
            inv = lax.rsqrt(var + EPS)
            ns = [(cs[g] * inv * gains[g]).astype(BF) for g in range(3)]
            for p in range(4):
                n_ref[p] = jnp.concatenate([ns[g][:, 64 * p : 64 * p + 64] for g in range(3)], axis=1)

        def mlp(ci):
            base = ci * CH
            here = wet_from(16 * ci)
            temps = []
            for p in range(4):
                act = gelu(jnp.dot(n_ref[p], up_ref[blk], preferred_element_type=F32)).astype(BF)
                inc = lax.dot_general(act, down_ref[blk], NT, preferred_element_type=F32)
                news = []
                for j in range(CH):
                    r = 4 * (base + j) + p
                    new = src[r] + here[:, 4 * j + p : 4 * j + p + 1] * inc[64 * j : 64 * j + 64]
                    if blk == 1:
                        out_ref[r] = new.astype(BF)
                        news.append(new)
                    else:
                        next_ref[r] = new
                if blk == 1:
                    hi, lo = split(jnp.concatenate(news, axis=0))
                    head_hi, head_lo = split(jnp.broadcast_to(head_ref[...].reshape(1, 192), (128, 192)))
                    temps.append(
                        lax.dot_general(hi, head_hi, NT, preferred_element_type=F32)
                        + lax.dot_general(lo, head_hi, NT, preferred_element_type=F32)
                        + lax.dot_general(hi, head_lo, NT, preferred_element_type=F32)
                    )
            if blk == 1:
                for s in range(2):
                    warm_ref[0] = temps[2 * s] + temps[2 * s + 1]
                    for j in range(CH):
                        both = here[:, 4 * j + 2 * s : 4 * j + 2 * s + 1] + here[:, 4 * j + 2 * s + 1 : 4 * j + 2 * s + 2]
                        warm_ref[1, 64 * j : 64 * j + 64] = jnp.broadcast_to(both, (64, 128))
                    pair = lambda k: warm_ref[k, pl.ds(0, 128, stride=2), :] + warm_ref[k, pl.ds(1, 128, stride=2), :]
                    warmth = pair(0) / jnp.maximum(pair(1), 1.0)
                    for j in range(CH):
                        r = 2 * j + s
                        start = [pl.multiple_of(128 * (ci % 2), 128) + 64 * (c // 2) + 8 * r for c in range(4)]
                        old = jnp.concatenate(
                            [second_ref[(2, 0, 0, 2)[c] + ci // 2, pl.ds(pl.multiple_of(start[c], 8), 8), :] for c in range(4)], axis=0
                        )
                        row = jnp.concatenate([warmth[32 * j : 32 * j + 32]] * 6, axis=1)
                        updated_ref[8 * ci + r] = (old + row * embed_ref[...].reshape(1, 768)).astype(BF)

        conv(0)
        if blk == 1:
            load.wait()

        def step(ci, _):
            norm()
            conv(ci)
            mlp(ci - 1)
            if comm and blk == 0:
                ship(1, next_ref, ci - 1)

                @pl.when(ci == 1)
                def _():
                    ship_down(1, next_ref)

            return 0

        lax.fori_loop(1, 16 // CH, step, 0)
        norm()
        mlp(16 // CH - 1)
        if comm and blk == 0:
            ship(1, next_ref, 16 // CH - 1)
            ship_up(1, next_ref)
    if comm:
        for blk in range(2):
            for c in [up_copy(blk), down_copy(blk), *corner_copies(blk)]:
                c.wait_send()
            for ci in range(4):
                for c in side_copies(blk, ci):
                    c.wait_send()


def ocean_step(comm, table, idx, remap, lift, ocean, wet, taps, gains, up, down, head, second, embed):
    vm = pl.BlockSpec(memory_space=pltpu.VMEM)
    far = pl.BlockSpec(memory_space=pl.ANY)
    width = second.shape[-1]
    dma = pltpu.SemaphoreType.DMA
    params = dict(collective_id=1, has_side_effects=True) if comm else {}
    return pl.pallas_call(
        functools.partial(ocean_kernel, comm),
        out_shape=[jax.ShapeDtypeStruct((32, 32, width), BF), jax.ShapeDtypeStruct((64, 64, 192), BF)],
        in_specs=[vm] * 11 + [far, vm],
        out_specs=[vm] * 2,
        scratch_shapes=[
            pltpu.VMEM((64, 64, 192), F32), pltpu.VMEM((64, 64, 192), F32), pltpu.VMEM((4, 256, width), F32),
            pltpu.VMEM((512, 256), BF), pltpu.VMEM((64, 128), F32), pltpu.VMEM((2, 3, 56, 128), F32),
            pltpu.VMEM((3, 21 * 256, 256), BF), pltpu.VMEM((3, 80, 256), F32), pltpu.VMEM((3, 18, 64, 1792), BF),
            pltpu.VMEM((3, CH * 64, 256), F32), pltpu.VMEM((4, CH * 64, 192), BF), pltpu.VMEM((2, CH * 64, 128), F32),
            pltpu.VMEM((2, 2, 3, 64, 192), BF), pltpu.VMEM((2, 2, 3, 64, 192), BF),
            pltpu.VMEM((2, 2, 32, 8, 192), BF), pltpu.VMEM((2, 2, 32, 8, 192), BF),
            pltpu.VMEM((2, 2, 2, 3, 8, 192), BF), pltpu.VMEM((2, 2, 2, 3, 8, 192), BF),
            dma, dma((2, 12)), dma((2, 12)),
        ],
        compiler_params=pltpu.CompilerParams(vmem_limit_bytes=60 * 2**20, **params),
        name="ocean",
        cost_estimate=pl.CostEstimate(flops=50 * 10**9, bytes_accessed=16 * 2**20, transcendentals=6 * 10**6),
    )(table, idx, remap, lift, ocean, wet, jnp.swapaxes(taps, 0, 1), gains, up, down, head, second, embed)


def air_kernel(comm, x_ref, gain_attn_ref, gain_mlp_ref, qkv_hbm, out_hbm, up_hbm, down_hbm, head_ref, second_ref, table_ref,
               qkv_w, out_w, up_w, down_w, normed, edge_send, edge_recv, qkv, beside, mixed, flux_ref, load_sem, send_sem, recv_sem, flux_send, flux_recv):
    width = x_ref.shape[-1]
    loads = [
        pltpu.make_async_copy(source, target, load_sem.at[i])
        for i, (source, target) in enumerate(((qkv_hbm, qkv_w), (out_hbm, out_w), (up_hbm, up_w), (down_hbm, down_w)))
    ]
    for load in loads:
        load.start()
    if comm:
        lat = lax.axis_index("lat")
        lon = lax.axis_index("lon")
        count = lax.axis_size("lon")
        west_id = (lat, lax.rem(lon + count - 1, count))
        east_id = (lat, lax.rem(lon + 1, count))
        barrier = pltpu.get_barrier_semaphore()

        def greet(k, _):
            pl.semaphore_signal(barrier, inc=1, device_id=(lat, lax.rem(lon + k, count)), device_id_type=MESH)
            return 0

        lax.fori_loop(1, count, greet, 0)

        def flux_copy(part, k):
            bands = (slice(0, 3), slice(3, 4))[part]
            return pltpu.make_async_remote_copy(
                src_ref=flux_ref.at[bands], dst_ref=table_ref.at[lon, bands], send_sem=flux_send.at[part, k],
                recv_sem=flux_recv.at[part, lon], device_id=(lat, lax.rem(lon + k, count)), device_id_type=MESH,
            )

        def flux_arrival(part, k):
            bands = (slice(0, 3), slice(3, 4))[part]
            peer = lax.rem(lon + k, count)
            return pltpu.make_async_remote_copy(
                src_ref=flux_ref.at[bands], dst_ref=table_ref.at[peer, bands], send_sem=flux_send.at[part, k],
                recv_sem=flux_recv.at[part, peer], device_id=(lat, peer), device_id_type=MESH,
            )

        def over_peers(part, act):
            def one(k, _):
                act(part, k)
                return 0

            lax.fori_loop(1, count, one, 0)

    def cells(band, j):
        return x_ref[band, :, 8 * j : 8 * j + 8, :].astype(F32).reshape(64, width)

    def rms(values, gain):
        return (values * lax.rsqrt(jnp.mean(values * values, axis=1, keepdims=True) + EPS) * gain).astype(BF)

    for band in range(4):
        for side, j in ((0, 0), (1, 3)):
            block = rms(cells(band, j), gain_attn_ref[...].reshape(1, width))
            normed[band, j] = block
            edge_send[side, band] = block
    if comm:
        pl.semaphore_wait(barrier, count - 1)
        copies = [
            pltpu.make_async_remote_copy(
                src_ref=edge_send.at[side], dst_ref=edge_recv.at[1 - side], send_sem=send_sem.at[side],
                recv_sem=recv_sem.at[1 - side], device_id=device, device_id_type=MESH,
            )
            for side, device in ((0, west_id), (1, east_id))
        ]
        for copy in copies:
            copy.start()
    for band in range(4):
        for j in (1, 2):
            normed[band, j] = rms(cells(band, j), gain_attn_ref[...].reshape(1, width))
    loads[0].wait()

    def project(band, _):
        rows = normed[band].reshape(256, width)
        for part in range(3):
            lanes = slice(width * part, width * part + width)
            result = jnp.dot(rows, qkv_w[:, lanes], preferred_element_type=F32)
            if part == 0:
                result = result.astype(BF) * BF(0.125)
            qkv[band, :, :, lanes] = result.astype(BF).reshape(4, 64, width)
        return 0

    lax.fori_loop(0, 4, project, 0)
    even = lax.broadcasted_iota(jnp.int32, (128, 128), 1) < 64
    zero = jnp.zeros((128, 128), BF)
    tally = jnp.concatenate([jnp.where(even, 1.0, 0.0), jnp.where(even, 0.0, 1.0)], axis=0).astype(BF)

    def paired(block):
        return jnp.concatenate([jnp.where(even, block, zero), jnp.where(even, zero, block)], axis=0)

    def window(keys, vals, query):
        keys = paired(stack(*keys))
        vals = jnp.concatenate([paired(stack(*vals)), tally], axis=1)
        scores = lax.dot_general(stack(*query), keys, NT, preferred_element_type=F32)
        parts = [scores[:, :128], scores[:, 128:]]
        parts = [jnp.exp(s - jnp.max(s, axis=1, keepdims=True)).astype(BF) for s in parts]
        result = jnp.dot(jnp.concatenate(parts, axis=1), vals, preferred_element_type=F32)
        return (result[:, :128] / result[:, 128:]).astype(BF)

    def stack(*blocks):
        return jnp.concatenate(blocks, axis=0)

    def pair_lanes(pair):
        return [slice(width * part + 128 * pair, width * part + 128 * pair + 128) for part in range(3)]

    def middle(band):
        for pair in range(6):
            q, k, v = pair_lanes(pair)
            mixed[0, band // 2, 128 * (band % 2) : 128 * (band % 2) + 128, q] = window(
                [qkv[band, 1, :, k], qkv[band, 2, :, k]], [qkv[band, 1, :, v], qkv[band, 2, :, v]], [qkv[band, 1, :, q], qkv[band, 2, :, q]]
            )

    def edges(band):
        base = 128 * (band % 2)
        for pair in range(6):
            q, k, v = pair_lanes(pair)
            mixed[1, band // 2, base : base + 64, q] = window(
                [beside[0, band, :, q], qkv[band, 0, :, k]], [beside[0, band, :, k], qkv[band, 0, :, v]], [qkv[band, 0, :, q]]
            )
            mixed[1, band // 2, base + 64 : base + 128, q] = window(
                [qkv[band, 3, :, k], beside[1, band, :, q]], [qkv[band, 3, :, v], beside[1, band, :, k]], [qkv[band, 3, :, q]]
            )

    def feed_forward(kind, pair):
        first = stack(*[cells(2 * pair + band, j) for band in range(2) for j in ((1, 2), (0, 3))[kind]])
        first = first + jnp.dot(mixed[kind, pair], out_w[...], preferred_element_type=F32)
        rows = rms(first, gain_mlp_ref[...].reshape(1, width))
        total = first
        for part in range(4):
            lanes = slice(width * part, width * part + width)
            hidden = gelu(jnp.dot(rows, up_w[:, lanes], preferred_element_type=F32)).astype(BF)
            total = total + jnp.dot(hidden, down_w[lanes, :], preferred_element_type=F32)
        second_ref[2 * kind + pair] = total
        flux_ref[2 * kind + pair] = lax.dot_general(head_ref[...], total.astype(BF), NT, preferred_element_type=F32).astype(BF)

    middle(0)
    middle(1)
    for load in loads[1:]:
        load.wait()
    feed_forward(0, 0)
    middle(2)
    middle(3)
    feed_forward(0, 1)
    if comm:
        for copy in copies:
            copy.wait_recv()

    def project_beside(side, _):
        rows = edge_recv[side].reshape(256, width)
        for part in range(2):
            lanes = slice(width * part, width * part + width)
            result = jnp.dot(rows, qkv_w[:, width * (part + 1) : width * (part + 2)], preferred_element_type=F32)
            beside[side, :, :, lanes] = result.astype(BF).reshape(4, 64, width)
        return 0

    lax.fori_loop(0, 2, project_beside, 0)
    edges(0)
    edges(1)
    feed_forward(1, 0)
    if comm:
        over_peers(0, lambda part, k: flux_copy(part, k).start())
    edges(2)
    edges(3)
    feed_forward(1, 1)
    if comm:
        over_peers(1, lambda part, k: flux_copy(part, k).start())
        table_ref[lon] = flux_ref[...]
        for copy in copies:
            copy.wait_send()
        for part in range(2):
            over_peers(part, lambda part, k: flux_arrival(part, k).wait_recv())
            over_peers(part, lambda part, k: flux_copy(part, k).wait_send())
    else:
        table_ref[0] = flux_ref[...]


def atmosphere(comm, x, gain_attn, gain_mlp, qkv_w, out_w, up_w, down_w, flux_head):
    width = x.shape[-1]
    vm = pl.BlockSpec(memory_space=pltpu.VMEM)
    far = pl.BlockSpec(memory_space=pl.ANY)
    params = dict(collective_id=2, has_side_effects=True) if comm else {}
    return pl.pallas_call(
        functools.partial(air_kernel, comm),
        out_shape=[jax.ShapeDtypeStruct((4, 256, width), F32), jax.ShapeDtypeStruct((16, 4, 8, 256), BF)],
        in_specs=[vm, vm, vm, far, far, far, far, vm],
        out_specs=[vm, vm],
        scratch_shapes=[
            pltpu.VMEM(qkv_w.shape, BF), pltpu.VMEM(out_w.shape, BF), pltpu.VMEM(up_w.shape, BF), pltpu.VMEM(down_w.shape, BF),
            pltpu.VMEM((4, 4, 64, width), BF),
            pltpu.VMEM((2, 4, 64, width), BF), pltpu.VMEM((2, 4, 64, width), BF),
            pltpu.VMEM((4, 4, 64, 3 * width), BF),
            pltpu.VMEM((2, 4, 64, 2 * width), BF),
            pltpu.VMEM((2, 2, 256, width), BF), pltpu.VMEM((4, 8, 256), BF),
            pltpu.SemaphoreType.DMA((4,)), pltpu.SemaphoreType.DMA((2,)), pltpu.SemaphoreType.DMA((2,)),
            pltpu.SemaphoreType.DMA((2, 16)), pltpu.SemaphoreType.DMA((2, 16)),
        ],
        compiler_params=pltpu.CompilerParams(vmem_limit_bytes=56 * 2**20, **params),
        name="air",
        cost_estimate=pl.CostEstimate(flops=16 * 10**9, bytes_accessed=20 * 2**20, transcendentals=5 * 10**6),
    )(x.reshape(4, 8, 32, width), gain_attn, gain_mlp, qkv_w, out_w, up_w, down_w, jnp.swapaxes(flux_head, 0, 1))


def body(
    atmos_features,
    ocean_features,
    wet_cell_mask,
    overlay_cell_index,
    remap_weight,
    query_key_value_weight,
    attention_out_weight,
    feedforward_up_weight,
    feedforward_down_weight,
    attention_gain,
    feedforward_gain,
    flux_head_weight,
    surface_temp_embedding,
    forcing_lift_weight,
    depthwise_kernels,
    ocean_norm_gains,
    ocean_up_weights,
    ocean_down_weights,
    surface_temp_head,
):
    second, table = atmosphere(
        True, atmos_features, attention_gain, feedforward_gain, query_key_value_weight, attention_out_weight,
        feedforward_up_weight, feedforward_down_weight, flux_head_weight,
    )
    updated, ocean_out = ocean_step(
        True, table, overlay_cell_index, remap_weight, forcing_lift_weight, ocean_features, wet_cell_mask, depthwise_kernels,
        ocean_norm_gains, ocean_up_weights, jnp.swapaxes(ocean_down_weights, 1, 2), surface_temp_head, second,
        surface_temp_embedding,
    )
    return (updated, ocean_out)


def solution(mesh):
    cells = P("lat", "lon", None)
    in_specs = (cells, cells, P("lat", "lon"), P(None, "lat", "lon"), P(None, "lat", "lon")) + (P(),) * 14
    return jax.shard_map(body, mesh=mesh, in_specs=in_specs, out_specs=(cells, cells), check_vma=False)
```

```python
import functools

import jax
import jax.numpy as jnp
from jax import lax
from jax.experimental import pallas as pl
from jax.experimental.pallas import tpu as pltpu
from jax.sharding import PartitionSpec as P

BF = jnp.bfloat16
F32 = jnp.float32
EPS = 1e-6
MESH = pl.DeviceIdType.MESH
CH = 4

CELLS = 512
def split(x):
    hi=x.astype(BF)
    return hi,(x-hi.astype(F32)).astype(BF)

def split_dot(x, ones):
    hi,lo=split(x)
    return jnp.dot(hi,ones,preferred_element_type=F32)+jnp.dot(lo,ones,preferred_element_type=F32)

def gelu(x):
    inner=x*(0.7978845608028654+0.035677408136300125*(x*x))
    h=0.5*x
    return h+h*jnp.tanh(inner)

NT = (((1,),(1,)),((),()))


def ocean_kernel(comm, table_ref, index_ref, remap_ref, lift_ref, ocean_ref, wet_ref, taps_ref, gains_ref, up_ref, down_ref, head_ref, second_hbm, embed_ref,
                 updated_ref, out_ref, field_ref, next_ref, second_ref, t_ref, wet_t, taps_pair, w_ref, x4_ref, a_ref, y_ref, n_ref, warm_ref,
                 rows_send, rows_recv, side_send, side_recv, corner_send, corner_recv, load_sem, send_sem, recv_sem):
    load = pltpu.make_async_copy(second_hbm, second_ref, load_sem)
    load.start()
    if comm:
        lat = lax.axis_index("lat")
        lon = lax.axis_index("lon")
        lats = lax.axis_size("lat")
        lons = lax.axis_size("lon")
        top = lat == lats - 1
        bottom = lat == 0
        mirror = lons - 1 - lon
        up_id = (jnp.where(top, lat, lat + 1), jnp.where(top, mirror, lon))
        down_id = (jnp.where(bottom, lat, lat - 1), jnp.where(bottom, mirror, lon))
        west_id = (lat, lax.rem(lon + lons - 1, lons))
        east_id = (lat, lax.rem(lon + 1, lons))
        barrier = pltpu.get_barrier_semaphore()

        for other in (up_id, down_id, west_id, east_id):
            pl.semaphore_signal(barrier, inc=1, device_id=other, device_id_type=MESH)
        up_slot = jnp.where(top, 0, 1)
        down_slot = jnp.where(bottom, 1, 0)

    wet = wet_ref[...].astype(F32)
    wet_t[...] = jnp.concatenate([wet, wet], axis=0).T

    def wet_from(row):
        return pltpu.roll(wet_t[...], 128 - row, axis=1)

    for blk in range(2):
        for g in range(3):
            piece = taps_ref[:, blk, 64 * g : 64 * g + 64]
            taps_pair[blk, g, 0:49] = jnp.concatenate([piece, piece], axis=1)
    sub = lax.broadcasted_iota(jnp.int32, (64, 128), 0)
    lane = lax.broadcasted_iota(jnp.int32, (64, 128), 1)
    low_diag = lane == sub
    high_diag = lane == sub + 64
    s2 = lax.broadcasted_iota(jnp.int32, (256, 256), 0) // 64
    l2 = lax.broadcasted_iota(jnp.int32, (256, 256), 1) // 64
    ones = jnp.where(s2 == l2, 1.0, 0.0).astype(BF)
    flip = lax.broadcasted_iota(jnp.int32, (64, 64), 0) + lax.broadcasted_iota(jnp.int32, (64, 64), 1)
    flip = jnp.where(flip == 63, 1.0, 0.0).astype(BF)

    def build_weights(blk):
        def build(b, _):
            for g in range(3):
                for d in range(3):
                    for q in range(4):
                        halves = []
                        for half in range(2):
                            a = 4 * (d - 1) + q - 2 * half + 3
                            value = jnp.zeros((64, 128), F32)
                            if 0 <= a - 1 < 7:
                                value = jnp.where(high_diag, taps_pair[blk, g, pl.ds(7 * (a - 1) + b, 1), :], value)
                            if 0 <= a < 7:
                                value = jnp.where(low_diag, taps_pair[blk, g, pl.ds(7 * a + b, 1), :], value)
                            halves.append(value.astype(BF))
                        row = pl.multiple_of(b * 256, 256) + (1792 * d + 64 * q)
                        w_ref[g, pl.ds(pl.multiple_of(row, 64), 64), :] = jnp.concatenate(halves, axis=1)
            return 0

        lax.fori_loop(0, 7, build, 0)

    for h in range(4):
        t_ref[128 * h : 128 * h + 128, :] = table_ref[:, h].astype(F32).reshape(128, 256).astype(BF)
    ids = lax.broadcasted_iota(jnp.int32, (256, CELLS), 0)
    lift_hi, lift_lo = split(lift_ref[...])
    lift = jnp.concatenate([lift_hi, lift_hi, lift_lo], axis=0)

    def line(rows):
        return jnp.concatenate([rows[j : j + 1] for j in range(8)], axis=1)

    def force(i, _):
        total = jnp.zeros((8, CELLS), F32)
        for e in range(4):
            index = line(index_ref[e, pl.ds(pl.multiple_of(8 * i, 8), 8), :])
            lo = ((index >> 12) & 1) << 7 | ((index >> 4) & 1) << 6 | ((index >> 9) & 7) << 3 | (index & 7)
            edge = 1 - (((index >> 4) ^ (index >> 3)) & 1)
            hi = jnp.broadcast_to(edge << 5 | (index >> 13) << 4 | ((index >> 5) & 15), (8, CELLS))
            hit = jnp.where(ids == lo, 1.0, 0.0).astype(BF)
            res = jnp.dot(t_ref[...], hit, preferred_element_type=F32)
            got = res[0:8]
            for k in range(1, 64):
                got = jnp.where(hi == k, res[8 * k : 8 * k + 8], got)
            total = total + got * line(remap_ref[e, pl.ds(pl.multiple_of(8 * i, 8), 8), :])
        high = total.astype(BF).astype(F32)
        spread = jnp.concatenate([high, total - high, high], axis=0).astype(BF)
        lifted = lax.dot_general(spread, lift, (((0,), (0,)), ((), ())), preferred_element_type=F32)
        here = wet_from(8 * i)
        for j in range(8):
            row = ocean_ref[8 * i + j].astype(F32) + lifted[64 * j : 64 * j + 64]
            field_ref[8 * i + j] = here[:, j : j + 1] * row
        return 0

    def remote(blk, source, target, index, slot, device):
        return pltpu.make_async_remote_copy(
            src_ref=source, dst_ref=target, send_sem=send_sem.at[blk, index], recv_sem=recv_sem.at[blk, slot],
            device_id=device, device_id_type=MESH,
        )

    def down_copy(blk):
        return remote(blk, rows_send.at[blk, 1], rows_recv.at[blk, down_slot], 1, down_slot, down_id)

    def up_copy(blk):
        return remote(blk, rows_send.at[blk, 0], rows_recv.at[blk, up_slot], 0, up_slot, up_id)

    def corner_copies(blk):
        return [
            remote(blk, corner_send.at[blk, 0], corner_recv.at[blk, 1], 2, 3, west_id),
            remote(blk, corner_send.at[blk, 1], corner_recv.at[blk, 0], 3, 2, east_id),
        ]

    def side_copies(blk, ci):
        part = pl.ds(8 * ci, 8)
        return [
            remote(blk, side_send.at[blk, 0, part], side_recv.at[blk, 1, part], 4 + ci, 8 + ci, west_id),
            remote(blk, side_send.at[blk, 1, part], side_recv.at[blk, 0, part], 8 + ci, 4 + ci, east_id),
        ]

    def ship(blk, src, ci):
        early = lax.broadcasted_iota(jnp.int32, (8, 8, 192), 1) < 4
        west = src[pl.ds(16 * ci, 16), 0:8, :].reshape(8, 2, 8, 192)
        east = src[pl.ds(16 * ci, 16), 56:64, :].reshape(8, 2, 8, 192)
        part = pl.ds(8 * ci, 8)
        side_send[blk, 0, part] = jnp.where(early, west[:, 0], pltpu.roll(west[:, 1], 4, axis=1)).astype(BF)
        side_send[blk, 1, part] = jnp.where(early, pltpu.roll(east[:, 0], 4, axis=1), east[:, 1]).astype(BF)
        for c in side_copies(blk, ci):
            c.start()

    def ship_down(blk, src):
        for k in range(3):
            rows_send[blk, 1, k] = src[k].astype(BF)
        down_copy(blk).start()

    def ship_up(blk, src):
        for k in range(3):
            turned = jnp.dot(flip, src[63 - k].astype(BF), preferred_element_type=F32)
            rows_send[blk, 0, k] = jnp.where(top, turned, src[61 + k]).astype(BF)
        up_copy(blk).start()

    if comm:
        pl.semaphore_wait(barrier, 4)

    def force_part(ci, _):
        force(2 * ci, 0)
        force(2 * ci + 1, 0)
        if comm:
            ship(0, field_ref, ci)

            @pl.when(ci == 0)
            def _():
                ship_down(0, field_ref)

        return 0

    lax.fori_loop(0, 4, force_part, 0)
    if comm:
        ship_up(0, field_ref)

    for blk in range(2):
        src = field_ref if blk == 0 else next_ref

        def spread_lanes(rows, g):
            return jnp.concatenate([r[:, 64 * g : 64 * g + 64] for r in rows], axis=1)

        def place(i, rows, first, last, slot=0):
            size = last - first
            for g in range(3):
                x4_ref[slot, g, 0 : size + 16] = spread_lanes(rows, g)
                for b in range(7):
                    a_ref[g, i, first:last, 256 * b : 256 * b + 256] = x4_ref[slot, g, pl.ds(5 + b, size), :].astype(BF)

        def inner(k, _):
            for slot in range(4):
                i = 4 * k + slot + 1
                place(i, [src[4 * (i - 1) + p][8:56] for p in range(4)], 16, 48, slot)
            return 0

        lax.fori_loop(0, 16 // 4, inner, 0)
        build_weights(blk)
        if comm:
            remote(blk, rows_send.at[blk, 0], rows_recv.at[blk, 0], 0, 0, up_id).wait_recv()
            remote(blk, rows_send.at[blk, 0], rows_recv.at[blk, 1], 0, 1, up_id).wait_recv()
            for s in range(2):
                corner_send[blk, 0, s] = rows_recv[blk, s, :, 0:8, :]
                corner_send[blk, 1, s] = rows_recv[blk, s, :, 56:64, :]
            for c in corner_copies(blk):
                c.start()
            for ci in range(4):
                for c in side_copies(blk, ci):
                    c.wait_recv()

        def outer_columns(i, slot):
            lefts = []
            rights = []
            for p in range(4):
                r = 4 * (i - 1) + p
                west = side_recv[blk, 0, 2 * (i - 1) + p // 2].astype(F32)
                east = side_recv[blk, 1, 2 * (i - 1) + p // 2].astype(F32)
                if p % 2 == 0:
                    west = pltpu.roll(west, 4, axis=0)
                else:
                    east = pltpu.roll(east, 4, axis=0)
                lefts.append(jnp.concatenate([west, src[r][0:24]], axis=0))
                rights.append(jnp.concatenate([src[r][40:64], east], axis=0))
            place(i, lefts, 0, 16, 2 * slot)
            place(i, rights, 48, 64, 2 * slot + 1)

        def outer_pair(k, _):
            for slot in range(4 // 2):
                outer_columns(4 // 2 * k + slot + 1, slot)
            return 0

        lax.fori_loop(0, 32 // 4, outer_pair, 0)
        if comm:
            for c in corner_copies(blk):
                c.wait_recv()
        empty = jnp.zeros((80, 192), F32)

        def outer(s, k):
            pieces = [corner_recv[blk, 0, s, k], rows_recv[blk, s, k], corner_recv[blk, 1, s, k]]
            return jnp.concatenate([piece.astype(F32) for piece in pieces], axis=0)

        place(17, [outer(0, k) for k in range(3)] + [empty], 0, 64)
        souths = [outer(1, k) for k in range(3)]
        if comm:
            souths = [jnp.where(bottom, 0.0, s) for s in souths]
        place(0, [empty] + souths, 0, 64)

        def conv(ci):
            base = ci * CH
            for g in range(3):
                acc = None
                for d in range(3):
                    lhs = a_ref[g, pl.ds(base + d, CH)].reshape(CH * 64, 1792)
                    part = jnp.dot(lhs, w_ref[g, d * 1792 : (d + 1) * 1792, :], preferred_element_type=F32)
                    acc = part if acc is None else acc + part
                y_ref[g] = acc

        gains = [jnp.concatenate([gains_ref[blk : blk + 1, 64 * g : 64 * g + 64]] * 4, axis=1) for g in range(3)]

        def norm():
            mean = split_dot(y_ref[0] + y_ref[1] + y_ref[2], ones) * (1 / 192)
            cs = [y_ref[g] - mean for g in range(3)]
            var = split_dot(cs[0] * cs[0] + cs[1] * cs[1] + cs[2] * cs[2], ones) * (1 / 192)
            inv = lax.rsqrt(var + EPS)
            ns = [(cs[g] * inv * gains[g]).astype(BF) for g in range(3)]
            for p in range(4):
                n_ref[p] = jnp.concatenate([ns[g][:, 64 * p : 64 * p + 64] for g in range(3)], axis=1)

        def mlp(ci):
            base = ci * CH
            here = wet_from(16 * ci)
            temps = []
            for p in range(4):
                act = gelu(jnp.dot(n_ref[p], up_ref[blk], preferred_element_type=F32)).astype(BF)
                inc = lax.dot_general(act, down_ref[blk], NT, preferred_element_type=F32)
                news = []
                for j in range(CH):
                    r = 4 * (base + j) + p
                    new = src[r] + here[:, 4 * j + p : 4 * j + p + 1] * inc[64 * j : 64 * j + 64]
                    if blk == 1:
                        out_ref[r] = new.astype(BF)
                        news.append(new)
                    else:
                        next_ref[r] = new
                if blk == 1:
                    hi, lo = split(jnp.concatenate(news, axis=0))
                    head_hi, head_lo = split(jnp.broadcast_to(head_ref[...].reshape(1, 192), (128, 192)))
                    temps.append(
                        lax.dot_general(hi, head_hi, NT, preferred_element_type=F32)
                        + lax.dot_general(lo, head_hi, NT, preferred_element_type=F32)
                        + lax.dot_general(hi, head_lo, NT, preferred_element_type=F32)
                    )
            if blk == 1:
                for s in range(2):
                    warm_ref[0] = temps[2 * s] + temps[2 * s + 1]
                    for j in range(CH):
                        both = here[:, 4 * j + 2 * s : 4 * j + 2 * s + 1] + here[:, 4 * j + 2 * s + 1 : 4 * j + 2 * s + 2]
                        warm_ref[1, 64 * j : 64 * j + 64] = jnp.broadcast_to(both, (64, 128))
                    pair = lambda k: warm_ref[k, pl.ds(0, 128, stride=2), :] + warm_ref[k, pl.ds(1, 128, stride=2), :]
                    warmth = pair(0) / jnp.maximum(pair(1), 1.0)
                    for j in range(CH):
                        r = 2 * j + s
                        start = [pl.multiple_of(128 * (ci % 2), 128) + 64 * (c // 2) + 8 * r for c in range(4)]
                        old = jnp.concatenate(
                            [second_ref[(2, 0, 0, 2)[c] + ci // 2, pl.ds(pl.multiple_of(start[c], 8), 8), :] for c in range(4)], axis=0
                        )
                        row = jnp.concatenate([warmth[32 * j : 32 * j + 32]] * 6, axis=1)
                        updated_ref[8 * ci + r] = (old + row * embed_ref[...].reshape(1, 768)).astype(BF)

        conv(0)
        if blk == 1:
            load.wait()

        def step(ci, _):
            norm()
            conv(ci)
            mlp(ci - 1)
            if comm and blk == 0:
                ship(1, next_ref, ci - 1)

                @pl.when(ci == 1)
                def _():
                    ship_down(1, next_ref)

            return 0

        lax.fori_loop(1, 16 // CH, step, 0)
        norm()
        mlp(16 // CH - 1)
        if comm and blk == 0:
            ship(1, next_ref, 16 // CH - 1)
            ship_up(1, next_ref)
    if comm:
        for blk in range(2):
            for c in [up_copy(blk), down_copy(blk), *corner_copies(blk)]:
                c.wait_send()
            for ci in range(4):
                for c in side_copies(blk, ci):
                    c.wait_send()


def ocean_step(comm, table, idx, remap, lift, ocean, wet, taps, gains, up, down, head, second, embed):
    vm = pl.BlockSpec(memory_space=pltpu.VMEM)
    far = pl.BlockSpec(memory_space=pl.ANY)
    width = second.shape[-1]
    dma = pltpu.SemaphoreType.DMA
    params = dict(collective_id=1, has_side_effects=True) if comm else {}
    return pl.pallas_call(
        functools.partial(ocean_kernel, comm),
        out_shape=[jax.ShapeDtypeStruct((32, 32, width), BF), jax.ShapeDtypeStruct((64, 64, 192), BF)],
        in_specs=[vm] * 11 + [far, vm],
        out_specs=[vm] * 2,
        scratch_shapes=[
            pltpu.VMEM((64, 64, 192), F32), pltpu.VMEM((64, 64, 192), F32), pltpu.VMEM((4, 256, width), F32),
            pltpu.VMEM((512, 256), BF), pltpu.VMEM((64, 128), F32), pltpu.VMEM((2, 3, 56, 128), F32),
            pltpu.VMEM((3, 21 * 256, 256), BF), pltpu.VMEM((4, 3, 80, 256), F32), pltpu.VMEM((3, 18, 64, 1792), BF),
            pltpu.VMEM((3, CH * 64, 256), F32), pltpu.VMEM((4, CH * 64, 192), BF), pltpu.VMEM((2, CH * 64, 128), F32),
            pltpu.VMEM((2, 2, 3, 64, 192), BF), pltpu.VMEM((2, 2, 3, 64, 192), BF),
            pltpu.VMEM((2, 2, 32, 8, 192), BF), pltpu.VMEM((2, 2, 32, 8, 192), BF),
            pltpu.VMEM((2, 2, 2, 3, 8, 192), BF), pltpu.VMEM((2, 2, 2, 3, 8, 192), BF),
            dma, dma((2, 12)), dma((2, 12)),
        ],
        compiler_params=pltpu.CompilerParams(vmem_limit_bytes=60 * 2**20, **params),
        name="ocean",
        cost_estimate=pl.CostEstimate(flops=50 * 10**9, bytes_accessed=16 * 2**20, transcendentals=6 * 10**6),
    )(table, idx, remap, lift, ocean, wet, jnp.swapaxes(taps, 0, 1), gains, up, down, head, second, embed)


def air_kernel(comm, x_ref, gain_attn_ref, gain_mlp_ref, qkv_hbm, out_hbm, up_hbm, down_hbm, head_ref, second_ref, table_ref,
               qkv_w, out_w, up_w, down_w, normed, edge_send, edge_recv, qkv, beside, mixed, flux_ref, load_sem, send_sem, recv_sem, flux_send, flux_recv):
    width = x_ref.shape[-1]
    loads = [
        pltpu.make_async_copy(source, target, load_sem.at[i])
        for i, (source, target) in enumerate(((qkv_hbm, qkv_w), (out_hbm, out_w), (up_hbm, up_w), (down_hbm, down_w)))
    ]
    for load in loads:
        load.start()
    if comm:
        lat = lax.axis_index("lat")
        lon = lax.axis_index("lon")
        count = lax.axis_size("lon")
        west_id = (lat, lax.rem(lon + count - 1, count))
        east_id = (lat, lax.rem(lon + 1, count))
        barrier = pltpu.get_barrier_semaphore()

        def greet(k, _):
            pl.semaphore_signal(barrier, inc=1, device_id=(lat, lax.rem(lon + k, count)), device_id_type=MESH)
            return 0

        lax.fori_loop(1, count, greet, 0)

        def flux_copy(part, k):
            bands = (slice(0, 3), slice(3, 4))[part]
            return pltpu.make_async_remote_copy(
                src_ref=flux_ref.at[bands], dst_ref=table_ref.at[lon, bands], send_sem=flux_send.at[part, k],
                recv_sem=flux_recv.at[part, lon], device_id=(lat, lax.rem(lon + k, count)), device_id_type=MESH,
            )

        def flux_arrival(part, k):
            bands = (slice(0, 3), slice(3, 4))[part]
            peer = lax.rem(lon + k, count)
            return pltpu.make_async_remote_copy(
                src_ref=flux_ref.at[bands], dst_ref=table_ref.at[peer, bands], send_sem=flux_send.at[part, k],
                recv_sem=flux_recv.at[part, peer], device_id=(lat, peer), device_id_type=MESH,
            )

        def over_peers(part, act):
            def one(k, _):
                act(part, k)
                return 0

            lax.fori_loop(1, count, one, 0)

    def cells(band, j):
        return x_ref[band, :, 8 * j : 8 * j + 8, :].astype(F32).reshape(64, width)

    def rms(values, gain):
        return (values * lax.rsqrt(jnp.mean(values * values, axis=1, keepdims=True) + EPS) * gain).astype(BF)

    for band in range(4):
        for side, j in ((0, 0), (1, 3)):
            block = rms(cells(band, j), gain_attn_ref[...].reshape(1, width))
            normed[band, j] = block
            edge_send[side, band] = block
    if comm:
        pl.semaphore_wait(barrier, count - 1)
        copies = [
            pltpu.make_async_remote_copy(
                src_ref=edge_send.at[side], dst_ref=edge_recv.at[1 - side], send_sem=send_sem.at[side],
                recv_sem=recv_sem.at[1 - side], device_id=device, device_id_type=MESH,
            )
            for side, device in ((0, west_id), (1, east_id))
        ]
        for copy in copies:
            copy.start()
    for band in range(4):
        for j in (1, 2):
            normed[band, j] = rms(cells(band, j), gain_attn_ref[...].reshape(1, width))
    loads[0].wait()

    def project(band, _):
        rows = normed[band].reshape(256, width)
        for part in range(3):
            lanes = slice(width * part, width * part + width)
            result = jnp.dot(rows, qkv_w[:, lanes], preferred_element_type=F32)
            if part == 0:
                result = result.astype(BF) * BF(0.125)
            qkv[band, :, :, lanes] = result.astype(BF).reshape(4, 64, width)
        return 0

    lax.fori_loop(0, 4, project, 0)
    even = lax.broadcasted_iota(jnp.int32, (128, 128), 1) < 64
    zero = jnp.zeros((128, 128), BF)
    tally = jnp.concatenate([jnp.where(even, 1.0, 0.0), jnp.where(even, 0.0, 1.0)], axis=0).astype(BF)

    def paired(block):
        return jnp.concatenate([jnp.where(even, block, zero), jnp.where(even, zero, block)], axis=0)

    def window(keys, vals, query):
        keys = paired(stack(*keys))
        vals = jnp.concatenate([paired(stack(*vals)), tally], axis=1)
        scores = lax.dot_general(stack(*query), keys, NT, preferred_element_type=F32)
        parts = [scores[:, :128], scores[:, 128:]]
        parts = [jnp.exp(s - jnp.max(s, axis=1, keepdims=True)).astype(BF) for s in parts]
        result = jnp.dot(jnp.concatenate(parts, axis=1), vals, preferred_element_type=F32)
        return (result[:, :128] / result[:, 128:]).astype(BF)

    def stack(*blocks):
        return jnp.concatenate(blocks, axis=0)

    def pair_lanes(pair):
        return [slice(width * part + 128 * pair, width * part + 128 * pair + 128) for part in range(3)]

    def middle(band):
        for pair in range(6):
            q, k, v = pair_lanes(pair)
            mixed[0, band // 2, 128 * (band % 2) : 128 * (band % 2) + 128, q] = window(
                [qkv[band, 1, :, k], qkv[band, 2, :, k]], [qkv[band, 1, :, v], qkv[band, 2, :, v]], [qkv[band, 1, :, q], qkv[band, 2, :, q]]
            )

    def edges(band):
        base = 128 * (band % 2)
        for pair in range(6):
            q, k, v = pair_lanes(pair)
            mixed[1, band // 2, base : base + 64, q] = window(
                [beside[0, band, :, q], qkv[band, 0, :, k]], [beside[0, band, :, k], qkv[band, 0, :, v]], [qkv[band, 0, :, q]]
            )
            mixed[1, band // 2, base + 64 : base + 128, q] = window(
                [qkv[band, 3, :, k], beside[1, band, :, q]], [qkv[band, 3, :, v], beside[1, band, :, k]], [qkv[band, 3, :, q]]
            )

    def feed_forward(kind, pair):
        first = stack(*[cells(2 * pair + band, j) for band in range(2) for j in ((1, 2), (0, 3))[kind]])
        first = first + jnp.dot(mixed[kind, pair], out_w[...], preferred_element_type=F32)
        rows = rms(first, gain_mlp_ref[...].reshape(1, width))
        total = first
        for part in range(4):
            lanes = slice(width * part, width * part + width)
            hidden = gelu(jnp.dot(rows, up_w[:, lanes], preferred_element_type=F32)).astype(BF)
            total = total + jnp.dot(hidden, down_w[lanes, :], preferred_element_type=F32)
        second_ref[2 * kind + pair] = total
        flux_ref[2 * kind + pair] = lax.dot_general(head_ref[...], total.astype(BF), NT, preferred_element_type=F32).astype(BF)

    middle(0)
    middle(1)
    for load in loads[1:]:
        load.wait()
    feed_forward(0, 0)
    middle(2)
    middle(3)
    feed_forward(0, 1)
    if comm:
        for copy in copies:
            copy.wait_recv()

    def project_beside(side, _):
        rows = edge_recv[side].reshape(256, width)
        for part in range(2):
            lanes = slice(width * part, width * part + width)
            result = jnp.dot(rows, qkv_w[:, width * (part + 1) : width * (part + 2)], preferred_element_type=F32)
            beside[side, :, :, lanes] = result.astype(BF).reshape(4, 64, width)
        return 0

    lax.fori_loop(0, 2, project_beside, 0)
    edges(0)
    edges(1)
    feed_forward(1, 0)
    if comm:
        over_peers(0, lambda part, k: flux_copy(part, k).start())
    edges(2)
    edges(3)
    feed_forward(1, 1)
    if comm:
        over_peers(1, lambda part, k: flux_copy(part, k).start())
        table_ref[lon] = flux_ref[...]
        for copy in copies:
            copy.wait_send()
        for part in range(2):
            over_peers(part, lambda part, k: flux_arrival(part, k).wait_recv())
            over_peers(part, lambda part, k: flux_copy(part, k).wait_send())
    else:
        table_ref[0] = flux_ref[...]


def atmosphere(comm, x, gain_attn, gain_mlp, qkv_w, out_w, up_w, down_w, flux_head):
    width = x.shape[-1]
    vm = pl.BlockSpec(memory_space=pltpu.VMEM)
    far = pl.BlockSpec(memory_space=pl.ANY)
    params = dict(collective_id=2, has_side_effects=True) if comm else {}
    return pl.pallas_call(
        functools.partial(air_kernel, comm),
        out_shape=[jax.ShapeDtypeStruct((4, 256, width), F32), jax.ShapeDtypeStruct((16, 4, 8, 256), BF)],
        in_specs=[vm, vm, vm, far, far, far, far, vm],
        out_specs=[vm, vm],
        scratch_shapes=[
            pltpu.VMEM(qkv_w.shape, BF), pltpu.VMEM(out_w.shape, BF), pltpu.VMEM(up_w.shape, BF), pltpu.VMEM(down_w.shape, BF),
            pltpu.VMEM((4, 4, 64, width), BF),
            pltpu.VMEM((2, 4, 64, width), BF), pltpu.VMEM((2, 4, 64, width), BF),
            pltpu.VMEM((4, 4, 64, 3 * width), BF),
            pltpu.VMEM((2, 4, 64, 2 * width), BF),
            pltpu.VMEM((2, 2, 256, width), BF), pltpu.VMEM((4, 8, 256), BF),
            pltpu.SemaphoreType.DMA((4,)), pltpu.SemaphoreType.DMA((2,)), pltpu.SemaphoreType.DMA((2,)),
            pltpu.SemaphoreType.DMA((2, 16)), pltpu.SemaphoreType.DMA((2, 16)),
        ],
        compiler_params=pltpu.CompilerParams(vmem_limit_bytes=56 * 2**20, **params),
        name="air",
        cost_estimate=pl.CostEstimate(flops=16 * 10**9, bytes_accessed=20 * 2**20, transcendentals=5 * 10**6),
    )(x.reshape(4, 8, 32, width), gain_attn, gain_mlp, qkv_w, out_w, up_w, down_w, jnp.swapaxes(flux_head, 0, 1))


def body(
    atmos_features,
    ocean_features,
    wet_cell_mask,
    overlay_cell_index,
    remap_weight,
    query_key_value_weight,
    attention_out_weight,
    feedforward_up_weight,
    feedforward_down_weight,
    attention_gain,
    feedforward_gain,
    flux_head_weight,
    surface_temp_embedding,
    forcing_lift_weight,
    depthwise_kernels,
    ocean_norm_gains,
    ocean_up_weights,
    ocean_down_weights,
    surface_temp_head,
):
    second, table = atmosphere(
        True, atmos_features, attention_gain, feedforward_gain, query_key_value_weight, attention_out_weight,
        feedforward_up_weight, feedforward_down_weight, flux_head_weight,
    )
    updated, ocean_out = ocean_step(
        True, table, overlay_cell_index, remap_weight, forcing_lift_weight, ocean_features, wet_cell_mask, depthwise_kernels,
        ocean_norm_gains, ocean_up_weights, jnp.swapaxes(ocean_down_weights, 1, 2), surface_temp_head, second,
        surface_temp_embedding,
    )
    return (updated, ocean_out)


def solution(mesh):
    cells = P("lat", "lon", None)
    in_specs = (cells, cells, P("lat", "lon"), P(None, "lat", "lon"), P(None, "lat", "lon")) + (P(),) * 14
    return jax.shard_map(body, mesh=mesh, in_specs=in_specs, out_specs=(cells, cells), check_vma=False)
```

```python
import functools

import jax
import jax.numpy as jnp
from jax import lax
from jax.experimental import pallas as pl
from jax.experimental.pallas import tpu as pltpu
from jax.sharding import PartitionSpec as P

BF = jnp.bfloat16
F32 = jnp.float32
EPS = 1e-6
MESH = pl.DeviceIdType.MESH
CH = 4

CELLS = 512
def split(x):
    hi=x.astype(BF)
    return hi,(x-hi.astype(F32)).astype(BF)

def split_dot(x, ones):
    hi,lo=split(x)
    return jnp.dot(hi,ones,preferred_element_type=F32)+jnp.dot(lo,ones,preferred_element_type=F32)

def gelu(x):
    inner=x*(0.7978845608028654+0.035677408136300125*(x*x))
    h=0.5*x
    return h+h*jnp.tanh(inner)

NT = (((1,),(1,)),((),()))


def ocean_kernel(comm, table_ref, index_ref, remap_ref, lift_ref, ocean_ref, wet_ref, taps_ref, gains_ref, up_ref, down_ref, head_ref, second_hbm, embed_ref,
                 updated_ref, out_ref, field_ref, next_ref, second_ref, t_ref, wet_t, taps_pair, w_ref, x4_ref, a_ref, y_ref, n_ref, warm_ref,
                 rows_send, rows_recv, side_send, side_recv, corner_send, corner_recv, load_sem, send_sem, recv_sem):
    load = pltpu.make_async_copy(second_hbm, second_ref, load_sem)
    load.start()
    if comm:
        lat = lax.axis_index("lat")
        lon = lax.axis_index("lon")
        lats = lax.axis_size("lat")
        lons = lax.axis_size("lon")
        top = lat == lats - 1
        bottom = lat == 0
        mirror = lons - 1 - lon
        up_id = (jnp.where(top, lat, lat + 1), jnp.where(top, mirror, lon))
        down_id = (jnp.where(bottom, lat, lat - 1), jnp.where(bottom, mirror, lon))
        west_id = (lat, lax.rem(lon + lons - 1, lons))
        east_id = (lat, lax.rem(lon + 1, lons))
        barrier = pltpu.get_barrier_semaphore()

        for other in (up_id, down_id, west_id, east_id):
            pl.semaphore_signal(barrier, inc=1, device_id=other, device_id_type=MESH)
        up_slot = jnp.where(top, 0, 1)
        down_slot = jnp.where(bottom, 1, 0)

    wet = wet_ref[...].astype(F32)
    wet_t[...] = jnp.concatenate([wet, wet], axis=0).T

    def wet_from(row):
        return pltpu.roll(wet_t[...], 128 - row, axis=1)

    for blk in range(2):
        for g in range(3):
            piece = taps_ref[:, blk, 64 * g : 64 * g + 64]
            taps_pair[blk, g, 0:49] = jnp.concatenate([piece, piece], axis=1)
    sub = lax.broadcasted_iota(jnp.int32, (64, 128), 0)
    lane = lax.broadcasted_iota(jnp.int32, (64, 128), 1)
    low_diag = lane == sub
    high_diag = lane == sub + 64
    s2 = lax.broadcasted_iota(jnp.int32, (256, 256), 0) // 64
    l2 = lax.broadcasted_iota(jnp.int32, (256, 256), 1) // 64
    ones = jnp.where(s2 == l2, 1.0, 0.0).astype(BF)
    flip = lax.broadcasted_iota(jnp.int32, (64, 64), 0) + lax.broadcasted_iota(jnp.int32, (64, 64), 1)
    flip = jnp.where(flip == 63, 1.0, 0.0).astype(BF)

    def build_weights(blk):
        def build(b, _):
            for g in range(3):
                for d in range(3):
                    for q in range(4):
                        halves = []
                        for half in range(2):
                            a = 4 * (d - 1) + q - 2 * half + 3
                            value = jnp.zeros((64, 128), F32)
                            if 0 <= a - 1 < 7:
                                value = jnp.where(high_diag, taps_pair[blk, g, pl.ds(7 * (a - 1) + b, 1), :], value)
                            if 0 <= a < 7:
                                value = jnp.where(low_diag, taps_pair[blk, g, pl.ds(7 * a + b, 1), :], value)
                            halves.append(value.astype(BF))
                        row = pl.multiple_of(b * 256, 256) + (1792 * d + 64 * q)
                        w_ref[g, pl.ds(pl.multiple_of(row, 64), 64), :] = jnp.concatenate(halves, axis=1)
            return 0

        lax.fori_loop(0, 7, build, 0)

    for h in range(4):
        t_ref[128 * h : 128 * h + 128, :] = table_ref[:, h].astype(F32).reshape(128, 256).astype(BF)
    ids = lax.broadcasted_iota(jnp.int32, (256, CELLS), 0)
    lift_hi, lift_lo = split(lift_ref[...])
    lift = jnp.concatenate([lift_hi, lift_hi, lift_lo], axis=0)

    def line(rows):
        return jnp.concatenate([rows[j : j + 1] for j in range(8)], axis=1)

    def force(i, _):
        total = jnp.zeros((8, CELLS), F32)
        for e in range(4):
            index = line(index_ref[e, pl.ds(pl.multiple_of(8 * i, 8), 8), :])
            lo = ((index >> 12) & 1) << 7 | ((index >> 4) & 1) << 6 | ((index >> 9) & 7) << 3 | (index & 7)
            edge = 1 - (((index >> 4) ^ (index >> 3)) & 1)
            hi = jnp.broadcast_to(edge << 5 | (index >> 13) << 4 | ((index >> 5) & 15), (8, CELLS))
            hit = jnp.where(ids == lo, 1.0, 0.0).astype(BF)
            res = jnp.dot(t_ref[...], hit, preferred_element_type=F32)
            got = res[0:8]
            for k in range(1, 64):
                got = jnp.where(hi == k, res[8 * k : 8 * k + 8], got)
            total = total + got * line(remap_ref[e, pl.ds(pl.multiple_of(8 * i, 8), 8), :])
        high = total.astype(BF).astype(F32)
        spread = jnp.concatenate([high, total - high, high], axis=0).astype(BF)
        lifted = lax.dot_general(spread, lift, (((0,), (0,)), ((), ())), preferred_element_type=F32)
        here = wet_from(8 * i)
        for j in range(8):
            row = ocean_ref[8 * i + j].astype(F32) + lifted[64 * j : 64 * j + 64]
            field_ref[8 * i + j] = here[:, j : j + 1] * row
        return 0

    def remote(blk, source, target, index, slot, device):
        return pltpu.make_async_remote_copy(
            src_ref=source, dst_ref=target, send_sem=send_sem.at[blk, index], recv_sem=recv_sem.at[blk, slot],
            device_id=device, device_id_type=MESH,
        )

    def down_copy(blk):
        return remote(blk, rows_send.at[blk, 1], rows_recv.at[blk, down_slot], 1, down_slot, down_id)

    def up_copy(blk):
        return remote(blk, rows_send.at[blk, 0], rows_recv.at[blk, up_slot], 0, up_slot, up_id)

    def corner_copies(blk):
        return [
            remote(blk, corner_send.at[blk, 0], corner_recv.at[blk, 1], 2, 3, west_id),
            remote(blk, corner_send.at[blk, 1], corner_recv.at[blk, 0], 3, 2, east_id),
        ]

    def side_copies(blk, ci):
        part = pl.ds(8 * ci, 8)
        return [
            remote(blk, side_send.at[blk, 0, part], side_recv.at[blk, 1, part], 4 + ci, 8 + ci, west_id),
            remote(blk, side_send.at[blk, 1, part], side_recv.at[blk, 0, part], 8 + ci, 4 + ci, east_id),
        ]

    def ship(blk, src, ci):
        early = lax.broadcasted_iota(jnp.int32, (8, 8, 192), 1) < 4
        west = src[pl.ds(16 * ci, 16), 0:8, :].reshape(8, 2, 8, 192)
        east = src[pl.ds(16 * ci, 16), 56:64, :].reshape(8, 2, 8, 192)
        part = pl.ds(8 * ci, 8)
        side_send[blk, 0, part] = jnp.where(early, west[:, 0], pltpu.roll(west[:, 1], 4, axis=1)).astype(BF)
        side_send[blk, 1, part] = jnp.where(early, pltpu.roll(east[:, 0], 4, axis=1), east[:, 1]).astype(BF)
        for c in side_copies(blk, ci):
            c.start()

    def ship_down(blk, src):
        for k in range(3):
            rows_send[blk, 1, k] = src[k].astype(BF)
        down_copy(blk).start()

    def ship_up(blk, src):
        for k in range(3):
            turned = jnp.dot(flip, src[63 - k].astype(BF), preferred_element_type=F32)
            rows_send[blk, 0, k] = jnp.where(top, turned, src[61 + k]).astype(BF)
        up_copy(blk).start()

    if comm:
        pl.semaphore_wait(barrier, 4)

    def force_part(ci, _):
        force(2 * ci, 0)
        force(2 * ci + 1, 0)
        if comm:
            ship(0, field_ref, ci)

            @pl.when(ci == 0)
            def _():
                ship_down(0, field_ref)

        return 0

    lax.fori_loop(0, 4, force_part, 0)
    if comm:
        ship_up(0, field_ref)

    for blk in range(2):
        src = field_ref if blk == 0 else next_ref

        build_weights(blk)
        if comm:
            remote(blk, rows_send.at[blk, 0], rows_recv.at[blk, 0], 0, 0, up_id).wait_recv()
            remote(blk, rows_send.at[blk, 0], rows_recv.at[blk, 1], 0, 1, up_id).wait_recv()
            for s in range(2):
                corner_send[blk, 0, s] = rows_recv[blk, s, :, 0:8, :]
                corner_send[blk, 1, s] = rows_recv[blk, s, :, 56:64, :]
            for c in corner_copies(blk):
                c.start()
            for ci in range(4):
                for c in side_copies(blk, ci):
                    c.wait_recv()

        def place(i, rows, slot=0):
            for g in range(3):
                x4_ref[slot, g] = jnp.concatenate([r[:, 64 * g : 64 * g + 64] for r in rows], axis=1)
                for b in range(7):
                    a_ref[g, i, :, 256 * b : 256 * b + 256] = x4_ref[slot, g, pl.ds(5 + b, 64), :].astype(BF)

        def group(i, slot):
            rows = []
            for p in range(4):
                r = 4 * (i - 1) + p
                west = side_recv[blk, 0, 2 * (i - 1) + p // 2].astype(F32)
                east = side_recv[blk, 1, 2 * (i - 1) + p // 2].astype(F32)
                if p % 2 == 0:
                    west = pltpu.roll(west, 4, axis=0)
                else:
                    east = pltpu.roll(east, 4, axis=0)
                rows.append(jnp.concatenate([west, src[r], east], axis=0))
            place(i, rows, slot)

        def groups(i, _):
            for slot in range(4):
                group(4 * i + slot + 1, slot)
            return 0

        lax.fori_loop(0, 16 // 4, groups, 0)
        if comm:
            for c in corner_copies(blk):
                c.wait_recv()
        empty = jnp.zeros((80, 192), F32)

        def outer(s, k):
            pieces = [corner_recv[blk, 0, s, k], rows_recv[blk, s, k], corner_recv[blk, 1, s, k]]
            return jnp.concatenate([piece.astype(F32) for piece in pieces], axis=0)

        place(17, [outer(0, k) for k in range(3)] + [empty])
        souths = [outer(1, k) for k in range(3)]
        if comm:
            souths = [jnp.where(bottom, 0.0, s) for s in souths]
        place(0, [empty] + souths)

        def conv(ci):
            base = ci * CH
            for g in range(3):
                acc = None
                for d in range(3):
                    lhs = a_ref[g, pl.ds(base + d, CH)].reshape(CH * 64, 1792)
                    part = jnp.dot(lhs, w_ref[g, d * 1792 : (d + 1) * 1792, :], preferred_element_type=F32)
                    acc = part if acc is None else acc + part
                y_ref[g] = acc

        gains = [jnp.concatenate([gains_ref[blk : blk + 1, 64 * g : 64 * g + 64]] * 4, axis=1) for g in range(3)]

        def norm():
            mean = split_dot(y_ref[0] + y_ref[1] + y_ref[2], ones) * (1 / 192)
            cs = [y_ref[g] - mean for g in range(3)]
            var = split_dot(cs[0] * cs[0] + cs[1] * cs[1] + cs[2] * cs[2], ones) * (1 / 192)
            inv = lax.rsqrt(var + EPS)
            ns = [(cs[g] * inv * gains[g]).astype(BF) for g in range(3)]
            for p in range(4):
                n_ref[p] = jnp.concatenate([ns[g][:, 64 * p : 64 * p + 64] for g in range(3)], axis=1)

        def mlp(ci):
            base = ci * CH
            here = wet_from(16 * ci)
            temps = []
            for p in range(4):
                act = gelu(jnp.dot(n_ref[p], up_ref[blk], preferred_element_type=F32)).astype(BF)
                inc = lax.dot_general(act, down_ref[blk], NT, preferred_element_type=F32)
                news = []
                for j in range(CH):
                    r = 4 * (base + j) + p
                    new = src[r] + here[:, 4 * j + p : 4 * j + p + 1] * inc[64 * j : 64 * j + 64]
                    if blk == 1:
                        out_ref[r] = new.astype(BF)
                        news.append(new)
                    else:
                        next_ref[r] = new
                if blk == 1:
                    hi, lo = split(jnp.concatenate(news, axis=0))
                    head_hi, head_lo = split(jnp.broadcast_to(head_ref[...].reshape(1, 192), (128, 192)))
                    temps.append(
                        lax.dot_general(hi, head_hi, NT, preferred_element_type=F32)
                        + lax.dot_general(lo, head_hi, NT, preferred_element_type=F32)
                        + lax.dot_general(hi, head_lo, NT, preferred_element_type=F32)
                    )
            if blk == 1:
                for s in range(2):
                    warm_ref[0] = temps[2 * s] + temps[2 * s + 1]
                    for j in range(CH):
                        both = here[:, 4 * j + 2 * s : 4 * j + 2 * s + 1] + here[:, 4 * j + 2 * s + 1 : 4 * j + 2 * s + 2]
                        warm_ref[1, 64 * j : 64 * j + 64] = jnp.broadcast_to(both, (64, 128))
                    pair = lambda k: warm_ref[k, pl.ds(0, 128, stride=2), :] + warm_ref[k, pl.ds(1, 128, stride=2), :]
                    warmth = pair(0) / jnp.maximum(pair(1), 1.0)
                    for j in range(CH):
                        r = 2 * j + s
                        start = [pl.multiple_of(128 * (ci % 2), 128) + 64 * (c // 2) + 8 * r for c in range(4)]
                        old = jnp.concatenate(
                            [second_ref[(2, 0, 0, 2)[c] + ci // 2, pl.ds(pl.multiple_of(start[c], 8), 8), :] for c in range(4)], axis=0
                        )
                        row = jnp.concatenate([warmth[32 * j : 32 * j + 32]] * 6, axis=1)
                        updated_ref[8 * ci + r] = (old + row * embed_ref[...].reshape(1, 768)).astype(BF)

        conv(0)
        if blk == 1:
            load.wait()

        def step(ci, _):
            norm()
            conv(ci)
            mlp(ci - 1)
            if comm and blk == 0:
                ship(1, next_ref, ci - 1)

                @pl.when(ci == 1)
                def _():
                    ship_down(1, next_ref)

            return 0

        lax.fori_loop(1, 16 // CH, step, 0)
        norm()
        mlp(16 // CH - 1)
        if comm and blk == 0:
            ship(1, next_ref, 16 // CH - 1)
            ship_up(1, next_ref)
    if comm:
        for blk in range(2):
            for c in [up_copy(blk), down_copy(blk), *corner_copies(blk)]:
                c.wait_send()
            for ci in range(4):
                for c in side_copies(blk, ci):
                    c.wait_send()


def ocean_step(comm, table, idx, remap, lift, ocean, wet, taps, gains, up, down, head, second, embed):
    vm = pl.BlockSpec(memory_space=pltpu.VMEM)
    far = pl.BlockSpec(memory_space=pl.ANY)
    width = second.shape[-1]
    dma = pltpu.SemaphoreType.DMA
    params = dict(collective_id=1, has_side_effects=True) if comm else {}
    return pl.pallas_call(
        functools.partial(ocean_kernel, comm),
        out_shape=[jax.ShapeDtypeStruct((32, 32, width), BF), jax.ShapeDtypeStruct((64, 64, 192), BF)],
        in_specs=[vm] * 11 + [far, vm],
        out_specs=[vm] * 2,
        scratch_shapes=[
            pltpu.VMEM((64, 64, 192), F32), pltpu.VMEM((64, 64, 192), F32), pltpu.VMEM((4, 256, width), F32),
            pltpu.VMEM((512, 256), BF), pltpu.VMEM((64, 128), F32), pltpu.VMEM((2, 3, 56, 128), F32),
            pltpu.VMEM((3, 21 * 256, 256), BF), pltpu.VMEM((4, 3, 80, 256), F32), pltpu.VMEM((3, 18, 64, 1792), BF),
            pltpu.VMEM((3, CH * 64, 256), F32), pltpu.VMEM((4, CH * 64, 192), BF), pltpu.VMEM((2, CH * 64, 128), F32),
            pltpu.VMEM((2, 2, 3, 64, 192), BF), pltpu.VMEM((2, 2, 3, 64, 192), BF),
            pltpu.VMEM((2, 2, 32, 8, 192), BF), pltpu.VMEM((2, 2, 32, 8, 192), BF),
            pltpu.VMEM((2, 2, 2, 3, 8, 192), BF), pltpu.VMEM((2, 2, 2, 3, 8, 192), BF),
            dma, dma((2, 12)), dma((2, 12)),
        ],
        compiler_params=pltpu.CompilerParams(vmem_limit_bytes=60 * 2**20, **params),
        name="ocean",
        cost_estimate=pl.CostEstimate(flops=50 * 10**9, bytes_accessed=16 * 2**20, transcendentals=6 * 10**6),
    )(table, idx, remap, lift, ocean, wet, jnp.swapaxes(taps, 0, 1), gains, up, down, head, second, embed)


def air_kernel(comm, x_ref, gain_attn_ref, gain_mlp_ref, qkv_hbm, out_hbm, up_hbm, down_hbm, head_ref, second_ref, table_ref,
               qkv_w, out_w, up_w, down_w, normed, edge_send, edge_recv, qkv, beside, mixed, flux_ref, load_sem, send_sem, recv_sem, flux_send, flux_recv):
    width = x_ref.shape[-1]
    loads = [
        pltpu.make_async_copy(source, target, load_sem.at[i])
        for i, (source, target) in enumerate(((qkv_hbm, qkv_w), (out_hbm, out_w), (up_hbm, up_w), (down_hbm, down_w)))
    ]
    for load in loads:
        load.start()
    if comm:
        lat = lax.axis_index("lat")
        lon = lax.axis_index("lon")
        count = lax.axis_size("lon")
        west_id = (lat, lax.rem(lon + count - 1, count))
        east_id = (lat, lax.rem(lon + 1, count))
        barrier = pltpu.get_barrier_semaphore()

        def greet(k, _):
            pl.semaphore_signal(barrier, inc=1, device_id=(lat, lax.rem(lon + k, count)), device_id_type=MESH)
            return 0

        lax.fori_loop(1, count, greet, 0)

        def flux_copy(part, k):
            bands = (slice(0, 3), slice(3, 4))[part]
            return pltpu.make_async_remote_copy(
                src_ref=flux_ref.at[bands], dst_ref=table_ref.at[lon, bands], send_sem=flux_send.at[part, k],
                recv_sem=flux_recv.at[part, lon], device_id=(lat, lax.rem(lon + k, count)), device_id_type=MESH,
            )

        def flux_arrival(part, k):
            bands = (slice(0, 3), slice(3, 4))[part]
            peer = lax.rem(lon + k, count)
            return pltpu.make_async_remote_copy(
                src_ref=flux_ref.at[bands], dst_ref=table_ref.at[peer, bands], send_sem=flux_send.at[part, k],
                recv_sem=flux_recv.at[part, peer], device_id=(lat, peer), device_id_type=MESH,
            )

        def over_peers(part, act):
            def one(k, _):
                act(part, k)
                return 0

            lax.fori_loop(1, count, one, 0)

    def cells(band, j):
        return x_ref[band, :, 8 * j : 8 * j + 8, :].astype(F32).reshape(64, width)

    def rms(values, gain):
        return (values * lax.rsqrt(jnp.mean(values * values, axis=1, keepdims=True) + EPS) * gain).astype(BF)

    for band in range(4):
        for side, j in ((0, 0), (1, 3)):
            block = rms(cells(band, j), gain_attn_ref[...].reshape(1, width))
            normed[band, j] = block
            edge_send[side, band] = block
    if comm:
        pl.semaphore_wait(barrier, count - 1)
        copies = [
            pltpu.make_async_remote_copy(
                src_ref=edge_send.at[side], dst_ref=edge_recv.at[1 - side], send_sem=send_sem.at[side],
                recv_sem=recv_sem.at[1 - side], device_id=device, device_id_type=MESH,
            )
            for side, device in ((0, west_id), (1, east_id))
        ]
        for copy in copies:
            copy.start()
    for band in range(4):
        for j in (1, 2):
            normed[band, j] = rms(cells(band, j), gain_attn_ref[...].reshape(1, width))
    loads[0].wait()

    def project(band, _):
        rows = normed[band].reshape(256, width)
        for part in range(3):
            lanes = slice(width * part, width * part + width)
            result = jnp.dot(rows, qkv_w[:, lanes], preferred_element_type=F32)
            if part == 0:
                result = result.astype(BF) * BF(0.125)
            qkv[band, :, :, lanes] = result.astype(BF).reshape(4, 64, width)
        return 0

    lax.fori_loop(0, 4, project, 0)
    even = lax.broadcasted_iota(jnp.int32, (128, 128), 1) < 64
    zero = jnp.zeros((128, 128), BF)
    tally = jnp.concatenate([jnp.where(even, 1.0, 0.0), jnp.where(even, 0.0, 1.0)], axis=0).astype(BF)

    def paired(block):
        return jnp.concatenate([jnp.where(even, block, zero), jnp.where(even, zero, block)], axis=0)

    def window(keys, vals, query):
        keys = paired(stack(*keys))
        vals = jnp.concatenate([paired(stack(*vals)), tally], axis=1)
        scores = lax.dot_general(stack(*query), keys, NT, preferred_element_type=F32)
        parts = [scores[:, :128], scores[:, 128:]]
        parts = [jnp.exp(s - jnp.max(s, axis=1, keepdims=True)).astype(BF) for s in parts]
        result = jnp.dot(jnp.concatenate(parts, axis=1), vals, preferred_element_type=F32)
        return (result[:, :128] / result[:, 128:]).astype(BF)

    def stack(*blocks):
        return jnp.concatenate(blocks, axis=0)

    def pair_lanes(pair):
        return [slice(width * part + 128 * pair, width * part + 128 * pair + 128) for part in range(3)]

    def middle(band):
        for pair in range(6):
            q, k, v = pair_lanes(pair)
            mixed[0, band // 2, 128 * (band % 2) : 128 * (band % 2) + 128, q] = window(
                [qkv[band, 1, :, k], qkv[band, 2, :, k]], [qkv[band, 1, :, v], qkv[band, 2, :, v]], [qkv[band, 1, :, q], qkv[band, 2, :, q]]
            )

    def edges(band):
        base = 128 * (band % 2)
        for pair in range(6):
            q, k, v = pair_lanes(pair)
            mixed[1, band // 2, base : base + 64, q] = window(
                [beside[0, band, :, q], qkv[band, 0, :, k]], [beside[0, band, :, k], qkv[band, 0, :, v]], [qkv[band, 0, :, q]]
            )
            mixed[1, band // 2, base + 64 : base + 128, q] = window(
                [qkv[band, 3, :, k], beside[1, band, :, q]], [qkv[band, 3, :, v], beside[1, band, :, k]], [qkv[band, 3, :, q]]
            )

    def feed_forward(kind, pair):
        first = stack(*[cells(2 * pair + band, j) for band in range(2) for j in ((1, 2), (0, 3))[kind]])
        first = first + jnp.dot(mixed[kind, pair], out_w[...], preferred_element_type=F32)
        rows = rms(first, gain_mlp_ref[...].reshape(1, width))
        total = first
        for part in range(4):
            lanes = slice(width * part, width * part + width)
            hidden = gelu(jnp.dot(rows, up_w[:, lanes], preferred_element_type=F32)).astype(BF)
            total = total + jnp.dot(hidden, down_w[lanes, :], preferred_element_type=F32)
        second_ref[2 * kind + pair] = total
        flux_ref[2 * kind + pair] = lax.dot_general(head_ref[...], total.astype(BF), NT, preferred_element_type=F32).astype(BF)

    middle(0)
    middle(1)
    for load in loads[1:]:
        load.wait()
    feed_forward(0, 0)
    middle(2)
    middle(3)
    feed_forward(0, 1)
    if comm:
        for copy in copies:
            copy.wait_recv()

    def project_beside(side, _):
        rows = edge_recv[side].reshape(256, width)
        for part in range(2):
            lanes = slice(width * part, width * part + width)
            result = jnp.dot(rows, qkv_w[:, width * (part + 1) : width * (part + 2)], preferred_element_type=F32)
            beside[side, :, :, lanes] = result.astype(BF).reshape(4, 64, width)
        return 0

    lax.fori_loop(0, 2, project_beside, 0)
    edges(0)
    edges(1)
    feed_forward(1, 0)
    if comm:
        over_peers(0, lambda part, k: flux_copy(part, k).start())
    edges(2)
    edges(3)
    feed_forward(1, 1)
    if comm:
        over_peers(1, lambda part, k: flux_copy(part, k).start())
        table_ref[lon] = flux_ref[...]
        for copy in copies:
            copy.wait_send()
        for part in range(2):
            over_peers(part, lambda part, k: flux_arrival(part, k).wait_recv())
            over_peers(part, lambda part, k: flux_copy(part, k).wait_send())
    else:
        table_ref[0] = flux_ref[...]


def atmosphere(comm, x, gain_attn, gain_mlp, qkv_w, out_w, up_w, down_w, flux_head):
    width = x.shape[-1]
    vm = pl.BlockSpec(memory_space=pltpu.VMEM)
    far = pl.BlockSpec(memory_space=pl.ANY)
    params = dict(collective_id=2, has_side_effects=True) if comm else {}
    return pl.pallas_call(
        functools.partial(air_kernel, comm),
        out_shape=[jax.ShapeDtypeStruct((4, 256, width), F32), jax.ShapeDtypeStruct((16, 4, 8, 256), BF)],
        in_specs=[vm, vm, vm, far, far, far, far, vm],
        out_specs=[vm, vm],
        scratch_shapes=[
            pltpu.VMEM(qkv_w.shape, BF), pltpu.VMEM(out_w.shape, BF), pltpu.VMEM(up_w.shape, BF), pltpu.VMEM(down_w.shape, BF),
            pltpu.VMEM((4, 4, 64, width), BF),
            pltpu.VMEM((2, 4, 64, width), BF), pltpu.VMEM((2, 4, 64, width), BF),
            pltpu.VMEM((4, 4, 64, 3 * width), BF),
            pltpu.VMEM((2, 4, 64, 2 * width), BF),
            pltpu.VMEM((2, 2, 256, width), BF), pltpu.VMEM((4, 8, 256), BF),
            pltpu.SemaphoreType.DMA((4,)), pltpu.SemaphoreType.DMA((2,)), pltpu.SemaphoreType.DMA((2,)),
            pltpu.SemaphoreType.DMA((2, 16)), pltpu.SemaphoreType.DMA((2, 16)),
        ],
        compiler_params=pltpu.CompilerParams(vmem_limit_bytes=56 * 2**20, **params),
        name="air",
        cost_estimate=pl.CostEstimate(flops=16 * 10**9, bytes_accessed=20 * 2**20, transcendentals=5 * 10**6),
    )(x.reshape(4, 8, 32, width), gain_attn, gain_mlp, qkv_w, out_w, up_w, down_w, jnp.swapaxes(flux_head, 0, 1))


def body(
    atmos_features,
    ocean_features,
    wet_cell_mask,
    overlay_cell_index,
    remap_weight,
    query_key_value_weight,
    attention_out_weight,
    feedforward_up_weight,
    feedforward_down_weight,
    attention_gain,
    feedforward_gain,
    flux_head_weight,
    surface_temp_embedding,
    forcing_lift_weight,
    depthwise_kernels,
    ocean_norm_gains,
    ocean_up_weights,
    ocean_down_weights,
    surface_temp_head,
):
    second, table = atmosphere(
        True, atmos_features, attention_gain, feedforward_gain, query_key_value_weight, attention_out_weight,
        feedforward_up_weight, feedforward_down_weight, flux_head_weight,
    )
    updated, ocean_out = ocean_step(
        True, table, overlay_cell_index, remap_weight, forcing_lift_weight, ocean_features, wet_cell_mask, depthwise_kernels,
        ocean_norm_gains, ocean_up_weights, jnp.swapaxes(ocean_down_weights, 1, 2), surface_temp_head, second,
        surface_temp_embedding,
    )
    return (updated, ocean_out)


def solution(mesh):
    cells = P("lat", "lon", None)
    in_specs = (cells, cells, P("lat", "lon"), P(None, "lat", "lon"), P(None, "lat", "lon")) + (P(),) * 14
    return jax.shard_map(body, mesh=mesh, in_specs=in_specs, out_specs=(cells, cells), check_vma=False)
```
